128 devices in a mesh: space: 16 (over z_lo, y, core), vec: 8 (over x, z_hi).
Axes of the slice: x: 4, y: 4, z: 4 (z_hi: 2, z_lo: 2; z = z_hi * 2 + z_lo), core: 2. Of those that a mesh axis runs over, the one named last changes fastest.
Arguments:
- vectors: float32 [192, 3, 16, 4096], P('vec', None, 'space'), may hold values from -6 to 6
- labels: int32 [16, 4096], P('space'), may hold values from 0 to 3
- stiffness: float32 [4, 3, 3, 3], replicated, may hold values from -0.45 to 8, as said below
- mass: float32 [4], replicated, may hold values from 0.5 to 2
Outputs:
- refined: float32 [192, 3, 16, 4096], P('vec', None, 'space')
- rayleigh: float32 [2, 192, 192], P(None, 'vec')
The draws below stay inside these ranges and needn't reach their ends.
Inputs may be any that keep to these rules, and one draw needn't show every extreme that they name: `stiffness`: each 3 x 3 coupling is symmetric, with diagonal entries larger than the sum of the magnitudes of the other entries of their row.
All inputs are finite; a program needn't handle non-finite values.
Results may differ from the reference program's by a relative error of at most 0.0001.
Values sent between devices are 32-bit elements; how exact they have to be, the bound alone decides.
No kernel may reach another device: no remote copies, remote signals or barrier semaphores. Data moves between devices by JAX's collectives and lax.ppermute only.
A program may use at most 128 MiB of HBM per device.

```python
import math
import jax
import jax.numpy as jnp
from jax import lax

NV = 192
NX = 64
NY = 64
NLAB = 4
ITERS = 2
NZ = 16
PLANE = 4096


def draw_stiffness(key, part):
    key = jax.random.fold_in(key, 11)
    key_diag, key_off = jax.random.split(key)
    diag = jnp.exp(jax.random.uniform(key_diag, (NLAB, 3, 3), jnp.float32, jnp.log(1.0), jnp.log(4.0)))
    off = jax.random.uniform(key_off, (NLAB, 3, 3, 3), jnp.float32, -0.3, 0.3)
    upper = jnp.triu(off, 1)
    symmetric = upper + jnp.swapaxes(upper, -1, -2)
    eye = jnp.eye(3, dtype=jnp.float32)
    return symmetric + diag[..., None] * eye


def with_ends(entries, own_key, smallest, largest):
    dims = entries.shape
    spot = [jax.random.randint(jax.random.fold_in(own_key, axis), (), 0, dims[axis]) for axis in range(len(dims))]
    entries = entries.at[tuple(spot)].set(smallest)
    longest = dims.index(max(dims))
    spot[longest] = (spot[longest] + 1) % dims[longest]
    return entries.at[tuple(spot)].set(largest)


def block_scale(own_key, extent, pieces, low, high):
    loudness = 1.0
    for dim, shards_of in pieces:
        steps = jax.random.uniform(jax.random.fold_in(jax.random.fold_in(own_key, 6), dim), (shards_of,), jnp.float32, low / len(pieces), high / len(pieces))
        loudness = loudness * jnp.repeat(jnp.exp(steps), extent[dim] // shards_of).reshape((-1,) + (1,) * (len(extent) - 1 - dim))
    return loudness


def noise(key, dims, deviation, limit, pieces=(), held_as=jnp.bfloat16):
    gain = block_scale(key, dims, pieces, -0.22, 0.18) if pieces else 1.0
    array = jax.random.normal(key, dims, jnp.float32) * deviation * gain
    return jnp.minimum(jnp.maximum(array, -limit), limit).astype(held_as)


def setup_inputs(seed: int = 0) -> dict:
    arg_keys = jax.random.split(jax.random.key(seed), 5)
    vectors = noise(arg_keys[0], (NV, 3, NZ, PLANE), 1.0, 6.0, ((0, 8), (2, 16)), jnp.float32)
    labels = with_ends(jax.random.randint(arg_keys[1], (NZ, PLANE), 0, NLAB), jax.random.fold_in(arg_keys[1], 1), 0, NLAB - 1).astype(jnp.int32)
    stiffness = draw_stiffness(jax.random.fold_in(arg_keys[4], 71), 0)
    mass = jnp.clip(jnp.exp(jax.random.uniform(arg_keys[3], (NLAB,), jnp.float32, math.log(0.5), math.log(2.0))), 0.5, 2.0)
    return dict(vectors=vectors, labels=labels, stiffness=stiffness, mass=mass)


def material(lab, table):
    out = jnp.zeros(table.shape[1:] + lab.shape, jnp.float32)
    for level in range(table.shape[0]):
        hit = (lab == level).astype(jnp.float32)
        out = out + table[level].reshape(table.shape[1:] + (1,) * lab.ndim) * hit
    return out

def mixing(coupling, differ):
    total = coupling[:, 0][None] * differ[:, 0:1]
    total = total + coupling[:, 1][None] * differ[:, 1:2]
    return total + coupling[:, 2][None] * differ[:, 2:3]

def build_fields(stiffness, mass, lab_lowz, lab_own, lab_lowy, plane_first, nz_all, start):
    count = lab_own.shape[1]
    knots = jnp.arange(lab_lowz.shape[0], dtype=jnp.int32) + plane_first
    valid_z = ((knots >= 0) & (knots <= nz_all - 2)).astype(jnp.float32)
    global_x = jnp.arange(count, dtype=jnp.int32) + start
    valid_x = (global_x % NX != NX - 1).astype(jnp.float32)
    global_y = jnp.arange(count + NX, dtype=jnp.int32) + start - NX
    valid_y = ((global_y >= 0) & (global_y < NX * NY - NX)).astype(jnp.float32)
    coupling_z = material(lab_lowz, stiffness[:, 2]) * valid_z[:, None]
    coupling_x = material(lab_own, stiffness[:, 0]) * valid_x
    coupling_y = material(lab_lowy, stiffness[:, 1]) * valid_y
    storage = material(lab_own, mass)
    return (coupling_z, coupling_x, coupling_y, storage)

def stiffness_apply(center, zext, yext, fields):
    coupling_z, coupling_x, coupling_y, storage = fields
    flux_z = mixing(coupling_z, zext[:, :, 1:] - zext[:, :, :-1])
    result = storage * center + flux_z[:, :, :-1] - flux_z[:, :, 1:]
    edge = jnp.zeros(center.shape[:-1] + (1,), jnp.float32)
    differ_x = jnp.concatenate([center[..., 1:] - center[..., :-1], edge], -1)
    flux_x = mixing(coupling_x, differ_x)
    result = result + jnp.concatenate([edge, flux_x[..., :-1]], -1) - flux_x
    flux_y = mixing(coupling_y, yext[..., NX:] - yext[..., :-NX])
    return result + flux_y[..., :-NX] - flux_y[..., NX:]

def reference(vectors, labels, stiffness, mass):
    cells = 3.0 * NZ * NX * NY
    zero_plane = jnp.zeros((1, NX * NY), jnp.int32)
    lab_lowz = jnp.concatenate([zero_plane, labels], 0)
    lab_lowy = jnp.concatenate([jnp.zeros((NZ, NX), jnp.int32), labels], 1)
    fields = build_fields(stiffness, mass, lab_lowz, labels, lab_lowy, -1, NZ, 0)

    def apply_block(block):
        zext = jnp.pad(block, ((0, 0), (0, 0), (1, 1), (0, 0)))
        yext = jnp.pad(block, ((0, 0), (0, 0), (0, 0), (NX, NX)))
        return stiffness_apply(block, zext, yext, fields)
    block = vectors
    crosses = []
    for step in range(ITERS):
        image = lax.map(apply_block, block.reshape((8, NV // 8) + block.shape[1:])).reshape(block.shape)
        flat_image = image.reshape(NV, -1)
        flat_block = block.reshape(NV, -1)
        gram = jnp.dot(flat_image.astype(jnp.float32), flat_image.T.astype(jnp.float32), precision=lax.Precision.HIGHEST, preferred_element_type=jnp.float32) / cells
        cross = jnp.dot(flat_block.astype(jnp.float32), flat_image.T.astype(jnp.float32), precision=lax.Precision.HIGHEST, preferred_element_type=jnp.float32) / cells
        lower = jnp.linalg.cholesky(gram)
        inverse = jax.scipy.linalg.solve_triangular(lower, jnp.eye(NV, dtype=jnp.float32), lower=True)
        block = jnp.dot(inverse.astype(jnp.float32), flat_image.astype(jnp.float32), precision=lax.Precision.HIGHEST, preferred_element_type=jnp.float32).reshape(image.shape)
        crosses.append(cross)
    return (block, jnp.stack(crosses))
```

```python
import functools

import jax
import jax.numpy as jnp
from jax import lax
from jax.experimental import pallas as pl
from jax.experimental.pallas import tpu as pltpu
from jax.sharding import PartitionSpec as P

NX = 64
LANES = 128
SUB = 8
LEVELS = 4
ENTRIES = ((0, 0), (0, 1), (0, 2), (1, 1), (1, 2), (2, 2))
ENTRY_OF = {pair: i for i, pair in enumerate(ENTRIES)}
VMEM_LIMIT = 48 * 1024 * 1024
SPACE = (2, 4, 2)
VEC = (4, 2)


def route(array, move):
    pairs = []
    for zl in range(SPACE[0]):
        for y in range(SPACE[1]):
            for core in range(SPACE[2]):
                for x in range(VEC[0]):
                    for zh in range(VEC[1]):
                        a, b, c, d, e = move(zl, y, core, x, zh)
                        here = (((zl * SPACE[1] + y) * SPACE[2] + core) * VEC[0] + x) * VEC[1] + zh
                        there = (((a * SPACE[1] + b) * SPACE[2] + c) * VEC[0] + d) * VEC[1] + e
                        pairs.append((here, there))
    return lax.ppermute(array, ("space", "vec"), pairs)


def step_along(array, axis, by):
    peers = lax.axis_size(axis)
    pairs = [(i, i + by) for i in range(peers) if 0 <= i + by < peers]
    return lax.ppermute(array, axis, pairs)


def spread_kernel(x_ref, o_ref, *, nvec, tiles):
    groups, per, comps = o_ref.shape[:3]
    stride = comps * tiles
    for h in range(groups):
        for t in range(per):
            for c in range(comps):
                for v in range(0, nvec, SUB):
                    o_ref[h, t, c, v : v + SUB, :] = x_ref[
                        pl.ds(v * stride + c * tiles + h * per + t, SUB, stride), :
                    ]


def collect_kernel(x_ref, o_ref, *, nvec, tiles):
    groups, per, comps = x_ref.shape[:3]
    stride = comps * tiles
    for h in range(groups):
        for t in range(per):
            for c in range(comps):
                for v in range(0, nvec, SUB):
                    o_ref[pl.ds(v * stride + c * tiles + h * per + t, SUB, stride), :] = x_ref[
                        h, t, c, v : v + SUB, :
                    ]


def stencil_kernel(stiff_ref, mass_ref, cls_ref, u_ref, zd_ref, zu_ref, yd_ref, yu_ref, w_ref, coef_ref):
    groups, per, comps, nvec = u_ref.shape[:4]
    lane = lax.broadcasted_iota(jnp.int32, (SUB, LANES), 1)
    low = lane < NX

    def pick(cls, values):
        out = jnp.zeros((SUB, LANES), jnp.float32)
        for level in range(LEVELS):
            out = jnp.where(cls == level, values[level], out)
        return out

    for t in range(per):
        for face, direction in enumerate((0, 1, 1, 2, 2)):
            cls = jnp.broadcast_to(cls_ref[face, t : t + 1, :], (SUB, LANES))
            for i, (a, b) in enumerate(ENTRIES):
                spots = [((level * 3 + direction) * 3 + a) * 3 + b for level in range(LEVELS)]
                coef_ref[t, face * 6 + i] = pick(cls, [stiff_ref[s] for s in spots])
        cls = jnp.broadcast_to(cls_ref[5, t : t + 1, :], (SUB, LANES))
        coef_ref[t, 30] = pick(cls, [mass_ref[level] for level in range(LEVELS)])

    def mix(t, face, d):
        s = [coef_ref[t, face * 6 + i] for i in range(6)]
        return [
            s[ENTRY_OF[min(a, 0), max(a, 0)]] * d[0]
            + s[ENTRY_OF[min(a, 1), max(a, 1)]] * d[1]
            + s[ENTRY_OF[min(a, 2), max(a, 2)]] * d[2]
            for a in range(3)
        ]

    steps = nvec // SUB

    def body(i, carry):
        g = i // steps
        rows = pl.ds(pl.multiple_of((i % steps) * SUB, SUB), SUB)
        tiles = [[u_ref[g, t, c, rows, :] for c in range(3)] for t in range(per)]
        swaps = [[yd_ref[g, c, rows, :] for c in range(3)]] + tiles + [[yu_ref[g, c, rows, :] for c in range(3)]]
        swaps = [[pltpu.roll(a, NX, 1) for a in line] for line in swaps]
        for t in range(per):
            u = tiles[t]
            f = mix(t, 0, [pltpu.roll(u[c], LANES - 1, 1) - u[c] for c in range(3)])
            acc = [coef_ref[t, 30] * u[c] + (pltpu.roll(f[c], 1, 1) - f[c]) for c in range(3)]
            f = mix(t, 1, [jnp.where(low, swaps[t + 1][c], swaps[t + 2][c]) - u[c] for c in range(3)])
            acc = [acc[c] - f[c] for c in range(3)]
            f = mix(t, 2, [u[c] - jnp.where(low, swaps[t][c], swaps[t + 1][c]) for c in range(3)])
            acc = [acc[c] + f[c] for c in range(3)]
            f = mix(t, 3, [zu_ref[g, t, c, rows, :] - u[c] for c in range(3)])
            acc = [acc[c] - f[c] for c in range(3)]
            f = mix(t, 4, [u[c] - zd_ref[g, t, c, rows, :] for c in range(3)])
            for c in range(3):
                w_ref[g, t, c, rows, :] = acc[c] + f[c]
        return carry

    lax.fori_loop(0, groups * steps, body, 0)


def stacked(ref, t, c):
    groups = ref.shape[0]
    return jnp.concatenate([ref[g, t, c] for g in range(groups)], 0)


def wide(ref, k):
    comps = ref.shape[2]
    return jnp.concatenate([stacked(ref, (2 * k + j) // comps, (2 * k + j) % comps) for j in range(2)], 1)


def gram_kernel(b_ref, a_ref, o_ref):
    chunks = a_ref.shape[1] * a_ref.shape[2] // 2
    total = None
    for k in range(chunks):
        a = wide(a_ref, k)
        both = jnp.concatenate([wide(b_ref, k), a], 0)
        part = lax.dot_general(
            a,
            both,
            (((1,), (1,)), ((), ())),
            precision=lax.Precision.HIGHEST,
            preferred_element_type=jnp.float32,
        )
        total = part if total is None else total + part
    o_ref[...] = total


def combine_kernel(inv_ref, w_ref, o_ref):
    groups, per, comps, nvec = w_ref.shape[:4]
    inv = inv_ref[...]
    for k in range(per * comps // 2):
        out = lax.dot_general(
            inv,
            wide(w_ref, k),
            (((1,), (0,)), ((), ())),
            precision=lax.Precision.HIGHEST,
            preferred_element_type=jnp.float32,
        )
        for j in range(2):
            t, c = (2 * k + j) // comps, (2 * k + j) % comps
            for g in range(groups):
                o_ref[g, t, c] = out[g * nvec : (g + 1) * nvec, j * LANES : (j + 1) * LANES]


def call(kernel, out, operands, scratch=(), smem=0, flops=0):
    specs = [pl.BlockSpec(memory_space=pltpu.SMEM)] * smem
    specs += [pl.BlockSpec(memory_space=pltpu.VMEM)] * (len(operands) - smem)
    size = sum(a.size * 4 for a in operands) + 4
    return pl.pallas_call(
        kernel,
        out_shape=jax.ShapeDtypeStruct(out, jnp.float32),
        in_specs=specs,
        out_specs=pl.BlockSpec(memory_space=pltpu.VMEM),
        scratch_shapes=list(scratch),
        compiler_params=pltpu.CompilerParams(vmem_limit_bytes=VMEM_LIMIT),
        cost_estimate=pl.CostEstimate(flops=flops, bytes_accessed=size, transcendentals=0),
    )(*operands)


def total_over_all(part):
    rows = part.shape[0]
    core = lax.axis_index("space") % 2
    y = (lax.axis_index("space") // 2) % 4
    half = rows // 2
    quarter = half // 4
    keep = lax.dynamic_slice_in_dim(part, core * half, half, 0)
    give = lax.dynamic_slice_in_dim(part, (1 - core) * half, half, 0)
    mine = keep + route(give, lambda zl, y, c, x, zh: (zl, y, 1 - c, x, zh))

    def chunk(k):
        return lax.dynamic_slice_in_dim(mine, ((y + k) % 4) * quarter, quarter, 0)

    def along_y(k):
        return lambda zl, y, c, x, zh: (zl, (y + k) % 4, c, x, zh)

    def along_x(k):
        return lambda zl, y, c, x, zh: (zl, y, c, (x + k) % 4, zh)

    def along_z(k):
        def move(zl, y, c, x, zh):
            z = (zh * 2 + zl + k) % 4
            return (z % 2, y, c, x, z // 2)

        return move

    got = [route(chunk(k), along_y(k)) for k in (1, 2, 3)]
    mine = (chunk(0) + got[1]) + (got[0] + got[2])
    for along in (along_x, along_z):
        got = [route(mine, along(k)) for k in (1, 2, 3)]
        mine = (mine + got[1]) + (got[0] + got[2])
    got = [mine] + [route(mine, along_y(k)) for k in (1, 2, 3)]
    mine = jnp.concatenate([lax.select_n((y - i) % 4, *got) for i in range(4)], 0)
    other = route(mine, lambda zl, y, c, x, zh: (zl, y, 1 - c, x, zh))
    return jnp.concatenate([jnp.where(core == 0, mine, other), jnp.where(core == 0, other, mine)], 0)


def local(vectors, labels, stiffness, mass):
    nvec, comps, _, plane = vectors.shape
    groups = lax.axis_size("vec")
    total = nvec * groups
    nz = lax.axis_size("space")
    cells = 3.0 * nz * plane
    tiles = plane // LANES
    per = tiles // groups
    z = lax.axis_index("space")
    h = lax.axis_index("vec")

    below = step_along(labels, "space", 1)
    lab = labels.reshape(plane // NX, NX)
    row = lax.broadcasted_iota(jnp.int32, lab.shape, 0)
    col = lax.broadcasted_iota(jnp.int32, lab.shape, 1)
    none = LEVELS
    upper = jnp.concatenate([jnp.full((1, NX), none, jnp.int32), lab[:-1]], 0)
    faces = jnp.stack(
        [
            jnp.where(col == NX - 1, none, lab),
            jnp.where(row == lab.shape[0] - 1, none, lab),
            upper,
            jnp.where(z == nz - 1, none, lab),
            jnp.where(z == 0, none, below.reshape(lab.shape)),
            lab,
        ]
    )
    faces = faces.reshape(6, tiles, LANES)
    faces = lax.dynamic_slice_in_dim(faces, h * per, per, 1)
    stiff = stiffness.reshape(-1)

    shape = (groups, per, comps, nvec, LANES)

    def apply(u):
        zd = step_along(u, "space", 1)
        zu = step_along(u, "space", -1)
        yd = step_along(u[:, per - 1], "vec", 1)
        yu = step_along(u[:, 0], "vec", -1)
        return call(
            stencil_kernel,
            shape,
            (stiff, mass, faces, u, zd, zu, yd, yu),
            scratch=[pltpu.VMEM((per, 31, SUB, LANES), jnp.float32)],
            smem=2,
            flops=20_000_000,
        )

    def gram(b, a):
        return call(gram_kernel, (total, 2 * total), (b, a), flops=6 * 4 * total * total * per * comps * LANES)

    start = call(
        functools.partial(spread_kernel, nvec=nvec, tiles=tiles),
        shape,
        (vectors.reshape(nvec * comps * tiles, LANES),),
    )
    v = lax.all_to_all(start, "vec", 0, 0)
    w1 = apply(v)
    w2 = apply(w1)
    early = total_over_all(gram(v, w1)) / cells
    late = total_over_all(gram(w1, w2)) / cells

    def inverse_factor(matrix):
        lower = jnp.linalg.cholesky(matrix)
        return jax.scipy.linalg.solve_triangular(lower, jnp.eye(total, dtype=jnp.float32), lower=True)

    inv_last = inverse_factor(late[:, total:])
    out = call(combine_kernel, shape, (inv_last, w2), flops=12 * total * total * per * comps * LANES)
    out = lax.all_to_all(out, "vec", 0, 0)
    refined = call(
        functools.partial(collect_kernel, nvec=nvec, tiles=tiles),
        (nvec * comps * tiles, LANES),
        (out,),
    ).reshape(vectors.shape)

    inv_first = inverse_factor(early[:, total:])
    first = lax.dynamic_slice_in_dim(early[:, :total], h * nvec, nvec, 0)
    rows = lax.dynamic_slice_in_dim(inv_first, h * nvec, nvec, 0)
    second = jnp.dot(rows, late[:, :total], precision=lax.Precision.HIGHEST)
    second = jnp.dot(second, inv_first.T, precision=lax.Precision.HIGHEST)
    return refined, jnp.stack([first, second])


def solution(mesh):
    return jax.shard_map(
        local,
        mesh=mesh,
        in_specs=(P("vec", None, "space", None), P("space", None), P(), P()),
        out_specs=(P("vec", None, "space", None), P(None, "vec", None)),
        check_vma=False,
    )
```

```python
import functools

import jax
import jax.numpy as jnp
from jax import lax
from jax.experimental import pallas as pl
from jax.experimental.pallas import tpu as pltpu
from jax.sharding import PartitionSpec as P

NX = 64
LANES = 128
SUB = 8
LEVELS = 4
BLOCK = 32
STEP = 4
ENTRIES = ((0, 0), (0, 1), (0, 2), (1, 1), (1, 2), (2, 2))
ENTRY_OF = {pair: i for i, pair in enumerate(ENTRIES)}
VMEM_LIMIT = 48 * 1024 * 1024
SPACE = (2, 4, 2)
VEC = (4, 2)


def route(array, move):
    pairs = []
    for zl in range(SPACE[0]):
        for y in range(SPACE[1]):
            for core in range(SPACE[2]):
                for x in range(VEC[0]):
                    for zh in range(VEC[1]):
                        a, b, c, d, e = move(zl, y, core, x, zh)
                        here = (((zl * SPACE[1] + y) * SPACE[2] + core) * VEC[0] + x) * VEC[1] + zh
                        there = (((a * SPACE[1] + b) * SPACE[2] + c) * VEC[0] + d) * VEC[1] + e
                        pairs.append((here, there))
    return lax.ppermute(array, ("space", "vec"), pairs)


def step_along(array, axis, by):
    peers = lax.axis_size(axis)
    pairs = [(i, i + by) for i in range(peers) if 0 <= i + by < peers]
    return lax.ppermute(array, axis, pairs)


def spread_kernel(x_ref, o_ref, *, nvec, tiles):
    groups, per, comps = o_ref.shape[:3]
    stride = comps * tiles
    for h in range(groups):
        for t in range(per):
            for c in range(comps):
                for v in range(0, nvec, SUB):
                    o_ref[h, t, c, v : v + SUB, :] = x_ref[
                        pl.ds(v * stride + c * tiles + h * per + t, SUB, stride), :
                    ]


def collect_kernel(x_ref, o_ref, *, nvec, tiles):
    groups, per, comps = x_ref.shape[:3]
    stride = comps * tiles
    for h in range(groups):
        for t in range(per):
            for c in range(comps):
                for v in range(0, nvec, SUB):
                    o_ref[pl.ds(v * stride + c * tiles + h * per + t, SUB, stride), :] = x_ref[
                        h, t, c, v : v + SUB, :
                    ]


def stencil_kernel(stiff_ref, mass_ref, cls_ref, u_ref, zd_ref, zu_ref, yd_ref, yu_ref, w_ref, coef_ref):
    groups, per, comps, nvec = u_ref.shape[:4]
    lane = lax.broadcasted_iota(jnp.int32, (SUB, LANES), 1)
    low = lane < NX

    def pick(cls, values):
        out = jnp.zeros((SUB, LANES), jnp.float32)
        for level in range(LEVELS):
            out = jnp.where(cls == level, values[level], out)
        return out

    for t in range(per):
        for face, direction in enumerate((0, 1, 1, 2, 2)):
            cls = jnp.broadcast_to(cls_ref[face, t : t + 1, :], (SUB, LANES))
            for i, (a, b) in enumerate(ENTRIES):
                spots = [((level * 3 + direction) * 3 + a) * 3 + b for level in range(LEVELS)]
                coef_ref[t, face * 6 + i] = pick(cls, [stiff_ref[s] for s in spots])
        cls = jnp.broadcast_to(cls_ref[5, t : t + 1, :], (SUB, LANES))
        coef_ref[t, 30] = pick(cls, [mass_ref[level] for level in range(LEVELS)])

    def mix(t, face, d):
        s = [coef_ref[t, face * 6 + i] for i in range(6)]
        return [
            s[ENTRY_OF[min(a, 0), max(a, 0)]] * d[0]
            + s[ENTRY_OF[min(a, 1), max(a, 1)]] * d[1]
            + s[ENTRY_OF[min(a, 2), max(a, 2)]] * d[2]
            for a in range(3)
        ]

    steps = nvec // SUB

    def body(i, carry):
        g = i // steps
        rows = pl.ds(pl.multiple_of((i % steps) * SUB, SUB), SUB)
        tiles = [[u_ref[g, t, c, rows, :] for c in range(3)] for t in range(per)]
        swaps = [[yd_ref[g, c, rows, :] for c in range(3)]] + tiles + [[yu_ref[g, c, rows, :] for c in range(3)]]
        swaps = [[pltpu.roll(a, NX, 1) for a in line] for line in swaps]
        for t in range(per):
            u = tiles[t]
            f = mix(t, 0, [pltpu.roll(u[c], LANES - 1, 1) - u[c] for c in range(3)])
            acc = [coef_ref[t, 30] * u[c] + (pltpu.roll(f[c], 1, 1) - f[c]) for c in range(3)]
            f = mix(t, 1, [jnp.where(low, swaps[t + 1][c], swaps[t + 2][c]) - u[c] for c in range(3)])
            acc = [acc[c] - f[c] for c in range(3)]
            f = mix(t, 2, [u[c] - jnp.where(low, swaps[t][c], swaps[t + 1][c]) for c in range(3)])
            acc = [acc[c] + f[c] for c in range(3)]
            f = mix(t, 3, [zu_ref[g, t, c, rows, :] - u[c] for c in range(3)])
            acc = [acc[c] - f[c] for c in range(3)]
            f = mix(t, 4, [u[c] - zd_ref[g, t, c, rows, :] for c in range(3)])
            for c in range(3):
                w_ref[g, t, c, rows, :] = acc[c] + f[c]
        return carry

    lax.fori_loop(0, groups * steps, body, 0)


def stacked(ref, t, c):
    groups = ref.shape[0]
    return jnp.concatenate([ref[g, t, c] for g in range(groups)], 0)


def wide(ref, k):
    comps = ref.shape[2]
    return jnp.concatenate([stacked(ref, (2 * k + j) // comps, (2 * k + j) % comps) for j in range(2)], 1)


def gram_kernel(b_ref, a_ref, o_ref):
    chunks = a_ref.shape[1] * a_ref.shape[2] // 2
    total = None
    for k in range(chunks):
        a = wide(a_ref, k)
        both = jnp.concatenate([wide(b_ref, k), a], 0)
        part = lax.dot_general(
            a,
            both,
            (((1,), (1,)), ((), ())),
            precision=lax.Precision.HIGHEST,
            preferred_element_type=jnp.float32,
        )
        total = part if total is None else total + part
    o_ref[...] = total


def eliminate(panels, cols):
    first, width = cols
    tile, lane0 = first // LANES, first % LANES
    lane = lax.broadcasted_iota(jnp.int32, (SUB, LANES), 1)
    sub = lax.broadcasted_iota(jnp.int32, (SUB, LANES), 0)
    strips = width // SUB
    states = []
    for panel in panels:
        state = [[panel[i * SUB : (i + 1) * SUB, a : a + LANES] for a in range(0, panel.shape[1], LANES)] for i in range(strips)]
        unit = [jnp.where(lane == lane0 + i * SUB + sub, 1.0, 0.0) for i in range(strips)]
        states.append([line + [u] for line, u in zip(state, unit)])
    scales = [[jnp.ones((SUB, LANES), jnp.float32) for _ in range(strips)] for _ in panels]

    def spread(row, like):
        return jnp.broadcast_to(row, (SUB, like.shape[1]))

    for j in range(0, width, STEP):
        strip, off = j // SUB, j % SUB
        for m, state in enumerate(states):
            columns = [
                [jnp.broadcast_to(state[i][tile][:, lane0 + j + s : lane0 + j + s + 1], (SUB, LANES)) for i in range(strip, strips)]
                for s in range(STEP)
            ]
            rows = [[spread(part[off + r : off + r + 1, :], part) for part in state[strip]] for r in range(STEP)]
            small = [[spread(columns[s][0][off + r : off + r + 1, :], columns[s][0]) for s in range(STEP)] for r in range(STEP)]
            inverse = []
            pivots = []
            for r in range(STEP):
                pivots.append(small[r][r])
                inverse.append(1.0 / small[r][r])
                for q in range(r + 1, STEP):
                    ratio = small[q][r] * inverse[r]
                    rows[q] = [a - ratio[:, : a.shape[1]] * b for a, b in zip(rows[q], rows[r])]
                    columns[q] = [a - ratio * b for a, b in zip(columns[q], columns[r])]
                    for p in range(q, STEP):
                        small[p][q] = small[p][q] - ratio * small[p][r]
            weights = [[a * inverse[s] for a in columns[s]] for s in range(STEP)]
            for i in range(strip, strips):
                line = []
                for n, part in enumerate(state[i]):
                    value = part
                    for s in range(STEP):
                        value = value - weights[s][i - strip][:, : part.shape[1]] * rows[s][n]
                    if i == strip:
                        at = sub[:, : part.shape[1]]
                        if off:
                            value = jnp.where(at < off, part, value)
                        for r in range(STEP):
                            value = jnp.where(at == off + r, rows[r][n], value)
                    line.append(value)
                state[i] = line
            for r in range(STEP):
                scales[m][strip] = jnp.where(sub == off + r, pivots[r], scales[m][strip])
    results = []
    for state, scale in zip(states, scales):
        inverse, reduced = [], []
        for line, pivot in zip(state, scale):
            root = lax.rsqrt(pivot)
            root = root * (1.5 - 0.5 * pivot * root * root)
            inverse.append(line[-1] * root)
            reduced.append(jnp.concatenate([part * root[:, : part.shape[1]] for part in line[:-1]], 1))
        results.append((jnp.concatenate(inverse, 0), jnp.concatenate(reduced, 0)))
    return results


def dot(a, b, dims):
    return lax.dot_general(
        a, b, ((dims[:1], dims[1:]), ((), ())), precision=lax.Precision.HIGHEST, preferred_element_type=jnp.float32
    )


def factor(scratch, total):
    count = scratch.shape[0]
    lane = lax.broadcasted_iota(jnp.int32, (1, total), 1)
    for first in range(0, total, BLOCK):
        last = first + BLOCK
        here = (lane >= first) & (lane < last)
        results = eliminate([scratch[m, first:last, :] for m in range(count)], (first, BLOCK))
        for m, (inverse, reduced) in enumerate(results):
            tile = first // LANES * LANES
            side = min(LANES, total - tile)
            parts = []
            if tile:
                parts.append(jnp.zeros((BLOCK, tile), jnp.float32))
            parts.append(inverse[:, :side])
            if tile + side < total:
                parts.append(jnp.zeros((BLOCK, total - tile - side), jnp.float32))
            inverse = jnp.concatenate(parts, 1)
            row = jnp.where(here, inverse, reduced)
            scratch[m, first:last, :] = jnp.where(lane < last, row, 0.0)
            if last < total:
                rest = scratch[m, last:, :]
                lower = dot(rest, inverse, (1, 1))
                scratch[m, last:, :] = jnp.where(here, 0.0, rest) - dot(lower, row, (1, 0))


def tail_kernel(h_ref, early_ref, late_ref, w_ref, o_ref, ray_ref, scratch, *, cells):
    groups, per, comps, nvec = w_ref.shape[:4]
    total = groups * nvec
    scale = 1.0 / cells
    scratch[0] = early_ref[:, total:] * scale
    scratch[1] = late_ref[:, total:] * scale
    factor(scratch, total)
    inv = scratch[1]
    for k in range(per * comps // 2):
        out = dot(inv, wide(w_ref, k), (1, 0))
        for j in range(2):
            t, c = (2 * k + j) // comps, (2 * k + j) % comps
            for g in range(groups):
                o_ref[g, t, c] = out[g * nvec : (g + 1) * nvec, j * LANES : (j + 1) * LANES]
    own = pl.ds(pl.multiple_of(h_ref[0] * nvec, SUB), nvec)
    ray_ref[0] = early_ref[own, :][:, :total] * scale
    rows = dot(scratch[0, own, :], late_ref[:, :total] * scale, (1, 0))
    ray_ref[1] = dot(rows, scratch[0], (1, 1))


def call(kernel, out, operands, scratch=(), smem=0, flops=0):
    specs = [pl.BlockSpec(memory_space=pltpu.SMEM)] * smem
    specs += [pl.BlockSpec(memory_space=pltpu.VMEM)] * (len(operands) - smem)
    size = sum(a.size * 4 for a in operands) + 4
    return pl.pallas_call(
        kernel,
        out_shape=jax.tree.map(lambda dims: jax.ShapeDtypeStruct(dims, jnp.float32), out, is_leaf=lambda d: isinstance(d[0], int)),
        in_specs=specs,
        out_specs=jax.tree.map(lambda dims: pl.BlockSpec(memory_space=pltpu.VMEM), out, is_leaf=lambda d: isinstance(d[0], int)),
        scratch_shapes=list(scratch),
        compiler_params=pltpu.CompilerParams(vmem_limit_bytes=VMEM_LIMIT),
        cost_estimate=pl.CostEstimate(flops=flops, bytes_accessed=size, transcendentals=0),
    )(*operands)


def total_over_all(part):
    rows = part.shape[0]
    core = lax.axis_index("space") % 2
    y = (lax.axis_index("space") // 2) % 4
    half = rows // 2
    quarter = half // 4
    keep = lax.dynamic_slice_in_dim(part, core * half, half, 0)
    give = lax.dynamic_slice_in_dim(part, (1 - core) * half, half, 0)
    mine = keep + route(give, lambda zl, y, c, x, zh: (zl, y, 1 - c, x, zh))

    def chunk(k):
        return lax.dynamic_slice_in_dim(mine, ((y + k) % 4) * quarter, quarter, 0)

    def along_y(k):
        return lambda zl, y, c, x, zh: (zl, (y + k) % 4, c, x, zh)

    def along_x(k):
        return lambda zl, y, c, x, zh: (zl, y, c, (x + k) % 4, zh)

    def along_z(k):
        def move(zl, y, c, x, zh):
            z = (zh * 2 + zl + k) % 4
            return (z % 2, y, c, x, z // 2)

        return move

    got = [route(chunk(k), along_y(k)) for k in (1, 2, 3)]
    mine = (chunk(0) + got[1]) + (got[0] + got[2])
    for along in (along_x, along_z):
        got = [route(mine, along(k)) for k in (1, 2, 3)]
        mine = (mine + got[1]) + (got[0] + got[2])
    got = [mine] + [route(mine, along_y(k)) for k in (1, 2, 3)]
    mine = jnp.concatenate([lax.select_n((y - i) % 4, *got) for i in range(4)], 0)
    other = route(mine, lambda zl, y, c, x, zh: (zl, y, 1 - c, x, zh))
    return jnp.concatenate([jnp.where(core == 0, mine, other), jnp.where(core == 0, other, mine)], 0)


def local(vectors, labels, stiffness, mass):
    nvec, comps, _, plane = vectors.shape
    groups = lax.axis_size("vec")
    total = nvec * groups
    nz = lax.axis_size("space")
    cells = 3.0 * nz * plane
    tiles = plane // LANES
    per = tiles // groups
    z = lax.axis_index("space")
    h = lax.axis_index("vec")

    below = step_along(labels, "space", 1)
    lab = labels.reshape(plane // NX, NX)
    row = lax.broadcasted_iota(jnp.int32, lab.shape, 0)
    col = lax.broadcasted_iota(jnp.int32, lab.shape, 1)
    none = LEVELS
    upper = jnp.concatenate([jnp.full((1, NX), none, jnp.int32), lab[:-1]], 0)
    faces = jnp.stack(
        [
            jnp.where(col == NX - 1, none, lab),
            jnp.where(row == lab.shape[0] - 1, none, lab),
            upper,
            jnp.where(z == nz - 1, none, lab),
            jnp.where(z == 0, none, below.reshape(lab.shape)),
            lab,
        ]
    )
    faces = faces.reshape(6, tiles, LANES)
    faces = lax.dynamic_slice_in_dim(faces, h * per, per, 1)
    stiff = stiffness.reshape(-1)

    shape = (groups, per, comps, nvec, LANES)

    def apply(u):
        zd = step_along(u, "space", 1)
        zu = step_along(u, "space", -1)
        yd = step_along(u[:, per - 1], "vec", 1)
        yu = step_along(u[:, 0], "vec", -1)
        return call(
            stencil_kernel,
            shape,
            (stiff, mass, faces, u, zd, zu, yd, yu),
            scratch=[pltpu.VMEM((per, 31, SUB, LANES), jnp.float32)],
            smem=2,
            flops=20_000_000,
        )

    def gram(b, a):
        return call(gram_kernel, (total, 2 * total), (b, a), flops=6 * 4 * total * total * per * comps * LANES)

    start = call(
        functools.partial(spread_kernel, nvec=nvec, tiles=tiles),
        shape,
        (vectors.reshape(nvec * comps * tiles, LANES),),
    )
    v = lax.all_to_all(start, "vec", 0, 0)
    w1 = apply(v)
    w2 = apply(w1)
    early = total_over_all(gram(v, w1))
    late = total_over_all(gram(w1, w2))
    out, rayleigh = call(
        functools.partial(tail_kernel, cells=cells),
        [shape, (2, nvec, total)],
        (h.reshape(1).astype(jnp.int32), early, late, w2),
        scratch=[pltpu.VMEM((2, total, total), jnp.float32)],
        smem=1,
        flops=14 * total * total * per * comps * LANES,
    )
    out = lax.all_to_all(out, "vec", 0, 0)
    refined = call(
        functools.partial(collect_kernel, nvec=nvec, tiles=tiles),
        (nvec * comps * tiles, LANES),
        (out,),
    )
    return refined.reshape(vectors.shape), rayleigh


def solution(mesh):
    return jax.shard_map(
        local,
        mesh=mesh,
        in_specs=(P("vec", None, "space", None), P("space", None), P(), P()),
        out_specs=(P("vec", None, "space", None), P(None, "vec", None)),
        check_vma=False,
    )
```

```python
import functools

import jax
import jax.numpy as jnp
from jax import lax
from jax.experimental import pallas as pl
from jax.experimental.pallas import tpu as pltpu
from jax.sharding import PartitionSpec as P

NX = 64
LANES = 128
SUB = 8
LEVELS = 4
BLOCK = 32
STEP = 4
ENTRIES = ((0, 0), (0, 1), (0, 2), (1, 1), (1, 2), (2, 2))
ENTRY_OF = {pair: i for i, pair in enumerate(ENTRIES)}
VMEM_LIMIT = 48 * 1024 * 1024
SPACE = (2, 4, 2)
VEC = (4, 2)
TILE = 64
PAIRS = ((0, 0), (1, 0), (1, 1), (2, 0), (2, 1), (2, 2))


def rows_of(device):
    x, far = device // VEC[1], device % VEC[1]
    return x + far * (2 * VEC[0] - 1 - 2 * x)


DEVICE_OF = sorted(range(VEC[0] * VEC[1]), key=rows_of)


def route(array, move):
    pairs = []
    for zl in range(SPACE[0]):
        for y in range(SPACE[1]):
            for core in range(SPACE[2]):
                for x in range(VEC[0]):
                    for zh in range(VEC[1]):
                        a, b, c, d, e = move(zl, y, core, x, zh)
                        here = (((zl * SPACE[1] + y) * SPACE[2] + core) * VEC[0] + x) * VEC[1] + zh
                        there = (((a * SPACE[1] + b) * SPACE[2] + c) * VEC[0] + d) * VEC[1] + e
                        pairs.append((here, there))
    return lax.ppermute(array, ("space", "vec"), pairs)


def step_along(array, axis, by):
    order = DEVICE_OF if axis == "vec" else range(lax.axis_size(axis))
    pairs = [(order[i], order[i + by]) for i in range(len(order)) if 0 <= i + by < len(order)]
    return lax.ppermute(array, axis, pairs)


def spread_kernel(x_ref, o_ref, *, nvec, tiles):
    groups, per, comps = o_ref.shape[:3]
    stride = comps * tiles
    for h in range(groups):
        for t in range(per):
            for c in range(comps):
                for v in range(0, nvec, SUB):
                    o_ref[h, t, c, v : v + SUB, :] = x_ref[
                        pl.ds(v * stride + c * tiles + rows_of(h) * per + t, SUB, stride), :
                    ]


def collect_kernel(x_ref, o_ref, *, nvec, tiles):
    groups, per, comps = x_ref.shape[:3]
    stride = comps * tiles
    for h in range(groups):
        for t in range(per):
            for c in range(comps):
                for v in range(0, nvec, SUB):
                    o_ref[pl.ds(v * stride + c * tiles + rows_of(h) * per + t, SUB, stride), :] = x_ref[
                        h, t, c, v : v + SUB, :
                    ]


def stencil_kernel(stiff_ref, mass_ref, cls_ref, u_ref, zd_ref, zu_ref, yd_ref, yu_ref, w_ref, coef_ref):
    groups, per, comps, nvec = u_ref.shape[:4]
    lane = lax.broadcasted_iota(jnp.int32, (SUB, LANES), 1)
    low = lane < NX

    def pick(cls, values):
        out = jnp.zeros((SUB, LANES), jnp.float32)
        for level in range(LEVELS):
            out = jnp.where(cls == level, values[level], out)
        return out

    for t in range(per):
        for face, direction in enumerate((0, 1, 1, 2, 2)):
            cls = jnp.broadcast_to(cls_ref[face, t : t + 1, :], (SUB, LANES))
            for i, (a, b) in enumerate(ENTRIES):
                spots = [((level * 3 + direction) * 3 + a) * 3 + b for level in range(LEVELS)]
                coef_ref[t, face * 6 + i] = pick(cls, [stiff_ref[s] for s in spots])
        cls = jnp.broadcast_to(cls_ref[5, t : t + 1, :], (SUB, LANES))
        coef_ref[t, 30] = pick(cls, [mass_ref[level] for level in range(LEVELS)])

    def mix(t, face, d):
        s = [coef_ref[t, face * 6 + i] for i in range(6)]
        return [
            s[ENTRY_OF[min(a, 0), max(a, 0)]] * d[0]
            + s[ENTRY_OF[min(a, 1), max(a, 1)]] * d[1]
            + s[ENTRY_OF[min(a, 2), max(a, 2)]] * d[2]
            for a in range(3)
        ]

    steps = nvec // SUB

    def body(i, carry):
        g = i // steps
        rows = pl.ds(pl.multiple_of((i % steps) * SUB, SUB), SUB)
        tiles = [[u_ref[g, t, c, rows, :] for c in range(3)] for t in range(per)]
        swaps = [[yd_ref[g, c, rows, :] for c in range(3)]] + tiles + [[yu_ref[g, c, rows, :] for c in range(3)]]
        swaps = [[pltpu.roll(a, NX, 1) for a in line] for line in swaps]
        for t in range(per):
            u = tiles[t]
            f = mix(t, 0, [pltpu.roll(u[c], LANES - 1, 1) - u[c] for c in range(3)])
            acc = [coef_ref[t, 30] * u[c] + (pltpu.roll(f[c], 1, 1) - f[c]) for c in range(3)]
            f = mix(t, 1, [jnp.where(low, swaps[t + 1][c], swaps[t + 2][c]) - u[c] for c in range(3)])
            acc = [acc[c] - f[c] for c in range(3)]
            f = mix(t, 2, [u[c] - jnp.where(low, swaps[t][c], swaps[t + 1][c]) for c in range(3)])
            acc = [acc[c] + f[c] for c in range(3)]
            f = mix(t, 3, [zu_ref[g, t, c, rows, :] - u[c] for c in range(3)])
            acc = [acc[c] - f[c] for c in range(3)]
            f = mix(t, 4, [u[c] - zd_ref[g, t, c, rows, :] for c in range(3)])
            for c in range(3):
                w_ref[g, t, c, rows, :] = acc[c] + f[c]
        return carry

    lax.fori_loop(0, groups * steps, body, 0)


def stacked(ref, t, c):
    groups = ref.shape[0]
    return jnp.concatenate([ref[g, t, c] for g in range(groups)], 0)


def wide(ref, k):
    comps = ref.shape[2]
    return jnp.concatenate([stacked(ref, (2 * k + j) // comps, (2 * k + j) % comps) for j in range(2)], 1)


def packed_products(b_ref, a_ref):
    chunks = a_ref.shape[1] * a_ref.shape[2] // 2
    total = None
    for k in range(chunks):
        a, b = wide(a_ref, k), wide(b_ref, k)
        both = [side[i : i + TILE] for i in range(0, a.shape[0], TILE) for side in (b, a)]
        part = dot(a, jnp.concatenate(both, 0), (1, 1))
        total = part if total is None else total + part
    return [total[i * TILE : (i + 1) * TILE, j * LANES : (j + 1) * LANES] for i, j in PAIRS]


def early_kernel(b_ref, a_ref, o_ref):
    for i, block in enumerate(packed_products(b_ref, a_ref)):
        o_ref[i * TILE : (i + 1) * TILE, :] = block


def late_kernel(place_ref, b_ref, a_ref, early_ref, keep_ref, give_ref, scratch):
    for i, block in enumerate(packed_products(b_ref, a_ref)):
        scratch[i * TILE : (i + 1) * TILE, LANES:] = block
    scratch[:, :LANES] = early_ref[...]
    half = keep_ref.shape[0]
    core = place_ref[2]
    keep_ref[...] = scratch[pl.ds(pl.multiple_of(core * half, SUB), half), :]
    give_ref[...] = scratch[pl.ds(pl.multiple_of((1 - core) * half, SUB), half), :]


def eliminate(panels, cols):
    first, width = cols
    tile, lane0 = first // LANES, first % LANES
    lane = lax.broadcasted_iota(jnp.int32, (SUB, LANES), 1)
    sub = lax.broadcasted_iota(jnp.int32, (SUB, LANES), 0)
    strips = width // SUB
    states = []
    for panel in panels:
        state = [[panel[i * SUB : (i + 1) * SUB, a : a + LANES] for a in range(0, panel.shape[1], LANES)] for i in range(strips)]
        unit = [jnp.where(lane == lane0 + i * SUB + sub, 1.0, 0.0) for i in range(strips)]
        states.append([line + [u] for line, u in zip(state, unit)])
    scales = [[jnp.ones((SUB, LANES), jnp.float32) for _ in range(strips)] for _ in panels]

    def spread(row, like):
        return jnp.broadcast_to(row, (SUB, like.shape[1]))

    for j in range(0, width, STEP):
        strip, off = j // SUB, j % SUB
        for m, state in enumerate(states):
            columns = [
                [jnp.broadcast_to(state[i][tile][:, lane0 + j + s : lane0 + j + s + 1], (SUB, LANES)) for i in range(strip, strips)]
                for s in range(STEP)
            ]
            rows = [[spread(part[off + r : off + r + 1, :], part) for part in state[strip]] for r in range(STEP)]
            small = [[spread(columns[s][0][off + r : off + r + 1, :], columns[s][0]) for s in range(STEP)] for r in range(STEP)]
            inverse = []
            pivots = []
            for r in range(STEP):
                pivots.append(small[r][r])
                inverse.append(1.0 / small[r][r])
                for q in range(r + 1, STEP):
                    ratio = small[q][r] * inverse[r]
                    rows[q] = [a - ratio[:, : a.shape[1]] * b for a, b in zip(rows[q], rows[r])]
                    columns[q] = [a - ratio * b for a, b in zip(columns[q], columns[r])]
                    for p in range(q, STEP):
                        small[p][q] = small[p][q] - ratio * small[p][r]
            weights = [[a * inverse[s] for a in columns[s]] for s in range(STEP)]
            for i in range(strip, strips):
                line = []
                for n, part in enumerate(state[i]):
                    value = part
                    for s in range(STEP):
                        value = value - weights[s][i - strip][:, : part.shape[1]] * rows[s][n]
                    if i == strip:
                        at = sub[:, : part.shape[1]]
                        if off:
                            value = jnp.where(at < off, part, value)
                        for r in range(STEP):
                            value = jnp.where(at == off + r, rows[r][n], value)
                    line.append(value)
                state[i] = line
            for r in range(STEP):
                scales[m][strip] = jnp.where(sub == off + r, pivots[r], scales[m][strip])
    results = []
    for state, scale in zip(states, scales):
        inverse, reduced = [], []
        for line, pivot in zip(state, scale):
            root = lax.rsqrt(pivot)
            root = root * (1.5 - 0.5 * pivot * root * root)
            inverse.append(line[-1] * root)
            reduced.append(jnp.concatenate([part * root[:, : part.shape[1]] for part in line[:-1]], 1))
        results.append((jnp.concatenate(inverse, 0), jnp.concatenate(reduced, 0)))
    return results


def dot(a, b, dims):
    return lax.dot_general(
        a, b, ((dims[:1], dims[1:]), ((), ())), precision=lax.Precision.HIGHEST, preferred_element_type=jnp.float32
    )


def factor(scratch, total):
    count = scratch.shape[0]
    lane = lax.broadcasted_iota(jnp.int32, (1, total), 1)
    for first in range(0, total, BLOCK):
        last = first + BLOCK
        here = (lane >= first) & (lane < last)
        results = eliminate([scratch[m, first:last, :] for m in range(count)], (first, BLOCK))
        for m, (inverse, reduced) in enumerate(results):
            tile = first // LANES * LANES
            side = min(LANES, total - tile)
            parts = []
            if tile:
                parts.append(jnp.zeros((BLOCK, tile), jnp.float32))
            parts.append(inverse[:, :side])
            if tile + side < total:
                parts.append(jnp.zeros((BLOCK, total - tile - side), jnp.float32))
            inverse = jnp.concatenate(parts, 1)
            row = jnp.where(here, inverse, reduced)
            scratch[m, first:last, :] = jnp.where(lane < last, row, 0.0)
            if last < total:
                rest = scratch[m, last:, :]
                lower = dot(rest, inverse, (1, 1))
                scratch[m, last:, :] = jnp.where(here, 0.0, rest) - dot(lower, row, (1, 0))


def tail_kernel(place_ref, own_ref, other_ref, w_ref, o_ref, ray_ref, packed, grams, scratch, *, cells):
    groups, per, comps, nvec = w_ref.shape[:4]
    total = groups * nvec
    scale = 1.0 / cells
    pieces, quarter = own_ref.shape[:2]
    for k in range(pieces):
        at = ((place_ref[1] + pieces - k) % pieces) * quarter
        for side, ref in ((place_ref[2], own_ref), (1 - place_ref[2], other_ref)):
            row = pl.multiple_of(side * pieces * quarter + at, SUB)
            packed[pl.ds(row, quarter), :] = ref[k] * scale
    for m in range(4):
        target, n = (grams, m // 2) if m % 2 == 0 else (scratch, m // 2)
        for q, (i, j) in enumerate(PAIRS):
            block = packed[q * TILE : (q + 1) * TILE, m * TILE : (m + 1) * TILE]
            target[n, i * TILE : (i + 1) * TILE, j * TILE : (j + 1) * TILE] = block
            if i != j:
                target[n, j * TILE : (j + 1) * TILE, i * TILE : (i + 1) * TILE] = block.T
    factor(scratch, total)
    inv = scratch[1]
    for k in range(per * comps // 2):
        out = dot(inv, wide(w_ref, k), (1, 0))
        for j in range(2):
            t, c = (2 * k + j) // comps, (2 * k + j) % comps
            for g in range(groups):
                o_ref[g, t, c] = out[g * nvec : (g + 1) * nvec, j * LANES : (j + 1) * LANES]
    own = pl.ds(pl.multiple_of(place_ref[0] * nvec, SUB), nvec)
    ray_ref[0] = grams[0, own, :]
    rows = dot(scratch[0, own, :], grams[1], (1, 0))
    ray_ref[1] = dot(rows, scratch[0], (1, 1))


def call(kernel, out, operands, scratch=(), smem=0, flops=0):
    specs = [pl.BlockSpec(memory_space=pltpu.SMEM)] * smem
    specs += [pl.BlockSpec(memory_space=pltpu.VMEM)] * (len(operands) - smem)
    size = sum(a.size * 4 for a in operands) + 4
    return pl.pallas_call(
        kernel,
        out_shape=jax.tree.map(lambda dims: jax.ShapeDtypeStruct(dims, jnp.float32), out, is_leaf=lambda d: isinstance(d[0], int)),
        in_specs=specs,
        out_specs=jax.tree.map(lambda dims: pl.BlockSpec(memory_space=pltpu.VMEM), out, is_leaf=lambda d: isinstance(d[0], int)),
        scratch_shapes=list(scratch),
        compiler_params=pltpu.CompilerParams(vmem_limit_bytes=VMEM_LIMIT),
        cost_estimate=pl.CostEstimate(flops=flops, bytes_accessed=size, transcendentals=0),
    )(*operands)


def total_over_all(keep, give):
    y = (lax.axis_index("space") // 2) % 4
    quarter = keep.shape[0] // 4

    def to_core(zl, y, c, x, zh):
        return (zl, y, 1 - c, x, zh)

    mine = keep + route(give, to_core)

    def chunk(k):
        return lax.dynamic_slice_in_dim(mine, ((y + k) % 4) * quarter, quarter, 0)

    def along_y(k):
        return lambda zl, y, c, x, zh: (zl, (y + k) % 4, c, x, zh)

    def along_x(k):
        return lambda zl, y, c, x, zh: (zl, y, c, (x + k) % 4, zh)

    def along_z(k):
        def move(zl, y, c, x, zh):
            z = (zh * 2 + zl + k) % 4
            return (z % 2, y, c, x, z // 2)

        return move

    got = [route(chunk(k), along_y(k)) for k in (1, 2, 3)]
    mine = (chunk(0) + got[1]) + (got[0] + got[2])
    for along in (along_x, along_z):
        got = [route(mine, along(k)) for k in (1, 2, 3)]
        mine = (mine + got[1]) + (got[0] + got[2])
    own = jnp.stack([mine] + [route(mine, along_y(k)) for k in (1, 2, 3)])
    return own, route(own, to_core)


def local(vectors, labels, stiffness, mass):
    nvec, comps, _, plane = vectors.shape
    groups = lax.axis_size("vec")
    total = nvec * groups
    nz = lax.axis_size("space")
    cells = 3.0 * nz * plane
    tiles = plane // LANES
    per = tiles // groups
    z = lax.axis_index("space")
    h = lax.axis_index("vec")

    below = step_along(labels, "space", 1)
    lab = labels.reshape(plane // NX, NX)
    row = lax.broadcasted_iota(jnp.int32, lab.shape, 0)
    col = lax.broadcasted_iota(jnp.int32, lab.shape, 1)
    none = LEVELS
    upper = jnp.concatenate([jnp.full((1, NX), none, jnp.int32), lab[:-1]], 0)
    faces = jnp.stack(
        [
            jnp.where(col == NX - 1, none, lab),
            jnp.where(row == lab.shape[0] - 1, none, lab),
            upper,
            jnp.where(z == nz - 1, none, lab),
            jnp.where(z == 0, none, below.reshape(lab.shape)),
            lab,
        ]
    )
    faces = faces.reshape(6, tiles, LANES)
    faces = lax.dynamic_slice_in_dim(faces, rows_of(h) * per, per, 1)
    stiff = stiffness.reshape(-1)

    shape = (groups, per, comps, nvec, LANES)

    def apply(u):
        zd = step_along(u, "space", 1)
        zu = step_along(u, "space", -1)
        yd = step_along(u[:, per - 1], "vec", 1)
        yu = step_along(u[:, 0], "vec", -1)
        return call(
            stencil_kernel,
            shape,
            (stiff, mass, faces, u, zd, zu, yd, yu),
            scratch=[pltpu.VMEM((per, 31, SUB, LANES), jnp.float32)],
            smem=2,
            flops=20_000_000,
        )

    start = call(
        functools.partial(spread_kernel, nvec=nvec, tiles=tiles),
        shape,
        (vectors.reshape(nvec * comps * tiles, LANES),),
    )
    v = lax.all_to_all(start, "vec", 0, 0)
    w1 = apply(v)
    w2 = apply(w1)
    place = jnp.stack([h, (z // 2) % 4, z % 2]).astype(jnp.int32)
    work = total * total * per * comps * LANES
    packed = len(PAIRS) * TILE
    early = call(early_kernel, (packed, LANES), (v, w1), flops=24 * work)
    keep, give = call(
        late_kernel,
        [(packed // 2, 2 * LANES)] * 2,
        (place, w1, w2, early),
        scratch=[pltpu.VMEM((packed, 2 * LANES), jnp.float32)],
        smem=1,
        flops=24 * work,
    )
    own, other = total_over_all(keep, give)
    out, rayleigh = call(
        functools.partial(tail_kernel, cells=cells),
        [shape, (2, nvec, total)],
        (place, own, other, w2),
        scratch=[
            pltpu.VMEM((packed, 2 * LANES), jnp.float32),
            pltpu.VMEM((2, total, total), jnp.float32),
            pltpu.VMEM((2, total, total), jnp.float32),
        ],
        smem=1,
        flops=14 * work,
    )
    out = lax.all_to_all(out, "vec", 0, 0)
    refined = call(
        functools.partial(collect_kernel, nvec=nvec, tiles=tiles),
        (nvec * comps * tiles, LANES),
        (out,),
    )
    return refined.reshape(vectors.shape), rayleigh


def solution(mesh):
    return jax.shard_map(
        local,
        mesh=mesh,
        in_specs=(P("vec", None, "space", None), P("space", None), P(), P()),
        out_specs=(P("vec", None, "space", None), P(None, "vec", None)),
        check_vma=False,
    )
```

```python
import functools

import jax
import jax.numpy as jnp
from jax import lax
from jax.experimental import pallas as pl
from jax.experimental.pallas import tpu as pltpu
from jax.sharding import PartitionSpec as P

NX = 64
LANES = 128
SUB = 8
LEVELS = 4
BLOCK = 32
STEP = 4
ENTRIES = ((0, 0), (0, 1), (0, 2), (1, 1), (1, 2), (2, 2))
ENTRY_OF = {pair: i for i, pair in enumerate(ENTRIES)}
VMEM_LIMIT = 48 * 1024 * 1024
SPACE = (2, 4, 2)
VEC = (4, 2)
TILE = 64
PAIRS = ((0, 0), (1, 0), (1, 1), (2, 0), (2, 1), (2, 2))


def rows_of(device):
    x, far = device // VEC[1], device % VEC[1]
    return x + far * (2 * VEC[0] - 1 - 2 * x)


DEVICE_OF = sorted(range(VEC[0] * VEC[1]), key=rows_of)


def route(array, move):
    pairs = []
    for zl in range(SPACE[0]):
        for y in range(SPACE[1]):
            for core in range(SPACE[2]):
                for x in range(VEC[0]):
                    for zh in range(VEC[1]):
                        a, b, c, d, e = move(zl, y, core, x, zh)
                        here = (((zl * SPACE[1] + y) * SPACE[2] + core) * VEC[0] + x) * VEC[1] + zh
                        there = (((a * SPACE[1] + b) * SPACE[2] + c) * VEC[0] + d) * VEC[1] + e
                        pairs.append((here, there))
    return lax.ppermute(array, ("space", "vec"), pairs)


def step_along(array, axis, by):
    order = DEVICE_OF if axis == "vec" else range(lax.axis_size(axis))
    pairs = [(order[i], order[i + by]) for i in range(len(order)) if 0 <= i + by < len(order)]
    return lax.ppermute(array, axis, pairs)


def partner(place_ref, k):
    return jnp.bitwise_xor(place_ref[0], k)


def spread_kernel(place_ref, x_ref, *o_refs, tiles):
    per, comps, nvec = o_refs[0].shape[:3]
    stride = comps * tiles
    for k, o_ref in enumerate(o_refs):
        first = rows_of(partner(place_ref, k)) * per
        for t in range(per):
            for c in range(comps):
                for v in range(0, nvec, SUB):
                    rows = pl.ds(first + (v * stride + c * tiles + t), SUB, stride)
                    o_ref[t, c, v : v + SUB, :] = x_ref[rows, :]


def collect_kernel(place_ref, *refs, tiles):
    o_ref = refs[-1]
    per, comps, nvec = refs[0].shape[:3]
    stride = comps * tiles
    for k, x_ref in enumerate(refs[:-1]):
        first = rows_of(partner(place_ref, k)) * per
        for t in range(per):
            for c in range(comps):
                for v in range(0, nvec, SUB):
                    rows = pl.ds(first + (v * stride + c * tiles + t), SUB, stride)
                    o_ref[rows, :] = x_ref[t, c, v : v + SUB, :]


def turn(a):
    return pltpu.roll(a, NX, 1)


def pack_edges(low, near, far, first_ref, last_ref, at):
    first_ref[at] = jnp.where(low, near[0], turn(far[0]))
    last_ref[at] = jnp.where(low, turn(near[1]), far[1])


def gather_kernel(place_ref, *refs):
    pieces, (o_ref, first_ref, last_ref) = refs[:-3], refs[-3:]
    groups, per, comps, nvec = o_ref.shape[:4]
    for k, x_ref in enumerate(pieces):
        o_ref[partner(place_ref, k)] = x_ref[...]
    low = lax.broadcasted_iota(jnp.int32, (SUB, LANES), 1) < NX
    for q in range(groups // 2):
        for c in range(comps):
            for v in range(0, nvec, SUB):
                rows = slice(v, v + SUB)
                near, far = [[o_ref[g, t, c, rows, :] for t in (0, per - 1)] for g in (q, q + groups // 2)]
                pack_edges(low, near, far, first_ref, last_ref, (q, c, rows, slice(None)))


def stencil_kernel(stiff_ref, mass_ref, cls_ref, u_ref, za_ref, zb_ref, yd_ref, yu_ref, w_ref, *rest):
    edges, coef_ref = rest[:-1], rest[-1]
    groups, per, comps, nvec = u_ref.shape[:4]
    lane = lax.broadcasted_iota(jnp.int32, (SUB, LANES), 1)
    low = lane < NX

    def pick(cls, values):
        out = jnp.zeros((SUB, LANES), jnp.float32)
        for level in range(LEVELS):
            out = jnp.where(cls == level, values[level], out)
        return out

    for t in range(per):
        for face, direction in enumerate((0, 1, 1, 2, 2)):
            cls = jnp.broadcast_to(cls_ref[face, t : t + 1, :], (SUB, LANES))
            for i, (a, b) in enumerate(ENTRIES):
                spots = [((level * 3 + direction) * 3 + a) * 3 + b for level in range(LEVELS)]
                coef_ref[t, face * 6 + i] = pick(cls, [stiff_ref[s] for s in spots])
        cls = jnp.broadcast_to(cls_ref[5, t : t + 1, :], (SUB, LANES))
        coef_ref[t, 30] = pick(cls, [mass_ref[level] for level in range(LEVELS)])

    def mix(t, face, d):
        s = [coef_ref[t, face * 6 + i] for i in range(6)]
        return [
            s[ENTRY_OF[min(a, 0), max(a, 0)]] * d[0]
            + s[ENTRY_OF[min(a, 1), max(a, 1)]] * d[1]
            + s[ENTRY_OF[min(a, 2), max(a, 2)]] * d[2]
            for a in range(3)
        ]

    steps = nvec // SUB
    half = groups // 2

    def body(i, carry):
        q = i // steps
        rows = pl.ds(pl.multiple_of((i % steps) * SUB, SUB), SUB)
        ends = []
        for part in range(2):
            g = q + part * half
            tiles = [[u_ref[g, t, c, rows, :] for c in range(3)] for t in range(per)]
            below = [yd_ref[q, c, rows, :] for c in range(3)]
            above = [yu_ref[q, c, rows, :] for c in range(3)]
            if part == 0:
                above = [turn(a) for a in above]
            else:
                below = [turn(a) for a in below]
            swaps = [below] + [[turn(a) for a in line] for line in tiles] + [above]
            done = []
            for t in range(per):
                u = tiles[t]
                f = mix(t, 0, [pltpu.roll(u[c], LANES - 1, 1) - u[c] for c in range(3)])
                acc = [coef_ref[t, 30] * u[c] + (pltpu.roll(f[c], 1, 1) - f[c]) for c in range(3)]
                f = mix(t, 1, [jnp.where(low, swaps[t + 1][c], swaps[t + 2][c]) - u[c] for c in range(3)])
                acc = [acc[c] - f[c] for c in range(3)]
                f = mix(t, 2, [u[c] - jnp.where(low, swaps[t][c], swaps[t + 1][c]) for c in range(3)])
                acc = [acc[c] + f[c] for c in range(3)]
                f = mix(t, 3, [za_ref[g, t, c, rows, :] - u[c] for c in range(3)])
                acc = [acc[c] - f[c] for c in range(3)]
                f = mix(t, 4, [zb_ref[g, t, c, rows, :] - u[c] for c in range(3)])
                done.append([acc[c] - f[c] for c in range(3)])
                for c in range(3):
                    w_ref[g, t, c, rows, :] = done[t][c]
            ends.append((done[0], done[-1]))
        if edges:
            for c in range(3):
                near, far = [[end[c] for end in pair] for pair in ends]
                pack_edges(low, near, far, *edges, (q, c, rows, slice(None)))
        return carry

    lax.fori_loop(0, half * steps, body, 0)


def stacked(ref, t, c):
    groups = ref.shape[0]
    return jnp.concatenate([ref[g, t, c] for g in range(groups)], 0)


def wide(ref, k):
    comps = ref.shape[2]
    return jnp.concatenate([stacked(ref, (2 * k + j) // comps, (2 * k + j) % comps) for j in range(2)], 1)


def packed_products(b_ref, a_ref):
    chunks = a_ref.shape[1] * a_ref.shape[2] // 2
    total = None
    for k in range(chunks):
        a, b = wide(a_ref, k), wide(b_ref, k)
        both = [side[i : i + TILE] for i in range(0, a.shape[0], TILE) for side in (b, a)]
        part = dot(a, jnp.concatenate(both, 0), (1, 1))
        total = part if total is None else total + part
    return [total[i * TILE : (i + 1) * TILE, j * LANES : (j + 1) * LANES] for i, j in PAIRS]


def early_kernel(b_ref, a_ref, o_ref):
    for i, block in enumerate(packed_products(b_ref, a_ref)):
        o_ref[i * TILE : (i + 1) * TILE, :] = block


def late_kernel(place_ref, b_ref, a_ref, early_ref, keep_ref, give_ref, scratch):
    for i, block in enumerate(packed_products(b_ref, a_ref)):
        scratch[i * TILE : (i + 1) * TILE, LANES:] = block
    scratch[:, :LANES] = early_ref[...]
    half = keep_ref.shape[0]
    core = place_ref[2]
    keep_ref[...] = scratch[pl.ds(pl.multiple_of(core * half, SUB), half), :]
    give_ref[...] = scratch[pl.ds(pl.multiple_of((1 - core) * half, SUB), half), :]


def eliminate(panels, cols):
    first, width = cols
    tile, lane0 = first // LANES, first % LANES
    lane = lax.broadcasted_iota(jnp.int32, (SUB, LANES), 1)
    sub = lax.broadcasted_iota(jnp.int32, (SUB, LANES), 0)
    strips = width // SUB
    states = []
    for panel in panels:
        state = [[panel[i * SUB : (i + 1) * SUB, a : a + LANES] for a in range(0, panel.shape[1], LANES)] for i in range(strips)]
        unit = [jnp.where(lane == lane0 + i * SUB + sub, 1.0, 0.0) for i in range(strips)]
        states.append([line + [u] for line, u in zip(state, unit)])
    scales = [[jnp.ones((SUB, LANES), jnp.float32) for _ in range(strips)] for _ in panels]

    def spread(row, like):
        return jnp.broadcast_to(row, (SUB, like.shape[1]))

    for j in range(0, width, STEP):
        strip, off = j // SUB, j % SUB
        for m, state in enumerate(states):
            columns = [
                [jnp.broadcast_to(state[i][tile][:, lane0 + j + s : lane0 + j + s + 1], (SUB, LANES)) for i in range(strip, strips)]
                for s in range(STEP)
            ]
            rows = [[spread(part[off + r : off + r + 1, :], part) for part in state[strip]] for r in range(STEP)]
            small = [[spread(columns[s][0][off + r : off + r + 1, :], columns[s][0]) for s in range(STEP)] for r in range(STEP)]
            inverse = []
            pivots = []
            for r in range(STEP):
                pivots.append(small[r][r])
                inverse.append(1.0 / small[r][r])
                for q in range(r + 1, STEP):
                    ratio = small[q][r] * inverse[r]
                    rows[q] = [a - ratio[:, : a.shape[1]] * b for a, b in zip(rows[q], rows[r])]
                    columns[q] = [a - ratio * b for a, b in zip(columns[q], columns[r])]
                    for p in range(q, STEP):
                        small[p][q] = small[p][q] - ratio * small[p][r]
            weights = [[a * inverse[s] for a in columns[s]] for s in range(STEP)]
            for i in range(strip, strips):
                line = []
                for n, part in enumerate(state[i]):
                    value = part
                    for s in range(STEP):
                        value = value - weights[s][i - strip][:, : part.shape[1]] * rows[s][n]
                    if i == strip:
                        at = sub[:, : part.shape[1]]
                        if off:
                            value = jnp.where(at < off, part, value)
                        for r in range(STEP):
                            value = jnp.where(at == off + r, rows[r][n], value)
                    line.append(value)
                state[i] = line
            for r in range(STEP):
                scales[m][strip] = jnp.where(sub == off + r, pivots[r], scales[m][strip])
    results = []
    for state, scale in zip(states, scales):
        inverse, reduced = [], []
        for line, pivot in zip(state, scale):
            root = lax.rsqrt(pivot)
            root = root * (1.5 - 0.5 * pivot * root * root)
            inverse.append(line[-1] * root)
            reduced.append(jnp.concatenate([part * root[:, : part.shape[1]] for part in line[:-1]], 1))
        results.append((jnp.concatenate(inverse, 0), jnp.concatenate(reduced, 0)))
    return results


def dot(a, b, dims):
    return lax.dot_general(
        a, b, ((dims[:1], dims[1:]), ((), ())), precision=lax.Precision.HIGHEST, preferred_element_type=jnp.float32
    )


def factor(scratch, total):
    count = scratch.shape[0]
    lane = lax.broadcasted_iota(jnp.int32, (1, total), 1)
    for first in range(0, total, BLOCK):
        last = first + BLOCK
        here = (lane >= first) & (lane < last)
        results = eliminate([scratch[m, first:last, :] for m in range(count)], (first, BLOCK))
        for m, (inverse, reduced) in enumerate(results):
            tile = first // LANES * LANES
            side = min(LANES, total - tile)
            parts = []
            if tile:
                parts.append(jnp.zeros((BLOCK, tile), jnp.float32))
            parts.append(inverse[:, :side])
            if tile + side < total:
                parts.append(jnp.zeros((BLOCK, total - tile - side), jnp.float32))
            inverse = jnp.concatenate(parts, 1)
            row = jnp.where(here, inverse, reduced)
            scratch[m, first:last, :] = jnp.where(lane < last, row, 0.0)
            if last < total:
                rest = scratch[m, last:, :]
                lower = dot(rest, inverse, (1, 1))
                scratch[m, last:, :] = jnp.where(here, 0.0, rest) - dot(lower, row, (1, 0))


def tail_kernel(place_ref, own_ref, other_ref, w_ref, *refs, cells):
    o_refs, (ray_ref, packed, grams, scratch) = refs[:-4], refs[-4:]
    groups, per, comps, nvec = w_ref.shape[:4]
    total = groups * nvec
    scale = 1.0 / cells
    pieces, quarter = own_ref.shape[:2]
    for k in range(pieces):
        at = ((place_ref[1] + pieces - k) % pieces) * quarter
        for side, ref in ((place_ref[2], own_ref), (1 - place_ref[2], other_ref)):
            row = pl.multiple_of(side * pieces * quarter + at, SUB)
            packed[pl.ds(row, quarter), :] = ref[k] * scale
    for m in range(4):
        target, n = (grams, m // 2) if m % 2 == 0 else (scratch, m // 2)
        for q, (i, j) in enumerate(PAIRS):
            block = packed[q * TILE : (q + 1) * TILE, m * TILE : (m + 1) * TILE]
            target[n, i * TILE : (i + 1) * TILE, j * TILE : (j + 1) * TILE] = block
            if i != j:
                target[n, j * TILE : (j + 1) * TILE, i * TILE : (i + 1) * TILE] = block.T
    factor(scratch, total)
    order = [pl.ds(pl.multiple_of(partner(place_ref, k) * nvec, SUB), nvec) for k in range(groups)]
    inv = jnp.concatenate([scratch[1, rows, :] for rows in order], 0)
    for n in range(per * comps // 2):
        out = dot(inv, wide(w_ref, n), (1, 0))
        for j in range(2):
            t, c = (2 * n + j) // comps, (2 * n + j) % comps
            for k in range(groups):
                o_refs[k][t, c] = out[k * nvec : (k + 1) * nvec, j * LANES : (j + 1) * LANES]
    own = pl.ds(pl.multiple_of(place_ref[0] * nvec, SUB), nvec)
    ray_ref[0] = grams[0, own, :]
    rows = dot(scratch[0, own, :], grams[1], (1, 0))
    ray_ref[1] = dot(rows, scratch[0], (1, 1))


def call(kernel, out, operands, scratch=(), smem=0, flops=0):
    specs = [pl.BlockSpec(memory_space=pltpu.SMEM)] * smem
    specs += [pl.BlockSpec(memory_space=pltpu.VMEM)] * (len(operands) - smem)
    size = sum(a.size * 4 for a in operands) + 4
    return pl.pallas_call(
        kernel,
        out_shape=jax.tree.map(lambda dims: jax.ShapeDtypeStruct(dims, jnp.float32), out, is_leaf=lambda d: isinstance(d[0], int)),
        in_specs=specs,
        out_specs=jax.tree.map(lambda dims: pl.BlockSpec(memory_space=pltpu.VMEM), out, is_leaf=lambda d: isinstance(d[0], int)),
        scratch_shapes=list(scratch),
        compiler_params=pltpu.CompilerParams(vmem_limit_bytes=VMEM_LIMIT),
        cost_estimate=pl.CostEstimate(flops=flops, bytes_accessed=size, transcendentals=0),
    )(*operands)


def total_over_all(keep, give):
    y = (lax.axis_index("space") // 2) % 4
    quarter = keep.shape[0] // 4

    def to_core(zl, y, c, x, zh):
        return (zl, y, 1 - c, x, zh)

    mine = keep + route(give, to_core)

    def chunk(k):
        return lax.dynamic_slice_in_dim(mine, ((y + k) % 4) * quarter, quarter, 0)

    def along_y(k):
        return lambda zl, y, c, x, zh: (zl, (y + k) % 4, c, x, zh)

    def along_x(k):
        return lambda zl, y, c, x, zh: (zl, y, c, (x + k) % 4, zh)

    def along_z(k):
        def move(zl, y, c, x, zh):
            z = (zh * 2 + zl + k) % 4
            return (z % 2, y, c, x, z // 2)

        return move

    got = [route(chunk(k), along_y(k)) for k in (1, 2, 3)]
    mine = (chunk(0) + got[1]) + (got[0] + got[2])
    for along in (along_x, along_z):
        got = [route(mine, along(k)) for k in (1, 2, 3)]
        mine = (mine + got[1]) + (got[0] + got[2])
    own = jnp.stack([mine] + [route(mine, along_y(k)) for k in (1, 2, 3)])
    return own, route(own, to_core)


def local(vectors, labels, stiffness, mass):
    nvec, comps, _, plane = vectors.shape
    groups = lax.axis_size("vec")
    total = nvec * groups
    nz = lax.axis_size("space")
    cells = 3.0 * nz * plane
    tiles = plane // LANES
    per = tiles // groups
    z = lax.axis_index("space")
    h = lax.axis_index("vec")

    below = step_along(labels, "space", 1)
    lab = labels.reshape(plane // NX, NX)
    row = lax.broadcasted_iota(jnp.int32, lab.shape, 0)
    col = lax.broadcasted_iota(jnp.int32, lab.shape, 1)
    none = LEVELS
    upper = jnp.concatenate([jnp.full((1, NX), none, jnp.int32), lab[:-1]], 0)
    over = jnp.where(z == nz - 1, none, lab)
    under = jnp.where(z == 0, none, below.reshape(lab.shape))
    core = z % 2
    faces = jnp.stack(
        [
            jnp.where(col == NX - 1, none, lab),
            jnp.where(row == lab.shape[0] - 1, none, lab),
            upper,
            jnp.where(core == 0, under, over),
            jnp.where(core == 0, over, under),
            lab,
        ]
    )
    faces = faces.reshape(6, tiles, LANES)
    faces = lax.dynamic_slice_in_dim(faces, rows_of(h) * per, per, 1)
    stiff = stiffness.reshape(-1)

    piece = (per, comps, nvec, LANES)
    shape = (groups,) + piece
    edge = (groups // 2, comps, nvec, LANES)

    def exchange(pieces):
        return [pieces[0]] + [
            lax.ppermute(pieces[k], "vec", [(i, i ^ k) for i in range(groups)]) for k in range(1, groups)
        ]

    def apply(u, first, last, more):
        za = lax.ppermute(u, "space", [(i, i + (1 if i % 2 else -1)) for i in range(1, nz - 1)])
        zb = lax.ppermute(u, "space", [(i, i ^ 1) for i in range(nz)])
        yd = step_along(last, "vec", 1)
        yu = step_along(first, "vec", -1)
        return call(
            stencil_kernel,
            [shape, edge, edge] if more else [shape],
            (stiff, mass, faces, u, za, zb, yd, yu),
            scratch=[pltpu.VMEM((per, 31, SUB, LANES), jnp.float32)],
            smem=2,
            flops=20_000_000,
        )

    place = jnp.stack([h, (z // 2) % 4, core]).astype(jnp.int32)
    work = total * total * per * comps * LANES
    packed = len(PAIRS) * TILE
    pieces = call(
        functools.partial(spread_kernel, tiles=tiles),
        [piece] * groups,
        (place, vectors.reshape(nvec * comps * tiles, LANES)),
        smem=1,
    )
    v, first, last = call(gather_kernel, [shape, edge, edge], [place] + exchange(pieces), smem=1)
    w1, first, last = apply(v, first, last, True)
    (w2,) = apply(w1, first, last, False)
    early = call(early_kernel, (packed, LANES), (v, w1), flops=24 * work)
    keep, give = call(
        late_kernel,
        [(packed // 2, 2 * LANES)] * 2,
        (place, w1, w2, early),
        scratch=[pltpu.VMEM((packed, 2 * LANES), jnp.float32)],
        smem=1,
        flops=24 * work,
    )
    own, other = total_over_all(keep, give)
    *pieces, rayleigh = call(
        functools.partial(tail_kernel, cells=cells),
        [piece] * groups + [(2, nvec, total)],
        (place, own, other, w2),
        scratch=[
            pltpu.VMEM((packed, 2 * LANES), jnp.float32),
            pltpu.VMEM((2, total, total), jnp.float32),
            pltpu.VMEM((2, total, total), jnp.float32),
        ],
        smem=1,
        flops=14 * work,
    )
    refined = call(
        functools.partial(collect_kernel, tiles=tiles),
        (nvec * comps * tiles, LANES),
        [place] + exchange(pieces),
        smem=1,
    )
    return refined.reshape(vectors.shape), rayleigh


def solution(mesh):
    return jax.shard_map(
        local,
        mesh=mesh,
        in_specs=(P("vec", None, "space", None), P("space", None), P(), P()),
        out_specs=(P("vec", None, "space", None), P(None, "vec", None)),
        check_vma=False,
    )
```

```python
import functools

import jax
import jax.numpy as jnp
from jax import lax
from jax.experimental import pallas as pl
from jax.experimental.pallas import tpu as pltpu
from jax.sharding import PartitionSpec as P

NX = 64
LANES = 128
SUB = 8
LEVELS = 4
BLOCK = 64
STEP = 8
ORDER = (0, 7, 5, 3, 4, 1, 6, 2)
ENTRIES = ((0, 0), (0, 1), (0, 2), (1, 1), (1, 2), (2, 2))
ENTRY_OF = {pair: i for i, pair in enumerate(ENTRIES)}
VMEM_LIMIT = 48 * 1024 * 1024
SPACE = (2, 4, 2)
VEC = (4, 2)
TILE = 64
PAIRS = ((0, 0), (1, 0), (1, 1), (2, 0), (2, 1), (2, 2))


def rows_of(device):
    x, far = device // VEC[1], device % VEC[1]
    return x + far * (2 * VEC[0] - 1 - 2 * x)


DEVICE_OF = sorted(range(VEC[0] * VEC[1]), key=rows_of)


def route(array, move):
    pairs = []
    for zl in range(SPACE[0]):
        for y in range(SPACE[1]):
            for core in range(SPACE[2]):
                for x in range(VEC[0]):
                    for zh in range(VEC[1]):
                        a, b, c, d, e = move(zl, y, core, x, zh)
                        here = (((zl * SPACE[1] + y) * SPACE[2] + core) * VEC[0] + x) * VEC[1] + zh
                        there = (((a * SPACE[1] + b) * SPACE[2] + c) * VEC[0] + d) * VEC[1] + e
                        pairs.append((here, there))
    return lax.ppermute(array, ("space", "vec"), pairs)


def step_along(array, axis, by):
    order = DEVICE_OF if axis == "vec" else range(lax.axis_size(axis))
    pairs = [(order[i], order[i + by]) for i in range(len(order)) if 0 <= i + by < len(order)]
    return lax.ppermute(array, axis, pairs)


def partner(place_ref, k):
    return jnp.bitwise_xor(place_ref[0], k)


def spread_kernel(place_ref, x_ref, *o_refs, tiles):
    per, comps, nvec = o_refs[0].shape[:3]
    stride = comps * tiles
    for k, o_ref in zip(ORDER, o_refs):
        first = rows_of(partner(place_ref, k)) * per
        for t in range(per):
            for c in range(comps):
                for v in range(0, nvec, SUB):
                    rows = pl.ds(first + (v * stride + c * tiles + t), SUB, stride)
                    o_ref[t, c, v : v + SUB, :] = x_ref[rows, :]


def collect_kernel(place_ref, *refs, tiles):
    o_ref = refs[-1]
    per, comps, nvec = refs[0].shape[:3]
    stride = comps * tiles
    for k, x_ref in zip(ORDER, refs[:-1]):
        first = rows_of(partner(place_ref, k)) * per
        for t in range(per):
            for c in range(comps):
                for v in range(0, nvec, SUB):
                    rows = pl.ds(first + (v * stride + c * tiles + t), SUB, stride)
                    o_ref[rows, :] = x_ref[t, c, v : v + SUB, :]


def turn(a):
    return pltpu.roll(a, NX, 1)


def pack_edges(low, near, far, first_ref, last_ref, at):
    first_ref[at] = jnp.where(low, near[0], turn(far[0]))
    last_ref[at] = jnp.where(low, turn(near[1]), far[1])


def gather_kernel(place_ref, *refs):
    pieces, (o_ref, first_ref, last_ref) = refs[:-3], refs[-3:]
    groups, per, comps, nvec = o_ref.shape[:4]
    for k, x_ref in zip(ORDER, pieces):
        o_ref[partner(place_ref, k)] = x_ref[...]
    low = lax.broadcasted_iota(jnp.int32, (SUB, LANES), 1) < NX
    for q in range(groups // 2):
        for c in range(comps):
            for v in range(0, nvec, SUB):
                rows = slice(v, v + SUB)
                near, far = [[o_ref[g, t, c, rows, :] for t in (0, per - 1)] for g in (q, q + groups // 2)]
                pack_edges(low, near, far, first_ref, last_ref, (q, c, rows, slice(None)))


def stencil_kernel(stiff_ref, mass_ref, cls_ref, u_ref, yd_ref, yu_ref, za_ref, zb_ref, w_ref, *rest):
    edges, coef_ref = rest[:-1], rest[-1]
    groups, per, comps, nvec = u_ref.shape[:4]
    lane = lax.broadcasted_iota(jnp.int32, (SUB, LANES), 1)
    low = lane < NX

    def pick(cls, values):
        out = jnp.zeros((SUB, LANES), jnp.float32)
        for level in range(LEVELS):
            out = jnp.where(cls == level, values[level], out)
        return out

    for t in range(per):
        for face, direction in enumerate((0, 1, 1, 2, 2)):
            cls = jnp.broadcast_to(cls_ref[face, t : t + 1, :], (SUB, LANES))
            for i, (a, b) in enumerate(ENTRIES):
                spots = [((level * 3 + direction) * 3 + a) * 3 + b for level in range(LEVELS)]
                coef_ref[t, face * 6 + i] = pick(cls, [stiff_ref[s] for s in spots])
        cls = jnp.broadcast_to(cls_ref[5, t : t + 1, :], (SUB, LANES))
        coef_ref[t, 30] = pick(cls, [mass_ref[level] for level in range(LEVELS)])

    def mix(t, face, d):
        s = [coef_ref[t, face * 6 + i] for i in range(6)]
        return [
            s[ENTRY_OF[min(a, 0), max(a, 0)]] * d[0]
            + s[ENTRY_OF[min(a, 1), max(a, 1)]] * d[1]
            + s[ENTRY_OF[min(a, 2), max(a, 2)]] * d[2]
            for a in range(3)
        ]

    steps = nvec // SUB
    half = groups // 2

    def body(i, carry):
        q = i // steps
        rows = pl.ds(pl.multiple_of((i % steps) * SUB, SUB), SUB)
        ends = []
        for part in range(2):
            g = q + part * half
            tiles = [[u_ref[g, t, c, rows, :] for c in range(3)] for t in range(per)]
            below = [yd_ref[q, c, rows, :] for c in range(3)]
            above = [yu_ref[q, c, rows, :] for c in range(3)]
            if part == 0:
                above = [turn(a) for a in above]
            else:
                below = [turn(a) for a in below]
            swaps = [below] + [[turn(a) for a in line] for line in tiles] + [above]
            done = []
            for t in range(per):
                u = tiles[t]
                f = mix(t, 0, [pltpu.roll(u[c], LANES - 1, 1) - u[c] for c in range(3)])
                acc = [coef_ref[t, 30] * u[c] + (pltpu.roll(f[c], 1, 1) - f[c]) for c in range(3)]
                f = mix(t, 1, [jnp.where(low, swaps[t + 1][c], swaps[t + 2][c]) - u[c] for c in range(3)])
                acc = [acc[c] - f[c] for c in range(3)]
                f = mix(t, 2, [u[c] - jnp.where(low, swaps[t][c], swaps[t + 1][c]) for c in range(3)])
                acc = [acc[c] + f[c] for c in range(3)]
                f = mix(t, 3, [za_ref[g, t, c, rows, :] - u[c] for c in range(3)])
                acc = [acc[c] - f[c] for c in range(3)]
                f = mix(t, 4, [zb_ref[g, t, c, rows, :] - u[c] for c in range(3)])
                done.append([acc[c] - f[c] for c in range(3)])
                for c in range(3):
                    w_ref[g, t, c, rows, :] = done[t][c]
            ends.append((done[0], done[-1]))
        if edges:
            for c in range(3):
                near, far = [[end[c] for end in pair] for pair in ends]
                pack_edges(low, near, far, *edges, (q, c, rows, slice(None)))
        return carry

    lax.fori_loop(0, half * steps, body, 0)


def stacked(ref, t, c):
    groups = ref.shape[0]
    return jnp.concatenate([ref[g, t, c] for g in range(groups)], 0)


def wide(ref, k):
    comps = ref.shape[2]
    return jnp.concatenate([stacked(ref, (2 * k + j) // comps, (2 * k + j) % comps) for j in range(2)], 1)


def packed_products(b_ref, a_ref):
    chunks = a_ref.shape[1] * a_ref.shape[2] // 2
    total = None
    for k in range(chunks):
        a, b = wide(a_ref, k), wide(b_ref, k)
        both = [side[i : i + TILE] for i in range(0, a.shape[0], TILE) for side in (b, a)]
        part = dot(a, jnp.concatenate(both, 0), (1, 1))
        total = part if total is None else total + part
    return [total[i * TILE : (i + 1) * TILE, j * LANES : (j + 1) * LANES] for i, j in PAIRS]


def early_kernel(b_ref, a_ref, o_ref):
    for i, block in enumerate(packed_products(b_ref, a_ref)):
        o_ref[i * TILE : (i + 1) * TILE, :] = block


def late_kernel(place_ref, b_ref, a_ref, early_ref, keep_ref, give_ref, scratch):
    for i, block in enumerate(packed_products(b_ref, a_ref)):
        scratch[i * TILE : (i + 1) * TILE, LANES:] = block
    scratch[:, :LANES] = early_ref[...]
    half = keep_ref.shape[0]
    core = place_ref[2]
    keep_ref[...] = scratch[pl.ds(pl.multiple_of(core * half, SUB), half), :]
    give_ref[...] = scratch[pl.ds(pl.multiple_of((1 - core) * half, SUB), half), :]


def eliminate(panels, cols):
    first, width = cols
    tile, lane0 = first // LANES, first % LANES
    lane = lax.broadcasted_iota(jnp.int32, (SUB, LANES), 1)
    sub = lax.broadcasted_iota(jnp.int32, (SUB, LANES), 0)
    strips = width // SUB
    states = []
    for panel in panels:
        state = [[panel[i * SUB : (i + 1) * SUB, a : a + LANES] for a in range(0, panel.shape[1], LANES)] for i in range(strips)]
        unit = [jnp.where(lane == lane0 + i * SUB + sub, 1.0, 0.0) for i in range(strips)]
        states.append([line + [u] for line, u in zip(state, unit)])
    scales = [[jnp.ones((SUB, LANES), jnp.float32) for _ in range(strips)] for _ in panels]

    def spread(row, like):
        return jnp.broadcast_to(row, (SUB, like.shape[1]))

    for j in range(0, width, STEP):
        strip, off = j // SUB, j % SUB
        for m, state in enumerate(states):
            columns = [
                [jnp.broadcast_to(state[i][tile][:, lane0 + j + s : lane0 + j + s + 1], (SUB, LANES)) for i in range(strip, strips)]
                for s in range(STEP)
            ]
            rows = [[spread(part[off + r : off + r + 1, :], part) for part in state[strip]] for r in range(STEP)]
            small = [[spread(columns[s][0][off + r : off + r + 1, :], columns[s][0]) for s in range(STEP)] for r in range(STEP)]
            inverse = []
            pivots = []
            for r in range(STEP):
                pivots.append(small[r][r])
                inverse.append(1.0 / small[r][r])
                for q in range(r + 1, STEP):
                    ratio = small[q][r] * inverse[r]
                    rows[q] = [a - ratio[:, : a.shape[1]] * b for a, b in zip(rows[q], rows[r])]
                    columns[q] = [a - ratio * b for a, b in zip(columns[q], columns[r])]
                    for p in range(q, STEP):
                        small[p][q] = small[p][q] - ratio * small[p][r]
            weights = [[a * inverse[s] for a in columns[s]] for s in range(STEP)]
            for i in range(strip, strips):
                line = []
                for n, part in enumerate(state[i]):
                    value = part
                    for s in range(STEP):
                        value = value - weights[s][i - strip][:, : part.shape[1]] * rows[s][n]
                    if i == strip:
                        at = sub[:, : part.shape[1]]
                        if off:
                            value = jnp.where(at < off, part, value)
                        for r in range(STEP):
                            value = jnp.where(at == off + r, rows[r][n], value)
                    line.append(value)
                state[i] = line
            for r in range(STEP):
                scales[m][strip] = jnp.where(sub == off + r, pivots[r], scales[m][strip])
    results = []
    for state, scale in zip(states, scales):
        inverse, reduced = [], []
        for line, pivot in zip(state, scale):
            root = lax.rsqrt(pivot)
            root = root * (1.5 - 0.5 * pivot * root * root)
            inverse.append(line[-1] * root)
            reduced.append(jnp.concatenate([part * root[:, : part.shape[1]] for part in line[:-1]], 1))
        results.append((jnp.concatenate(inverse, 0), jnp.concatenate(reduced, 0)))
    return results


def dot(a, b, dims):
    return lax.dot_general(
        a, b, ((dims[:1], dims[1:]), ((), ())), precision=lax.Precision.HIGHEST, preferred_element_type=jnp.float32
    )


def factor(scratch, total):
    count = scratch.shape[0]
    lane = lax.broadcasted_iota(jnp.int32, (1, total), 1)
    for first in range(0, total, BLOCK):
        last = first + BLOCK
        here = (lane >= first) & (lane < last)
        results = eliminate([scratch[m, first:last, :] for m in range(count)], (first, BLOCK))
        for m, (inverse, reduced) in enumerate(results):
            tile = first // LANES * LANES
            side = min(LANES, total - tile)
            parts = []
            if tile:
                parts.append(jnp.zeros((BLOCK, tile), jnp.float32))
            parts.append(inverse[:, :side])
            if tile + side < total:
                parts.append(jnp.zeros((BLOCK, total - tile - side), jnp.float32))
            inverse = jnp.concatenate(parts, 1)
            row = jnp.where(here, inverse, reduced)
            scratch[m, first:last, :] = jnp.where(lane < last, row, 0.0)
            if last < total:
                rest = scratch[m, last:, :]
                lower = dot(rest, inverse, (1, 1))
                scratch[m, last:, :] = jnp.where(here, 0.0, rest) - dot(lower, row, (1, 0))


def unpack(place_ref, own_ref, other_ref, packed, targets, scale):
    pieces, quarter = own_ref.shape[:2]
    for k in range(pieces):
        at = ((place_ref[1] + pieces - k) % pieces) * quarter
        for side, ref in ((place_ref[2], own_ref), (1 - place_ref[2], other_ref)):
            row = pl.multiple_of(side * pieces * quarter + at, SUB)
            packed[pl.ds(row, quarter), :] = ref[k] * scale
    for m, target in targets:
        for q, (i, j) in enumerate(PAIRS):
            block = packed[q * TILE : (q + 1) * TILE, m * TILE : (m + 1) * TILE]
            target[i * TILE : (i + 1) * TILE, j * TILE : (j + 1) * TILE] = block
            if i != j:
                target[j * TILE : (j + 1) * TILE, i * TILE : (i + 1) * TILE] = block.T


def combine_kernel(place_ref, own_ref, other_ref, w_ref, *refs, cells):
    o_refs, (packed, scratch) = refs[:-2], refs[-2:]
    groups, per, comps, nvec = w_ref.shape[:4]
    total = groups * nvec
    unpack(place_ref, own_ref, other_ref, packed, [(3, scratch.at[0])], 1.0 / cells)
    factor(scratch, total)
    order = [pl.ds(pl.multiple_of(partner(place_ref, k) * nvec, SUB), nvec) for k in ORDER]
    inv = jnp.concatenate([scratch[0, rows, :] for rows in order], 0)
    for n in range(per * comps // 2):
        out = dot(inv, wide(w_ref, n), (1, 0))
        for j in range(2):
            t, c = (2 * n + j) // comps, (2 * n + j) % comps
            for k in range(groups):
                o_refs[k][t, c] = out[k * nvec : (k + 1) * nvec, j * LANES : (j + 1) * LANES]


def rayleigh_kernel(place_ref, own_ref, other_ref, ray_ref, packed, grams, scratch, *, cells):
    nvec, total = ray_ref.shape[1:]
    targets = [(0, grams.at[0]), (1, scratch.at[0]), (2, grams.at[1])]
    unpack(place_ref, own_ref, other_ref, packed, targets, 1.0 / cells)
    factor(scratch, total)
    own = pl.ds(pl.multiple_of(place_ref[0] * nvec, SUB), nvec)
    ray_ref[0] = grams[0, own, :]
    rows = dot(scratch[0, own, :], grams[1], (1, 0))
    ray_ref[1] = dot(rows, scratch[0], (1, 1))


def call(kernel, out, operands, scratch=(), smem=0, flops=0):
    specs = [pl.BlockSpec(memory_space=pltpu.SMEM)] * smem
    specs += [pl.BlockSpec(memory_space=pltpu.VMEM)] * (len(operands) - smem)
    size = sum(a.size * 4 for a in operands) + 4
    return pl.pallas_call(
        kernel,
        out_shape=jax.tree.map(lambda dims: jax.ShapeDtypeStruct(dims, jnp.float32), out, is_leaf=lambda d: isinstance(d[0], int)),
        in_specs=specs,
        out_specs=jax.tree.map(lambda dims: pl.BlockSpec(memory_space=pltpu.VMEM), out, is_leaf=lambda d: isinstance(d[0], int)),
        scratch_shapes=list(scratch),
        compiler_params=pltpu.CompilerParams(vmem_limit_bytes=VMEM_LIMIT),
        cost_estimate=pl.CostEstimate(flops=flops, bytes_accessed=size, transcendentals=0),
    )(*operands)


def total_over_all(keep, give):
    y = (lax.axis_index("space") // 2) % 4
    quarter = keep.shape[0] // 4

    def to_core(zl, y, c, x, zh):
        return (zl, y, 1 - c, x, zh)

    mine = keep + route(give, to_core)

    def chunk(k):
        return lax.dynamic_slice_in_dim(mine, ((y + k) % 4) * quarter, quarter, 0)

    def along_y(k):
        return lambda zl, y, c, x, zh: (zl, (y + k) % 4, c, x, zh)

    def along_x(k):
        return lambda zl, y, c, x, zh: (zl, y, c, (x + k) % 4, zh)

    def along_z(k):
        def move(zl, y, c, x, zh):
            z = (zh * 2 + zl + k) % 4
            return (z % 2, y, c, x, z // 2)

        return move

    got = [route(chunk(k), along_y(k)) for k in (1, 2, 3)]
    mine = (chunk(0) + got[1]) + (got[0] + got[2])
    for along in (along_x, along_z):
        got = [route(mine, along(k)) for k in (1, 2, 3)]
        mine = (mine + got[1]) + (got[0] + got[2])
    own = jnp.stack([mine] + [route(mine, along_y(k)) for k in (1, 2, 3)])
    return own, route(own, to_core)


def local(vectors, labels, stiffness, mass):
    nvec, comps, _, plane = vectors.shape
    groups = lax.axis_size("vec")
    total = nvec * groups
    nz = lax.axis_size("space")
    cells = 3.0 * nz * plane
    tiles = plane // LANES
    per = tiles // groups
    z = lax.axis_index("space")
    h = lax.axis_index("vec")

    below = step_along(labels, "space", 1)
    lab = labels.reshape(plane // NX, NX)
    row = lax.broadcasted_iota(jnp.int32, lab.shape, 0)
    col = lax.broadcasted_iota(jnp.int32, lab.shape, 1)
    none = LEVELS
    upper = jnp.concatenate([jnp.full((1, NX), none, jnp.int32), lab[:-1]], 0)
    over = jnp.where(z == nz - 1, none, lab)
    under = jnp.where(z == 0, none, below.reshape(lab.shape))
    core = z % 2
    faces = jnp.stack(
        [
            jnp.where(col == NX - 1, none, lab),
            jnp.where(row == lab.shape[0] - 1, none, lab),
            upper,
            jnp.where(core == 0, under, over),
            jnp.where(core == 0, over, under),
            lab,
        ]
    )
    faces = faces.reshape(6, tiles, LANES)
    faces = lax.dynamic_slice_in_dim(faces, rows_of(h) * per, per, 1)
    stiff = stiffness.reshape(-1)

    piece = (per, comps, nvec, LANES)
    shape = (groups,) + piece
    edge = (groups // 2, comps, nvec, LANES)

    def exchange(pieces):
        got = [lax.ppermute(a, "vec", [(i, i ^ k) for i in range(groups)]) for k, a in zip(ORDER[1:], pieces[1:])]
        return [pieces[0]] + got

    def apply(u, first, last, more):
        yd = step_along(last, "vec", 1)
        yu = step_along(first, "vec", -1)
        za = lax.ppermute(u, "space", [(i, i + (1 if i % 2 else -1)) for i in range(1, nz - 1)])
        zb = lax.ppermute(u, "space", [(i, i ^ 1) for i in range(nz)])
        return call(
            stencil_kernel,
            [shape, edge, edge] if more else [shape],
            (stiff, mass, faces, u, yd, yu, za, zb),
            scratch=[pltpu.VMEM((per, 31, SUB, LANES), jnp.float32)],
            smem=2,
            flops=20_000_000,
        )

    place = jnp.stack([h, (z // 2) % 4, core]).astype(jnp.int32)
    work = total * total * per * comps * LANES
    packed = len(PAIRS) * TILE
    pieces = call(
        functools.partial(spread_kernel, tiles=tiles),
        [piece] * groups,
        (place, vectors.reshape(nvec * comps * tiles, LANES)),
        smem=1,
    )
    v, first, last = call(gather_kernel, [shape, edge, edge], [place] + exchange(pieces), smem=1)
    w1, first, last = apply(v, first, last, True)
    (w2,) = apply(w1, first, last, False)
    early = call(early_kernel, (packed, LANES), (v, w1), flops=24 * work)
    keep, give = call(
        late_kernel,
        [(packed // 2, 2 * LANES)] * 2,
        (place, w1, w2, early),
        scratch=[pltpu.VMEM((packed, 2 * LANES), jnp.float32)],
        smem=1,
        flops=24 * work,
    )
    own, other = total_over_all(keep, give)
    pieces = call(
        functools.partial(combine_kernel, cells=cells),
        [piece] * groups,
        (place, own, other, w2),
        scratch=[pltpu.VMEM((packed, 2 * LANES), jnp.float32), pltpu.VMEM((1, total, total), jnp.float32)],
        smem=1,
        flops=12 * work,
    )
    *pieces, own, other = lax.optimization_barrier((*pieces, own, other))
    (rayleigh,) = call(
        functools.partial(rayleigh_kernel, cells=cells),
        [(2, nvec, total)],
        (place, own, other),
        scratch=[
            pltpu.VMEM((packed, 2 * LANES), jnp.float32),
            pltpu.VMEM((2, total, total), jnp.float32),
            pltpu.VMEM((1, total, total), jnp.float32),
        ],
        smem=1,
        flops=2 * work,
    )
    refined = call(
        functools.partial(collect_kernel, tiles=tiles),
        (nvec * comps * tiles, LANES),
        [place] + exchange(pieces),
        smem=1,
    )
    return refined.reshape(vectors.shape), rayleigh


def solution(mesh):
    return jax.shard_map(
        local,
        mesh=mesh,
        in_specs=(P("vec", None, "space", None), P("space", None), P(), P()),
        out_specs=(P("vec", None, "space", None), P(None, "vec", None)),
        check_vma=False,
    )
```

```python
import functools

import jax
import jax.numpy as jnp
from jax import lax
from jax.experimental import pallas as pl
from jax.experimental.pallas import tpu as pltpu
from jax.sharding import PartitionSpec as P

NX = 64
LANES = 128
SUB = 8
LEVELS = 4
BLOCK = 64
STEP = 8
ORDER = (0, 7, 5, 3, 4, 1, 6, 2)
ENTRIES = ((0, 0), (0, 1), (0, 2), (1, 1), (1, 2), (2, 2))
ENTRY_OF = {pair: i for i, pair in enumerate(ENTRIES)}
VMEM_LIMIT = 48 * 1024 * 1024
SPACE = (2, 4, 2)
VEC = (4, 2)
TILE = 64
PAIRS = ((0, 0), (1, 0), (1, 1), (2, 0), (2, 1), (2, 2))


def rows_of(device):
    x, far = device // VEC[1], device % VEC[1]
    return x + far * (2 * VEC[0] - 1 - 2 * x)


DEVICE_OF = sorted(range(VEC[0] * VEC[1]), key=rows_of)


def route(array, move):
    pairs = []
    for zl in range(SPACE[0]):
        for y in range(SPACE[1]):
            for core in range(SPACE[2]):
                for x in range(VEC[0]):
                    for zh in range(VEC[1]):
                        a, b, c, d, e = move(zl, y, core, x, zh)
                        here = (((zl * SPACE[1] + y) * SPACE[2] + core) * VEC[0] + x) * VEC[1] + zh
                        there = (((a * SPACE[1] + b) * SPACE[2] + c) * VEC[0] + d) * VEC[1] + e
                        pairs.append((here, there))
    return lax.ppermute(array, ("space", "vec"), pairs)


def step_along(array, axis, by):
    order = DEVICE_OF if axis == "vec" else range(lax.axis_size(axis))
    pairs = [(order[i], order[i + by]) for i in range(len(order)) if 0 <= i + by < len(order)]
    return lax.ppermute(array, axis, pairs)


def partner(place_ref, k):
    return jnp.bitwise_xor(place_ref[0], k)


def spread_kernel(place_ref, x_ref, *o_refs, tiles):
    per, comps, nvec = o_refs[0].shape[:3]
    stride = comps * tiles
    for k, o_ref in zip(ORDER, o_refs):
        first = rows_of(partner(place_ref, k)) * per
        for t in range(per):
            for c in range(comps):
                for v in range(0, nvec, SUB):
                    rows = pl.ds(first + (v * stride + c * tiles + t), SUB, stride)
                    o_ref[t, c, v : v + SUB, :] = x_ref[rows, :]


def collect_kernel(place_ref, *refs, tiles):
    o_ref = refs[-1]
    per, comps, nvec = refs[0].shape[:3]
    stride = comps * tiles
    for k, x_ref in zip(ORDER, refs[:-1]):
        first = rows_of(partner(place_ref, k)) * per
        for t in range(per):
            for c in range(comps):
                for v in range(0, nvec, SUB):
                    rows = pl.ds(first + (v * stride + c * tiles + t), SUB, stride)
                    o_ref[rows, :] = x_ref[t, c, v : v + SUB, :]


def turn(a):
    return pltpu.roll(a, NX, 1)


def pack_edges(low, near, far, first_ref, last_ref, at):
    first_ref[at] = jnp.where(low, near[0], turn(far[0]))
    last_ref[at] = jnp.where(low, turn(near[1]), far[1])


def gather_kernel(place_ref, *refs):
    pieces, (o_ref, first_ref, last_ref) = refs[:-3], refs[-3:]
    groups, per, comps, nvec = o_ref.shape[:4]
    for k, x_ref in zip(ORDER, pieces):
        o_ref[partner(place_ref, k)] = x_ref[...]
    low = lax.broadcasted_iota(jnp.int32, (SUB, LANES), 1) < NX
    for q in range(groups // 2):
        for c in range(comps):
            for v in range(0, nvec, SUB):
                rows = slice(v, v + SUB)
                near, far = [[o_ref[g, t, c, rows, :] for t in (0, per - 1)] for g in (q, q + groups // 2)]
                pack_edges(low, near, far, first_ref, last_ref, (q, c, rows, slice(None)))


def stencil_kernel(stiff_ref, mass_ref, cls_ref, u_ref, yd_ref, yu_ref, za_ref, zb_ref, w_ref, *rest):
    edges, coef_ref = rest[:-1], rest[-1]
    groups, per, comps, nvec = u_ref.shape[:4]
    lane = lax.broadcasted_iota(jnp.int32, (SUB, LANES), 1)
    low = lane < NX

    def pick(cls, values):
        out = jnp.zeros((SUB, LANES), jnp.float32)
        for level in range(LEVELS):
            out = jnp.where(cls == level, values[level], out)
        return out

    for t in range(per):
        for face, direction in enumerate((0, 1, 1, 2, 2)):
            cls = jnp.broadcast_to(cls_ref[face, t : t + 1, :], (SUB, LANES))
            for i, (a, b) in enumerate(ENTRIES):
                spots = [((level * 3 + direction) * 3 + a) * 3 + b for level in range(LEVELS)]
                coef_ref[t, face * 6 + i] = pick(cls, [stiff_ref[s] for s in spots])
        cls = jnp.broadcast_to(cls_ref[5, t : t + 1, :], (SUB, LANES))
        coef_ref[t, 30] = pick(cls, [mass_ref[level] for level in range(LEVELS)])

    def mix(t, face, d):
        s = [coef_ref[t, face * 6 + i] for i in range(6)]
        return [
            s[ENTRY_OF[min(a, 0), max(a, 0)]] * d[0]
            + s[ENTRY_OF[min(a, 1), max(a, 1)]] * d[1]
            + s[ENTRY_OF[min(a, 2), max(a, 2)]] * d[2]
            for a in range(3)
        ]

    steps = nvec // SUB
    half = groups // 2

    def body(i, carry):
        q = i // steps
        rows = pl.ds(pl.multiple_of((i % steps) * SUB, SUB), SUB)
        ends = []
        for part in range(2):
            g = q + part * half
            tiles = [[u_ref[g, t, c, rows, :] for c in range(3)] for t in range(per)]
            below = [yd_ref[q, c, rows, :] for c in range(3)]
            above = [yu_ref[q, c, rows, :] for c in range(3)]
            if part == 0:
                above = [turn(a) for a in above]
            else:
                below = [turn(a) for a in below]
            swaps = [below] + [[turn(a) for a in line] for line in tiles] + [above]
            done = []
            for t in range(per):
                u = tiles[t]
                f = mix(t, 0, [pltpu.roll(u[c], LANES - 1, 1) - u[c] for c in range(3)])
                acc = [coef_ref[t, 30] * u[c] + (pltpu.roll(f[c], 1, 1) - f[c]) for c in range(3)]
                f = mix(t, 1, [jnp.where(low, swaps[t + 1][c], swaps[t + 2][c]) - u[c] for c in range(3)])
                acc = [acc[c] - f[c] for c in range(3)]
                f = mix(t, 2, [u[c] - jnp.where(low, swaps[t][c], swaps[t + 1][c]) for c in range(3)])
                acc = [acc[c] + f[c] for c in range(3)]
                f = mix(t, 3, [za_ref[g, t, c, rows, :] - u[c] for c in range(3)])
                acc = [acc[c] - f[c] for c in range(3)]
                f = mix(t, 4, [zb_ref[g, t, c, rows, :] - u[c] for c in range(3)])
                done.append([acc[c] - f[c] for c in range(3)])
                for c in range(3):
                    w_ref[g, t, c, rows, :] = done[t][c]
            ends.append((done[0], done[-1]))
        if edges:
            for c in range(3):
                near, far = [[end[c] for end in pair] for pair in ends]
                pack_edges(low, near, far, *edges, (q, c, rows, slice(None)))
        return carry

    lax.fori_loop(0, half * steps, body, 0)


def stacked(ref, t, c):
    groups = ref.shape[0]
    return jnp.concatenate([ref[g, t, c] for g in range(groups)], 0)


def wide(ref, k):
    comps = ref.shape[2]
    return jnp.concatenate([stacked(ref, (2 * k + j) // comps, (2 * k + j) % comps) for j in range(2)], 1)


def packed_products(b_ref, a_ref):
    chunks = a_ref.shape[1] * a_ref.shape[2] // 2
    total = None
    for k in range(chunks):
        a, b = wide(a_ref, k), wide(b_ref, k)
        both = [side[i : i + TILE] for i in range(0, a.shape[0], TILE) for side in (b, a)]
        part = dot(a, jnp.concatenate(both, 0), (1, 1))
        total = part if total is None else total + part
    return [total[i * TILE : (i + 1) * TILE, j * LANES : (j + 1) * LANES] for i, j in PAIRS]


def early_kernel(b_ref, a_ref, o_ref):
    for i, block in enumerate(packed_products(b_ref, a_ref)):
        o_ref[i * TILE : (i + 1) * TILE, :] = block


def late_kernel(place_ref, b_ref, a_ref, early_ref, keep_ref, give_ref):
    even = place_ref[2] == 0
    for i, block in enumerate(packed_products(b_ref, a_ref)):
        rows = slice(i * TILE, (i + 1) * TILE)
        early = early_ref[rows, :]
        keep_ref[rows, :] = jnp.where(even, block, early)
        give_ref[rows, :] = jnp.where(even, early, block)


def eliminate(panels, cols):
    first, width = cols
    tile, lane0 = first // LANES, first % LANES
    lane = lax.broadcasted_iota(jnp.int32, (SUB, LANES), 1)
    sub = lax.broadcasted_iota(jnp.int32, (SUB, LANES), 0)
    strips = width // SUB
    states = []
    for panel in panels:
        state = [[panel[i * SUB : (i + 1) * SUB, a : a + LANES] for a in range(0, panel.shape[1], LANES)] for i in range(strips)]
        unit = [jnp.where(lane == lane0 + i * SUB + sub, 1.0, 0.0) for i in range(strips)]
        states.append([line + [u] for line, u in zip(state, unit)])
    scales = [[jnp.ones((SUB, LANES), jnp.float32) for _ in range(strips)] for _ in panels]

    def spread(row, like):
        return jnp.broadcast_to(row, (SUB, like.shape[1]))

    for j in range(0, width, STEP):
        strip, off = j // SUB, j % SUB
        for m, state in enumerate(states):
            columns = [
                [jnp.broadcast_to(state[i][tile][:, lane0 + j + s : lane0 + j + s + 1], (SUB, LANES)) for i in range(strip, strips)]
                for s in range(STEP)
            ]
            rows = [[spread(part[off + r : off + r + 1, :], part) for part in state[strip]] for r in range(STEP)]
            small = [[spread(columns[s][0][off + r : off + r + 1, :], columns[s][0]) for s in range(STEP)] for r in range(STEP)]
            inverse = []
            pivots = []
            for r in range(STEP):
                pivots.append(small[r][r])
                inverse.append(1.0 / small[r][r])
                for q in range(r + 1, STEP):
                    ratio = small[q][r] * inverse[r]
                    rows[q] = [a - ratio[:, : a.shape[1]] * b for a, b in zip(rows[q], rows[r])]
                    columns[q] = [a - ratio * b for a, b in zip(columns[q], columns[r])]
                    for p in range(q, STEP):
                        small[p][q] = small[p][q] - ratio * small[p][r]
            weights = [[a * inverse[s] for a in columns[s]] for s in range(STEP)]
            for i in range(strip, strips):
                line = []
                for n, part in enumerate(state[i]):
                    value = part
                    for s in range(STEP):
                        value = value - weights[s][i - strip][:, : part.shape[1]] * rows[s][n]
                    if i == strip:
                        at = sub[:, : part.shape[1]]
                        if off:
                            value = jnp.where(at < off, part, value)
                        for r in range(STEP):
                            value = jnp.where(at == off + r, rows[r][n], value)
                    line.append(value)
                state[i] = line
            for r in range(STEP):
                scales[m][strip] = jnp.where(sub == off + r, pivots[r], scales[m][strip])
    results = []
    for state, scale in zip(states, scales):
        inverse, reduced = [], []
        for line, pivot in zip(state, scale):
            root = lax.rsqrt(pivot)
            root = root * (1.5 - 0.5 * pivot * root * root)
            inverse.append(line[-1] * root)
            reduced.append(jnp.concatenate([part * root[:, : part.shape[1]] for part in line[:-1]], 1))
        results.append((jnp.concatenate(inverse, 0), jnp.concatenate(reduced, 0)))
    return results


def dot(a, b, dims):
    return lax.dot_general(
        a, b, ((dims[:1], dims[1:]), ((), ())), precision=lax.Precision.HIGHEST, preferred_element_type=jnp.float32
    )


def factor(scratch, total):
    count = scratch.shape[0]
    lane = lax.broadcasted_iota(jnp.int32, (1, total), 1)
    for first in range(0, total, BLOCK):
        last = first + BLOCK
        here = (lane >= first) & (lane < last)
        results = eliminate([scratch[m, first:last, :] for m in range(count)], (first, BLOCK))
        for m, (inverse, reduced) in enumerate(results):
            tile = first // LANES * LANES
            side = min(LANES, total - tile)
            parts = []
            if tile:
                parts.append(jnp.zeros((BLOCK, tile), jnp.float32))
            parts.append(inverse[:, :side])
            if tile + side < total:
                parts.append(jnp.zeros((BLOCK, total - tile - side), jnp.float32))
            inverse = jnp.concatenate(parts, 1)
            row = jnp.where(here, inverse, reduced)
            scratch[m, first:last, :] = jnp.where(lane < last, row, 0.0)
            if last < total:
                rest = scratch[m, last:, :]
                lower = dot(rest, inverse, (1, 1))
                scratch[m, last:, :] = jnp.where(here, 0.0, rest) - dot(lower, row, (1, 0))


def factor_kernel(place_ref, own_ref, o_ref, packed, scratch, *, cells):
    pieces, quarter = own_ref.shape[:2]
    total = o_ref.shape[1]
    for k in range(pieces):
        at = ((place_ref[1] + pieces - k) % pieces) * quarter
        packed[pl.ds(pl.multiple_of(at, SUB), quarter), :] = own_ref[k] * (1.0 / cells)
    for m, target in enumerate((o_ref.at[1], scratch.at[0])):
        for q, (i, j) in enumerate(PAIRS):
            block = packed[q * TILE : (q + 1) * TILE, m * TILE : (m + 1) * TILE]
            target[i * TILE : (i + 1) * TILE, j * TILE : (j + 1) * TILE] = block
            if i != j:
                target[j * TILE : (j + 1) * TILE, i * TILE : (i + 1) * TILE] = block.T
    factor(scratch, total)
    o_ref[0] = scratch[0]


def combine_kernel(place_ref, mine_ref, other_ref, w_ref, *o_refs):
    per, comps, nvec = w_ref.shape[1:4]
    groups = w_ref.shape[0]
    even = place_ref[2] == 0
    order = [pl.ds(pl.multiple_of(partner(place_ref, k) * nvec, SUB), nvec) for k in ORDER]
    inv = jnp.concatenate([jnp.where(even, mine_ref[0, rows, :], other_ref[0, rows, :]) for rows in order], 0)
    for n in range(per * comps // 2):
        out = dot(inv, wide(w_ref, n), (1, 0))
        for j in range(2):
            t, c = (2 * n + j) // comps, (2 * n + j) % comps
            for k in range(groups):
                o_refs[k][t, c] = out[k * nvec : (k + 1) * nvec, j * LANES : (j + 1) * LANES]


def rayleigh_kernel(place_ref, mine_ref, other_ref, ray_ref):
    nvec = ray_ref.shape[1]
    even = place_ref[2] == 0
    own = pl.ds(pl.multiple_of(place_ref[0] * nvec, SUB), nvec)
    ray_ref[0] = jnp.where(even, other_ref[1, own, :], mine_ref[1, own, :])
    rows = jnp.where(even, other_ref[0, own, :], mine_ref[0, own, :])
    rows = dot(rows, jnp.where(even, mine_ref[1], other_ref[1]), (1, 0))
    ray_ref[1] = dot(rows, jnp.where(even, other_ref[0], mine_ref[0]), (1, 1))


def call(kernel, out, operands, scratch=(), smem=0, flops=0):
    specs = [pl.BlockSpec(memory_space=pltpu.SMEM)] * smem
    specs += [pl.BlockSpec(memory_space=pltpu.VMEM)] * (len(operands) - smem)
    size = sum(a.size * 4 for a in operands) + 4
    return pl.pallas_call(
        kernel,
        out_shape=jax.tree.map(lambda dims: jax.ShapeDtypeStruct(dims, jnp.float32), out, is_leaf=lambda d: isinstance(d[0], int)),
        in_specs=specs,
        out_specs=jax.tree.map(lambda dims: pl.BlockSpec(memory_space=pltpu.VMEM), out, is_leaf=lambda d: isinstance(d[0], int)),
        scratch_shapes=list(scratch),
        compiler_params=pltpu.CompilerParams(vmem_limit_bytes=VMEM_LIMIT),
        cost_estimate=pl.CostEstimate(flops=flops, bytes_accessed=size, transcendentals=0),
    )(*operands)


def to_core(zl, y, core, x, zh):
    return (zl, y, 1 - core, x, zh)


def total_over_all(keep, give):
    y = (lax.axis_index("space") // 2) % 4
    quarter = keep.shape[0] // 4
    mine = keep + route(give, to_core)

    def chunk(k):
        return lax.dynamic_slice_in_dim(mine, ((y + k) % 4) * quarter, quarter, 0)

    def along_y(k):
        return lambda zl, y, c, x, zh: (zl, (y + k) % 4, c, x, zh)

    def along_x(k):
        return lambda zl, y, c, x, zh: (zl, y, c, (x + k) % 4, zh)

    def along_z(k):
        def move(zl, y, c, x, zh):
            z = (zh * 2 + zl + k) % 4
            return (z % 2, y, c, x, z // 2)

        return move

    got = [route(chunk(k), along_y(k)) for k in (1, 2, 3)]
    mine = (chunk(0) + got[1]) + (got[0] + got[2])
    for along in (along_x, along_z):
        got = [route(mine, along(k)) for k in (1, 2, 3)]
        mine = (mine + got[1]) + (got[0] + got[2])
    return jnp.stack([mine] + [route(mine, along_y(k)) for k in (1, 2, 3)])


def local(vectors, labels, stiffness, mass):
    nvec, comps, _, plane = vectors.shape
    groups = lax.axis_size("vec")
    total = nvec * groups
    nz = lax.axis_size("space")
    cells = 3.0 * nz * plane
    tiles = plane // LANES
    per = tiles // groups
    z = lax.axis_index("space")
    h = lax.axis_index("vec")

    below = step_along(labels, "space", 1)
    lab = labels.reshape(plane // NX, NX)
    row = lax.broadcasted_iota(jnp.int32, lab.shape, 0)
    col = lax.broadcasted_iota(jnp.int32, lab.shape, 1)
    none = LEVELS
    upper = jnp.concatenate([jnp.full((1, NX), none, jnp.int32), lab[:-1]], 0)
    over = jnp.where(z == nz - 1, none, lab)
    under = jnp.where(z == 0, none, below.reshape(lab.shape))
    core = z % 2
    faces = jnp.stack(
        [
            jnp.where(col == NX - 1, none, lab),
            jnp.where(row == lab.shape[0] - 1, none, lab),
            upper,
            jnp.where(core == 0, under, over),
            jnp.where(core == 0, over, under),
            lab,
        ]
    )
    faces = faces.reshape(6, tiles, LANES)
    faces = lax.dynamic_slice_in_dim(faces, rows_of(h) * per, per, 1)
    stiff = stiffness.reshape(-1)

    piece = (per, comps, nvec, LANES)
    shape = (groups,) + piece
    edge = (groups // 2, comps, nvec, LANES)

    def exchange(pieces):
        got = [lax.ppermute(a, "vec", [(i, i ^ k) for i in range(groups)]) for k, a in zip(ORDER[1:], pieces[1:])]
        return [pieces[0]] + got

    def apply(u, first, last, more):
        yd = step_along(last, "vec", 1)
        yu = step_along(first, "vec", -1)
        za = lax.ppermute(u, "space", [(i, i + (1 if i % 2 else -1)) for i in range(1, nz - 1)])
        zb = lax.ppermute(u, "space", [(i, i ^ 1) for i in range(nz)])
        return call(
            stencil_kernel,
            [shape, edge, edge] if more else [shape],
            (stiff, mass, faces, u, yd, yu, za, zb),
            scratch=[pltpu.VMEM((per, 31, SUB, LANES), jnp.float32)],
            smem=2,
            flops=20_000_000,
        )

    place = jnp.stack([h, (z // 2) % 4, core]).astype(jnp.int32)
    work = total * total * per * comps * LANES
    packed = len(PAIRS) * TILE
    pieces = call(
        functools.partial(spread_kernel, tiles=tiles),
        [piece] * groups,
        (place, vectors.reshape(nvec * comps * tiles, LANES)),
        smem=1,
    )
    v, first, last = call(gather_kernel, [shape, edge, edge], [place] + exchange(pieces), smem=1)
    w1, first, last = apply(v, first, last, True)
    (w2,) = apply(w1, first, last, False)
    early = call(early_kernel, (packed, LANES), (v, w1), flops=24 * work)
    keep, give = call(
        late_kernel,
        [(packed, LANES)] * 2,
        (place, w1, w2, early),
        smem=1,
        flops=24 * work,
    )
    (mine,) = call(
        functools.partial(factor_kernel, cells=cells),
        [(2, total, total)],
        (place, total_over_all(keep, give)),
        scratch=[pltpu.VMEM((packed, LANES), jnp.float32), pltpu.VMEM((1, total, total), jnp.float32)],
        smem=1,
        flops=2 * work,
    )
    other = route(mine, to_core)
    pieces = call(combine_kernel, [piece] * groups, (place, mine, other, w2), smem=1, flops=12 * work)
    *pieces, mine, other = lax.optimization_barrier((*pieces, mine, other))
    (rayleigh,) = call(rayleigh_kernel, [(2, nvec, total)], (place, mine, other), smem=1, flops=2 * work)
    refined = call(
        functools.partial(collect_kernel, tiles=tiles),
        (nvec * comps * tiles, LANES),
        [place] + exchange(pieces),
        smem=1,
    )
    return refined.reshape(vectors.shape), rayleigh


def solution(mesh):
    return jax.shard_map(
        local,
        mesh=mesh,
        in_specs=(P("vec", None, "space", None), P("space", None), P(), P()),
        out_specs=(P("vec", None, "space", None), P(None, "vec", None)),
        check_vma=False,
    )
```

```python
import functools

import jax
import jax.numpy as jnp
from jax import lax
from jax.experimental import pallas as pl
from jax.experimental.pallas import tpu as pltpu
from jax.sharding import PartitionSpec as P

NX = 64
LANES = 128
SUB = 8
LEVELS = 4
BLOCK = 64
STEP = 8
ORDER = (0, 7, 5, 3, 4, 1, 6, 2)
ENTRIES = ((0, 0), (0, 1), (0, 2), (1, 1), (1, 2), (2, 2))
ENTRY_OF = {pair: i for i, pair in enumerate(ENTRIES)}
VMEM_LIMIT = 48 * 1024 * 1024
SPACE = (2, 4, 2)
VEC = (4, 2)
TILE = 64
PAIRS = ((0, 0), (1, 0), (1, 1), (2, 0), (2, 1), (2, 2))


def rows_of(device):
    x, far = device // VEC[1], device % VEC[1]
    return x + far * (2 * VEC[0] - 1 - 2 * x)


DEVICE_OF = sorted(range(VEC[0] * VEC[1]), key=rows_of)


def route(array, move):
    pairs = []
    for zl in range(SPACE[0]):
        for y in range(SPACE[1]):
            for core in range(SPACE[2]):
                for x in range(VEC[0]):
                    for zh in range(VEC[1]):
                        a, b, c, d, e = move(zl, y, core, x, zh)
                        here = (((zl * SPACE[1] + y) * SPACE[2] + core) * VEC[0] + x) * VEC[1] + zh
                        there = (((a * SPACE[1] + b) * SPACE[2] + c) * VEC[0] + d) * VEC[1] + e
                        pairs.append((here, there))
    return lax.ppermute(array, ("space", "vec"), pairs)


def step_along(array, axis, by):
    order = DEVICE_OF if axis == "vec" else range(lax.axis_size(axis))
    pairs = [(order[i], order[i + by]) for i in range(len(order)) if 0 <= i + by < len(order)]
    return lax.ppermute(array, axis, pairs)


def partner(place_ref, k):
    return jnp.bitwise_xor(place_ref[0], k)


def spread_kernel(place_ref, x_ref, *o_refs, tiles):
    per, comps, nvec = o_refs[0].shape[:3]
    stride = comps * tiles
    for k, o_ref in zip(ORDER, o_refs):
        first = rows_of(partner(place_ref, k)) * per
        for t in range(per):
            for c in range(comps):
                for v in range(0, nvec, SUB):
                    rows = pl.ds(first + (v * stride + c * tiles + t), SUB, stride)
                    o_ref[t, c, v : v + SUB, :] = x_ref[rows, :]


def collect_kernel(place_ref, *refs, tiles):
    x_refs, (o_ref, held, sems) = refs[:-3], refs[-3:]
    per, comps, nvec = x_refs[0].shape[:3]
    stride = comps * tiles
    stores = []
    for i, v in enumerate(range(0, nvec, SUB)):
        for k, x_ref in zip(ORDER, x_refs):
            first = rows_of(partner(place_ref, k)) * per
            for t in range(per):
                for c in range(comps):
                    rows = pl.ds(first + (v * stride + c * tiles + t), SUB, stride)
                    held[rows, :] = x_ref[t, c, v : v + SUB, :]
        rows = pl.ds(v * stride, SUB * stride)
        store = pltpu.make_async_copy(held.at[rows], o_ref.at[rows], sems.at[i])
        store.start()
        stores.append(store)
    for store in stores:
        store.wait()


def turn(a):
    return pltpu.roll(a, NX, 1)


def pack_edges(low, near, far, first_ref, last_ref, at):
    first_ref[at] = jnp.where(low, near[0], turn(far[0]))
    last_ref[at] = jnp.where(low, turn(near[1]), far[1])


def gather_kernel(place_ref, *refs):
    pieces, (o_ref, first_ref, last_ref) = refs[:-3], refs[-3:]
    groups, per, comps, nvec = o_ref.shape[:4]
    for k, x_ref in zip(ORDER, pieces):
        o_ref[partner(place_ref, k)] = x_ref[...]
    low = lax.broadcasted_iota(jnp.int32, (SUB, LANES), 1) < NX
    for q in range(groups // 2):
        for c in range(comps):
            for v in range(0, nvec, SUB):
                rows = slice(v, v + SUB)
                near, far = [[o_ref[g, t, c, rows, :] for t in (0, per - 1)] for g in (q, q + groups // 2)]
                pack_edges(low, near, far, first_ref, last_ref, (q, c, rows, slice(None)))


def stencil_kernel(stiff_ref, mass_ref, cls_ref, u_ref, yd_ref, yu_ref, za_ref, zb_ref, w_ref, *rest):
    edges, coef_ref = rest[:-1], rest[-1]
    groups, per, comps, nvec = u_ref.shape[:4]
    lane = lax.broadcasted_iota(jnp.int32, (SUB, LANES), 1)
    low = lane < NX

    def pick(cls, values):
        out = jnp.zeros((SUB, LANES), jnp.float32)
        for level in range(LEVELS):
            out = jnp.where(cls == level, values[level], out)
        return out

    for t in range(per):
        for face, direction in enumerate((0, 1, 1, 2, 2)):
            cls = jnp.broadcast_to(cls_ref[face, t : t + 1, :], (SUB, LANES))
            for i, (a, b) in enumerate(ENTRIES):
                spots = [((level * 3 + direction) * 3 + a) * 3 + b for level in range(LEVELS)]
                coef_ref[t, face * 6 + i] = pick(cls, [stiff_ref[s] for s in spots])
        cls = jnp.broadcast_to(cls_ref[5, t : t + 1, :], (SUB, LANES))
        coef_ref[t, 30] = pick(cls, [mass_ref[level] for level in range(LEVELS)])

    def mix(t, face, d):
        s = [coef_ref[t, face * 6 + i] for i in range(6)]
        return [
            s[ENTRY_OF[min(a, 0), max(a, 0)]] * d[0]
            + s[ENTRY_OF[min(a, 1), max(a, 1)]] * d[1]
            + s[ENTRY_OF[min(a, 2), max(a, 2)]] * d[2]
            for a in range(3)
        ]

    steps = nvec // SUB
    half = groups // 2

    def body(i, carry):
        q = i // steps
        rows = pl.ds(pl.multiple_of((i % steps) * SUB, SUB), SUB)
        ends = []
        for part in range(2):
            g = q + part * half
            tiles = [[u_ref[g, t, c, rows, :] for c in range(3)] for t in range(per)]
            below = [yd_ref[q, c, rows, :] for c in range(3)]
            above = [yu_ref[q, c, rows, :] for c in range(3)]
            if part == 0:
                above = [turn(a) for a in above]
            else:
                below = [turn(a) for a in below]
            swaps = [below] + [[turn(a) for a in line] for line in tiles] + [above]
            done = []
            for t in range(per):
                u = tiles[t]
                f = mix(t, 0, [pltpu.roll(u[c], LANES - 1, 1) - u[c] for c in range(3)])
                acc = [coef_ref[t, 30] * u[c] + (pltpu.roll(f[c], 1, 1) - f[c]) for c in range(3)]
                f = mix(t, 1, [jnp.where(low, swaps[t + 1][c], swaps[t + 2][c]) - u[c] for c in range(3)])
                acc = [acc[c] - f[c] for c in range(3)]
                f = mix(t, 2, [u[c] - jnp.where(low, swaps[t][c], swaps[t + 1][c]) for c in range(3)])
                acc = [acc[c] + f[c] for c in range(3)]
                f = mix(t, 3, [za_ref[g, t, c, rows, :] - u[c] for c in range(3)])
                acc = [acc[c] - f[c] for c in range(3)]
                f = mix(t, 4, [zb_ref[g, t, c, rows, :] - u[c] for c in range(3)])
                done.append([acc[c] - f[c] for c in range(3)])
                for c in range(3):
                    w_ref[g, t, c, rows, :] = done[t][c]
            ends.append((done[0], done[-1]))
        if edges:
            for c in range(3):
                near, far = [[end[c] for end in pair] for pair in ends]
                pack_edges(low, near, far, *edges, (q, c, rows, slice(None)))
        return carry

    lax.fori_loop(0, half * steps, body, 0)


def stacked(ref, t, c):
    groups = ref.shape[0]
    return jnp.concatenate([ref[g, t, c] for g in range(groups)], 0)


def wide(ref, k):
    comps = ref.shape[2]
    return jnp.concatenate([stacked(ref, (2 * k + j) // comps, (2 * k + j) % comps) for j in range(2)], 1)


def packed_products(b_ref, a_ref):
    chunks = a_ref.shape[1] * a_ref.shape[2] // 2
    total = None
    for k in range(chunks):
        a, b = wide(a_ref, k), wide(b_ref, k)
        both = [side[i : i + TILE] for i in range(0, a.shape[0], TILE) for side in (b, a)]
        part = dot(a, jnp.concatenate(both, 0), (1, 1))
        total = part if total is None else total + part
    return [total[i * TILE : (i + 1) * TILE, j * LANES : (j + 1) * LANES] for i, j in PAIRS]


def early_kernel(b_ref, a_ref, o_ref):
    for i, block in enumerate(packed_products(b_ref, a_ref)):
        o_ref[i * TILE : (i + 1) * TILE, :] = block


def late_kernel(place_ref, *refs):
    early_ref, w_ref, keep_ref, give_ref, coef_ref = refs[-5:]
    u_ref = refs[3]
    stencil_kernel(*refs[:-5], w_ref, coef_ref)
    even = place_ref[2] == 0
    for i, block in enumerate(packed_products(u_ref, w_ref)):
        rows = slice(i * TILE, (i + 1) * TILE)
        early = early_ref[rows, :]
        keep_ref[rows, :] = jnp.where(even, block, early)
        give_ref[rows, :] = jnp.where(even, early, block)


def eliminate(panels, cols):
    first, width = cols
    tile, lane0 = first // LANES, first % LANES
    lane = lax.broadcasted_iota(jnp.int32, (SUB, LANES), 1)
    sub = lax.broadcasted_iota(jnp.int32, (SUB, LANES), 0)
    strips = width // SUB
    states = []
    for panel in panels:
        state = [[panel[i * SUB : (i + 1) * SUB, a : a + LANES] for a in range(0, panel.shape[1], LANES)] for i in range(strips)]
        unit = [jnp.where(lane == lane0 + i * SUB + sub, 1.0, 0.0) for i in range(strips)]
        states.append([line + [u] for line, u in zip(state, unit)])
    scales = [[jnp.ones((SUB, LANES), jnp.float32) for _ in range(strips)] for _ in panels]

    def spread(row, like):
        return jnp.broadcast_to(row, (SUB, like.shape[1]))

    for j in range(0, width, STEP):
        strip, off = j // SUB, j % SUB
        for m, state in enumerate(states):
            columns = [
                [jnp.broadcast_to(state[i][tile][:, lane0 + j + s : lane0 + j + s + 1], (SUB, LANES)) for i in range(strip, strips)]
                for s in range(STEP)
            ]
            rows = [[spread(part[off + r : off + r + 1, :], part) for part in state[strip]] for r in range(STEP)]
            small = [[spread(columns[s][0][off + r : off + r + 1, :], columns[s][0]) for s in range(STEP)] for r in range(STEP)]
            inverse = []
            pivots = []
            for r in range(STEP):
                pivots.append(small[r][r])
                inverse.append(1.0 / small[r][r])
                for q in range(r + 1, STEP):
                    ratio = small[q][r] * inverse[r]
                    rows[q] = [a - ratio[:, : a.shape[1]] * b for a, b in zip(rows[q], rows[r])]
                    columns[q] = [a - ratio * b for a, b in zip(columns[q], columns[r])]
                    for p in range(q, STEP):
                        small[p][q] = small[p][q] - ratio * small[p][r]
            weights = [[a * inverse[s] for a in columns[s]] for s in range(STEP)]
            for i in range(strip, strips):
                line = []
                for n, part in enumerate(state[i]):
                    value = part
                    for s in range(STEP):
                        value = value - weights[s][i - strip][:, : part.shape[1]] * rows[s][n]
                    if i == strip:
                        at = sub[:, : part.shape[1]]
                        if off:
                            value = jnp.where(at < off, part, value)
                        for r in range(STEP):
                            value = jnp.where(at == off + r, rows[r][n], value)
                    line.append(value)
                state[i] = line
            for r in range(STEP):
                scales[m][strip] = jnp.where(sub == off + r, pivots[r], scales[m][strip])
    results = []
    for state, scale in zip(states, scales):
        inverse, reduced = [], []
        for line, pivot in zip(state, scale):
            root = lax.rsqrt(pivot)
            root = root * (1.5 - 0.5 * pivot * root * root)
            inverse.append(line[-1] * root)
            reduced.append(jnp.concatenate([part * root[:, : part.shape[1]] for part in line[:-1]], 1))
        results.append((jnp.concatenate(inverse, 0), jnp.concatenate(reduced, 0)))
    return results


def dot(a, b, dims):
    return lax.dot_general(
        a, b, ((dims[:1], dims[1:]), ((), ())), precision=lax.Precision.HIGHEST, preferred_element_type=jnp.float32
    )


def factor(scratch, total):
    count = scratch.shape[0]
    lane = lax.broadcasted_iota(jnp.int32, (1, total), 1)
    for first in range(0, total, BLOCK):
        last = first + BLOCK
        here = (lane >= first) & (lane < last)
        results = eliminate([scratch[m, first:last, :] for m in range(count)], (first, BLOCK))
        for m, (inverse, reduced) in enumerate(results):
            tile = first // LANES * LANES
            side = min(LANES, total - tile)
            parts = []
            if tile:
                parts.append(jnp.zeros((BLOCK, tile), jnp.float32))
            parts.append(inverse[:, :side])
            if tile + side < total:
                parts.append(jnp.zeros((BLOCK, total - tile - side), jnp.float32))
            inverse = jnp.concatenate(parts, 1)
            row = jnp.where(here, inverse, reduced)
            scratch[m, first:last, :] = jnp.where(lane < last, row, 0.0)
            if last < total:
                rest = scratch[m, last:, :]
                lower = dot(rest, inverse, (1, 1))
                scratch[m, last:, :] = jnp.where(here, 0.0, rest) - dot(lower, row, (1, 0))


def factor_kernel(place_ref, own_ref, o_ref, packed, scratch, *, cells):
    pieces, quarter = own_ref.shape[:2]
    total = o_ref.shape[1]
    for k in range(pieces):
        at = ((place_ref[1] + pieces - k) % pieces) * quarter
        packed[pl.ds(pl.multiple_of(at, SUB), quarter), :] = own_ref[k] * (1.0 / cells)
    for m, target in enumerate((o_ref.at[1], scratch.at[0])):
        for q, (i, j) in enumerate(PAIRS):
            block = packed[q * TILE : (q + 1) * TILE, m * TILE : (m + 1) * TILE]
            target[i * TILE : (i + 1) * TILE, j * TILE : (j + 1) * TILE] = block
            if i != j:
                target[j * TILE : (j + 1) * TILE, i * TILE : (i + 1) * TILE] = block.T
    factor(scratch, total)
    o_ref[0] = scratch[0]


def combine_kernel(place_ref, mine_ref, other_ref, w_ref, *o_refs):
    per, comps, nvec = w_ref.shape[1:4]
    groups = w_ref.shape[0]
    even = place_ref[2] == 0
    order = [pl.ds(pl.multiple_of(partner(place_ref, k) * nvec, SUB), nvec) for k in ORDER]
    inv = jnp.concatenate([jnp.where(even, mine_ref[0, rows, :], other_ref[0, rows, :]) for rows in order], 0)
    for n in range(per * comps // 2):
        out = dot(inv, wide(w_ref, n), (1, 0))
        for j in range(2):
            t, c = (2 * n + j) // comps, (2 * n + j) % comps
            for k in range(groups):
                o_refs[k][t, c] = out[k * nvec : (k + 1) * nvec, j * LANES : (j + 1) * LANES]


def rayleigh_kernel(place_ref, mine_ref, other_ref, ray_ref):
    nvec = ray_ref.shape[1]
    even = place_ref[2] == 0
    own = pl.ds(pl.multiple_of(place_ref[0] * nvec, SUB), nvec)
    ray_ref[0] = jnp.where(even, other_ref[1, own, :], mine_ref[1, own, :])
    rows = jnp.where(even, other_ref[0, own, :], mine_ref[0, own, :])
    rows = dot(rows, jnp.where(even, mine_ref[1], other_ref[1]), (1, 0))
    ray_ref[1] = dot(rows, jnp.where(even, other_ref[0], mine_ref[0]), (1, 1))


def call(kernel, outs, operands, scratch=(), smem=0, flops=0, far_out=False):
    inside, outside = pl.BlockSpec(memory_space=pltpu.VMEM), pl.BlockSpec(memory_space=pl.ANY)
    specs = [pl.BlockSpec(memory_space=pltpu.SMEM)] * smem
    specs += [inside] * (len(operands) - smem)
    size = sum(a.size * 4 for a in operands) + 4
    return pl.pallas_call(
        kernel,
        out_shape=[jax.ShapeDtypeStruct(dims, jnp.float32) for dims in outs],
        in_specs=specs,
        out_specs=[outside if far_out else inside] * len(outs),
        scratch_shapes=list(scratch),
        compiler_params=pltpu.CompilerParams(vmem_limit_bytes=VMEM_LIMIT),
        cost_estimate=pl.CostEstimate(flops=flops, bytes_accessed=size, transcendentals=0),
    )(*operands)


def to_core(zl, y, core, x, zh):
    return (zl, y, 1 - core, x, zh)


def total_over_all(keep, give):
    y = (lax.axis_index("space") // 2) % 4
    quarter = keep.shape[0] // 4
    mine = keep + route(give, to_core)

    def chunk(k):
        return lax.dynamic_slice_in_dim(mine, ((y + k) % 4) * quarter, quarter, 0)

    def along_y(k):
        return lambda zl, y, c, x, zh: (zl, (y + k) % 4, c, x, zh)

    def along_x(k):
        return lambda zl, y, c, x, zh: (zl, y, c, (x + k) % 4, zh)

    def along_z(k):
        def move(zl, y, c, x, zh):
            z = (zh * 2 + zl + k) % 4
            return (z % 2, y, c, x, z // 2)

        return move

    got = [route(chunk(k), along_y(k)) for k in (1, 2, 3)]
    mine = (chunk(0) + got[1]) + (got[0] + got[2])
    for along in (along_x, along_z):
        got = [route(mine, along(k)) for k in (1, 2, 3)]
        mine = (mine + got[1]) + (got[0] + got[2])
    return jnp.stack([mine] + [route(mine, along_y(k)) for k in (1, 2, 3)])


def local(vectors, labels, stiffness, mass):
    nvec, comps, _, plane = vectors.shape
    groups = lax.axis_size("vec")
    total = nvec * groups
    nz = lax.axis_size("space")
    cells = 3.0 * nz * plane
    tiles = plane // LANES
    per = tiles // groups
    z = lax.axis_index("space")
    h = lax.axis_index("vec")

    below = step_along(labels, "space", 1)
    lab = labels.reshape(plane // NX, NX)
    row = lax.broadcasted_iota(jnp.int32, lab.shape, 0)
    col = lax.broadcasted_iota(jnp.int32, lab.shape, 1)
    none = LEVELS
    upper = jnp.concatenate([jnp.full((1, NX), none, jnp.int32), lab[:-1]], 0)
    over = jnp.where(z == nz - 1, none, lab)
    under = jnp.where(z == 0, none, below.reshape(lab.shape))
    core = z % 2
    faces = jnp.stack(
        [
            jnp.where(col == NX - 1, none, lab),
            jnp.where(row == lab.shape[0] - 1, none, lab),
            upper,
            jnp.where(core == 0, under, over),
            jnp.where(core == 0, over, under),
            lab,
        ]
    )
    faces = faces.reshape(6, tiles, LANES)
    faces = lax.dynamic_slice_in_dim(faces, rows_of(h) * per, per, 1)
    stiff = stiffness.reshape(-1)

    piece = (per, comps, nvec, LANES)
    shape = (groups,) + piece
    edge = (groups // 2, comps, nvec, LANES)

    def exchange(pieces):
        got = [lax.ppermute(a, "vec", [(i, i ^ k) for i in range(groups)]) for k, a in zip(ORDER[1:], pieces[1:])]
        return [pieces[0]] + got

    def halo(u, first, last):
        yd = step_along(last, "vec", 1)
        yu = step_along(first, "vec", -1)
        za = lax.ppermute(u, "space", [(i, i + (1 if i % 2 else -1)) for i in range(1, nz - 1)])
        zb = lax.ppermute(u, "space", [(i, i ^ 1) for i in range(nz)])
        return u, yd, yu, za, zb

    coefs = [pltpu.VMEM((per, 31, SUB, LANES), jnp.float32)]
    moving = [pltpu.VMEM((nvec * comps * tiles, LANES), jnp.float32), pltpu.SemaphoreType.DMA((nvec // SUB,))]
    place = jnp.stack([h, (z // 2) % 4, core]).astype(jnp.int32)
    work = total * total * per * comps * LANES
    packed = len(PAIRS) * TILE
    pieces = call(
        functools.partial(spread_kernel, tiles=tiles),
        [piece] * groups,
        (place, vectors.reshape(nvec * comps * tiles, LANES)),
        smem=1,
    )
    v, first, last = call(gather_kernel, [shape, edge, edge], [place] + exchange(pieces), smem=1)
    w1, first, last = call(
        stencil_kernel,
        [shape, edge, edge],
        (stiff, mass, faces, *halo(v, first, last)),
        scratch=coefs,
        smem=2,
        flops=20_000_000,
    )
    (early,) = call(early_kernel, [(packed, LANES)], (v, w1), flops=24 * work)
    w2, keep, give = call(
        late_kernel,
        [shape, (packed, LANES), (packed, LANES)],
        (place, stiff, mass, faces, *halo(w1, first, last), early),
        scratch=coefs,
        smem=3,
        flops=24 * work,
    )
    (mine,) = call(
        functools.partial(factor_kernel, cells=cells),
        [(2, total, total)],
        (place, total_over_all(keep, give)),
        scratch=[pltpu.VMEM((packed, LANES), jnp.float32), pltpu.VMEM((1, total, total), jnp.float32)],
        smem=1,
        flops=2 * work,
    )
    other = route(mine, to_core)
    pieces = call(combine_kernel, [piece] * groups, (place, mine, other, w2), smem=1, flops=12 * work)
    *pieces, mine, other = lax.optimization_barrier((*pieces, mine, other))
    (rayleigh,) = call(rayleigh_kernel, [(2, nvec, total)], (place, mine, other), smem=1, flops=2 * work)
    (refined,) = call(
        functools.partial(collect_kernel, tiles=tiles),
        [(nvec * comps * tiles, LANES)],
        [place] + exchange(pieces),
        scratch=moving,
        smem=1,
        far_out=True,
    )
    return refined.reshape(vectors.shape), rayleigh


def solution(mesh):
    return jax.shard_map(
        local,
        mesh=mesh,
        in_specs=(P("vec", None, "space", None), P("space", None), P(), P()),
        out_specs=(P("vec", None, "space", None), P(None, "vec", None)),
        check_vma=False,
    )
```

```python
import functools

import jax
import jax.numpy as jnp
from jax import lax
from jax.experimental import pallas as pl
from jax.experimental.pallas import tpu as pltpu
from jax.sharding import PartitionSpec as P

NX = 64
LANES = 128
SUB = 8
LEVELS = 4
BLOCK = 64
STEP = 8
ORDER = (0, 7, 5, 3, 4, 1, 6, 2)
ENTRIES = ((0, 0), (0, 1), (0, 2), (1, 1), (1, 2), (2, 2))
ENTRY_OF = {pair: i for i, pair in enumerate(ENTRIES)}
VMEM_LIMIT = 48 * 1024 * 1024
SPACE = (2, 4, 2)
VEC = (4, 2)
TILE = 64
PAIRS = ((0, 0), (1, 0), (1, 1), (2, 0), (2, 1), (2, 2))


def rows_of(device):
    x, far = device // VEC[1], device % VEC[1]
    return x + far * (2 * VEC[0] - 1 - 2 * x)


DEVICE_OF = sorted(range(VEC[0] * VEC[1]), key=rows_of)


def route(array, move):
    pairs = []
    for zl in range(SPACE[0]):
        for y in range(SPACE[1]):
            for core in range(SPACE[2]):
                for x in range(VEC[0]):
                    for zh in range(VEC[1]):
                        a, b, c, d, e = move(zl, y, core, x, zh)
                        here = (((zl * SPACE[1] + y) * SPACE[2] + core) * VEC[0] + x) * VEC[1] + zh
                        there = (((a * SPACE[1] + b) * SPACE[2] + c) * VEC[0] + d) * VEC[1] + e
                        pairs.append((here, there))
    return lax.ppermute(array, ("space", "vec"), pairs)


def step_along(array, axis, by):
    order = DEVICE_OF if axis == "vec" else range(lax.axis_size(axis))
    pairs = [(order[i], order[i + by]) for i in range(len(order)) if 0 <= i + by < len(order)]
    return lax.ppermute(array, axis, pairs)


def partner(place_ref, k):
    return jnp.bitwise_xor(place_ref[0], k)


def spread_kernel(place_ref, x_ref, *o_refs, tiles):
    per, comps, nvec = o_refs[0].shape[:3]
    stride = comps * tiles
    for k, o_ref in zip(ORDER, o_refs):
        first = rows_of(partner(place_ref, k)) * per
        for t in range(per):
            for c in range(comps):
                for v in range(0, nvec, SUB):
                    rows = pl.ds(first + (v * stride + c * tiles + t), SUB, stride)
                    o_ref[t, c, v : v + SUB, :] = x_ref[rows, :]


def collect_kernel(place_ref, *refs, tiles):
    x_refs, (o_ref, held, sems) = refs[:-3], refs[-3:]
    per, comps, nvec = x_refs[0].shape[:3]
    stride = comps * tiles
    stores = []
    for i, v in enumerate(range(0, nvec, SUB)):
        for k, x_ref in zip(ORDER, x_refs):
            first = rows_of(partner(place_ref, k)) * per
            for t in range(per):
                for c in range(comps):
                    rows = pl.ds(first + (v * stride + c * tiles + t), SUB, stride)
                    held[rows, :] = x_ref[t, c, v : v + SUB, :]
        rows = pl.ds(v * stride, SUB * stride)
        store = pltpu.make_async_copy(held.at[rows], o_ref.at[rows], sems.at[i])
        store.start()
        stores.append(store)
    for store in stores:
        store.wait()


def turn(a):
    return pltpu.roll(a, NX, 1)


def pack_edges(low, near, far, first_ref, last_ref, at):
    first_ref[at] = jnp.where(low, near[0], turn(far[0]))
    last_ref[at] = jnp.where(low, turn(near[1]), far[1])


def gather_kernel(place_ref, *refs):
    pieces, (o_ref, first_ref, last_ref) = refs[:-3], refs[-3:]
    groups, per, comps, nvec = o_ref.shape[:4]
    for k, x_ref in zip(ORDER, pieces):
        o_ref[partner(place_ref, k)] = x_ref[...]
    low = lax.broadcasted_iota(jnp.int32, (SUB, LANES), 1) < NX
    for q in range(groups // 2):
        for c in range(comps):
            for v in range(0, nvec, SUB):
                rows = slice(v, v + SUB)
                near, far = [[o_ref[g, t, c, rows, :] for t in (0, per - 1)] for g in (q, q + groups // 2)]
                pack_edges(low, near, far, first_ref, last_ref, (q, c, rows, slice(None)))


def stencil_kernel(stiff_ref, mass_ref, cls_ref, u_ref, yd_ref, yu_ref, za_ref, zb_ref, w_ref, *rest):
    edges, coef_ref = rest[:-1], rest[-1]
    groups, per, comps, nvec = u_ref.shape[:4]
    lane = lax.broadcasted_iota(jnp.int32, (SUB, LANES), 1)
    low = lane < NX

    def pick(cls, values):
        out = jnp.zeros((SUB, LANES), jnp.float32)
        for level in range(LEVELS):
            out = jnp.where(cls == level, values[level], out)
        return out

    for t in range(per):
        for face, direction in enumerate((0, 1, 1, 2, 2)):
            cls = jnp.broadcast_to(cls_ref[face, t : t + 1, :], (SUB, LANES))
            for i, (a, b) in enumerate(ENTRIES):
                spots = [((level * 3 + direction) * 3 + a) * 3 + b for level in range(LEVELS)]
                coef_ref[t, face * 6 + i] = pick(cls, [stiff_ref[s] for s in spots])
        cls = jnp.broadcast_to(cls_ref[5, t : t + 1, :], (SUB, LANES))
        coef_ref[t, 30] = pick(cls, [mass_ref[level] for level in range(LEVELS)])

    def mix(t, face, d):
        s = [coef_ref[t, face * 6 + i] for i in range(6)]
        return [
            s[ENTRY_OF[min(a, 0), max(a, 0)]] * d[0]
            + s[ENTRY_OF[min(a, 1), max(a, 1)]] * d[1]
            + s[ENTRY_OF[min(a, 2), max(a, 2)]] * d[2]
            for a in range(3)
        ]

    steps = nvec // SUB
    half = groups // 2

    def body(i, carry):
        q = i // steps
        rows = pl.ds(pl.multiple_of((i % steps) * SUB, SUB), SUB)
        ends = []
        for part in range(2):
            g = q + part * half
            tiles = [[u_ref[g, t, c, rows, :] for c in range(3)] for t in range(per)]
            below = [yd_ref[q, c, rows, :] for c in range(3)]
            above = [yu_ref[q, c, rows, :] for c in range(3)]
            if part == 0:
                above = [turn(a) for a in above]
            else:
                below = [turn(a) for a in below]
            swaps = [below] + [[turn(a) for a in line] for line in tiles] + [above]
            done = []
            for t in range(per):
                u = tiles[t]
                f = mix(t, 0, [pltpu.roll(u[c], LANES - 1, 1) - u[c] for c in range(3)])
                acc = [coef_ref[t, 30] * u[c] + (pltpu.roll(f[c], 1, 1) - f[c]) for c in range(3)]
                f = mix(t, 1, [jnp.where(low, swaps[t + 1][c], swaps[t + 2][c]) - u[c] for c in range(3)])
                acc = [acc[c] - f[c] for c in range(3)]
                f = mix(t, 2, [u[c] - jnp.where(low, swaps[t][c], swaps[t + 1][c]) for c in range(3)])
                acc = [acc[c] + f[c] for c in range(3)]
                f = mix(t, 3, [za_ref[g, t, c, rows, :] - u[c] for c in range(3)])
                acc = [acc[c] - f[c] for c in range(3)]
                f = mix(t, 4, [zb_ref[g, t, c, rows, :] - u[c] for c in range(3)])
                done.append([acc[c] - f[c] for c in range(3)])
                for c in range(3):
                    w_ref[g, t, c, rows, :] = done[t][c]
            ends.append((done[0], done[-1]))
        if edges:
            for c in range(3):
                near, far = [[end[c] for end in pair] for pair in ends]
                pack_edges(low, near, far, *edges, (q, c, rows, slice(None)))
        return carry

    lax.fori_loop(0, half * steps, body, 0)


def stacked(ref, t, c):
    groups = ref.shape[0]
    return jnp.concatenate([ref[g, t, c] for g in range(groups)], 0)


def wide(ref, k):
    comps = ref.shape[2]
    return jnp.concatenate([stacked(ref, (2 * k + j) // comps, (2 * k + j) % comps) for j in range(2)], 1)


def packed_products(b_ref, a_ref):
    chunks = a_ref.shape[1] * a_ref.shape[2] // 2
    total = None
    for k in range(chunks):
        a, b = wide(a_ref, k), wide(b_ref, k)
        both = [side[i : i + TILE] for i in range(0, a.shape[0], TILE) for side in (b, a)]
        part = dot(a, jnp.concatenate(both, 0), (1, 1))
        total = part if total is None else total + part
    return [total[i * TILE : (i + 1) * TILE, j * LANES : (j + 1) * LANES] for i, j in PAIRS]


def early_kernel(b_ref, a_ref, o_ref):
    for i, block in enumerate(packed_products(b_ref, a_ref)):
        o_ref[i * TILE : (i + 1) * TILE, :] = block


def late_kernel(place_ref, *refs):
    early_ref, w_ref, keep_ref, give_ref, coef_ref = refs[-5:]
    u_ref = refs[3]
    stencil_kernel(*refs[:-5], w_ref, coef_ref)
    even = place_ref[2] == 0
    for i, block in enumerate(packed_products(u_ref, w_ref)):
        rows = slice(i * TILE, (i + 1) * TILE)
        early = early_ref[rows, :]
        keep_ref[rows, :] = jnp.where(even, block, early)
        give_ref[rows, :] = jnp.where(even, early, block)


def eliminate(panels, cols):
    first, width = cols
    tile, lane0 = first // LANES, first % LANES
    lane = lax.broadcasted_iota(jnp.int32, (SUB, LANES), 1)
    sub = lax.broadcasted_iota(jnp.int32, (SUB, LANES), 0)
    strips = width // SUB
    states = []
    for panel in panels:
        state = [[panel[i * SUB : (i + 1) * SUB, a : a + LANES] for a in range(0, panel.shape[1], LANES)] for i in range(strips)]
        unit = [jnp.where(lane == lane0 + i * SUB + sub, 1.0, 0.0) for i in range(strips)]
        states.append([line + [u] for line, u in zip(state, unit)])
    scales = [[jnp.ones((SUB, LANES), jnp.float32) for _ in range(strips)] for _ in panels]

    def spread(row, like):
        return jnp.broadcast_to(row, (SUB, like.shape[1]))

    for j in range(0, width, STEP):
        strip, off = j // SUB, j % SUB
        for m, state in enumerate(states):
            columns = [
                [jnp.broadcast_to(state[i][tile][:, lane0 + j + s : lane0 + j + s + 1], (SUB, LANES)) for i in range(strip, strips)]
                for s in range(STEP)
            ]
            rows = [[spread(part[off + r : off + r + 1, :], part) for part in state[strip]] for r in range(STEP)]
            small = [[spread(columns[s][0][off + r : off + r + 1, :], columns[s][0]) for s in range(STEP)] for r in range(STEP)]
            inverse = []
            pivots = []
            for r in range(STEP):
                pivots.append(small[r][r])
                inverse.append(1.0 / small[r][r])
                for q in range(r + 1, STEP):
                    ratio = small[q][r] * inverse[r]
                    rows[q] = [a - ratio[:, : a.shape[1]] * b for a, b in zip(rows[q], rows[r])]
                    columns[q] = [a - ratio * b for a, b in zip(columns[q], columns[r])]
                    for p in range(q, STEP):
                        small[p][q] = small[p][q] - ratio * small[p][r]
            weights = [[a * inverse[s] for a in columns[s]] for s in range(STEP)]
            for i in range(strip, strips):
                line = []
                for n, part in enumerate(state[i]):
                    value = part
                    for s in range(STEP):
                        value = value - weights[s][i - strip][:, : part.shape[1]] * rows[s][n]
                    if i == strip:
                        at = sub[:, : part.shape[1]]
                        if off:
                            value = jnp.where(at < off, part, value)
                        for r in range(STEP):
                            value = jnp.where(at == off + r, rows[r][n], value)
                    line.append(value)
                state[i] = line
            for r in range(STEP):
                scales[m][strip] = jnp.where(sub == off + r, pivots[r], scales[m][strip])
    results = []
    for state, scale in zip(states, scales):
        inverse, reduced = [], []
        for line, pivot in zip(state, scale):
            root = lax.rsqrt(pivot)
            root = root * (1.5 - 0.5 * pivot * root * root)
            inverse.append(line[-1] * root)
            reduced.append(jnp.concatenate([part * root[:, : part.shape[1]] for part in line[:-1]], 1))
        results.append((jnp.concatenate(inverse, 0), jnp.concatenate(reduced, 0)))
    return results


def dot(a, b, dims):
    return lax.dot_general(
        a, b, ((dims[:1], dims[1:]), ((), ())), precision=lax.Precision.HIGHEST, preferred_element_type=jnp.float32
    )


def factor(scratch, total):
    count = scratch.shape[0]
    lane = lax.broadcasted_iota(jnp.int32, (1, total), 1)
    for first in range(0, total, BLOCK):
        last = first + BLOCK
        here = (lane >= first) & (lane < last)
        results = eliminate([scratch[m, first:last, :] for m in range(count)], (first, BLOCK))
        for m, (inverse, reduced) in enumerate(results):
            tile = first // LANES * LANES
            side = min(LANES, total - tile)
            parts = []
            if tile:
                parts.append(jnp.zeros((BLOCK, tile), jnp.float32))
            parts.append(inverse[:, :side])
            if tile + side < total:
                parts.append(jnp.zeros((BLOCK, total - tile - side), jnp.float32))
            inverse = jnp.concatenate(parts, 1)
            row = jnp.where(here, inverse, reduced)
            scratch[m, first:last, :] = jnp.where(lane < last, row, 0.0)
            if last < total:
                rest = scratch[m, last:, :]
                lower = dot(rest, inverse, (1, 1))
                scratch[m, last:, :] = jnp.where(here, 0.0, rest) - dot(lower, row, (1, 0))


def factor_kernel(place_ref, own_ref, o_ref, packed, scratch, *, cells):
    pieces, quarter = own_ref.shape[:2]
    total = o_ref.shape[1]
    for k in range(pieces):
        at = ((place_ref[1] + pieces - k) % pieces) * quarter
        packed[pl.ds(pl.multiple_of(at, SUB), quarter), :] = own_ref[k] * (1.0 / cells)
    for m, target in enumerate((o_ref.at[1], scratch.at[0])):
        for q, (i, j) in enumerate(PAIRS):
            block = packed[q * TILE : (q + 1) * TILE, m * TILE : (m + 1) * TILE]
            target[i * TILE : (i + 1) * TILE, j * TILE : (j + 1) * TILE] = block
            if i != j:
                target[j * TILE : (j + 1) * TILE, i * TILE : (i + 1) * TILE] = block.T
    factor(scratch, total)
    o_ref[0] = scratch[0]


def combine_kernel(place_ref, mine_ref, other_ref, w_ref, *o_refs):
    per, comps, nvec = w_ref.shape[1:4]
    groups = w_ref.shape[0]
    even = place_ref[2] == 0
    order = [pl.ds(pl.multiple_of(partner(place_ref, k) * nvec, SUB), nvec) for k in ORDER]
    inv = jnp.concatenate([jnp.where(even, mine_ref[0, rows, :], other_ref[0, rows, :]) for rows in order], 0)
    for n in range(per * comps // 2):
        out = dot(inv, wide(w_ref, n), (1, 0))
        for j in range(2):
            t, c = (2 * n + j) // comps, (2 * n + j) % comps
            for k in range(groups):
                o_refs[k][t, c] = out[k * nvec : (k + 1) * nvec, j * LANES : (j + 1) * LANES]


def rayleigh_kernel(place_ref, mine_ref, other_ref, ray_ref):
    nvec = ray_ref.shape[1]
    even = place_ref[2] == 0
    own = pl.ds(pl.multiple_of(place_ref[0] * nvec, SUB), nvec)
    ray_ref[0] = jnp.where(even, other_ref[1, own, :], mine_ref[1, own, :])
    rows = jnp.where(even, other_ref[0, own, :], mine_ref[0, own, :])
    rows = dot(rows, jnp.where(even, mine_ref[1], other_ref[1]), (1, 0))
    ray_ref[1] = dot(rows, jnp.where(even, other_ref[0], mine_ref[0]), (1, 1))


def call(kernel, outs, operands, scratch=(), smem=0, flops=0, far_out=False):
    inside, outside = pl.BlockSpec(memory_space=pltpu.VMEM), pl.BlockSpec(memory_space=pl.ANY)
    specs = [pl.BlockSpec(memory_space=pltpu.SMEM)] * smem
    specs += [inside] * (len(operands) - smem)
    size = sum(a.size * 4 for a in operands) + 4
    return pl.pallas_call(
        kernel,
        out_shape=[jax.ShapeDtypeStruct(dims, jnp.float32) for dims in outs],
        in_specs=specs,
        out_specs=[outside if far_out else inside] * len(outs),
        scratch_shapes=list(scratch),
        compiler_params=pltpu.CompilerParams(vmem_limit_bytes=VMEM_LIMIT),
        cost_estimate=pl.CostEstimate(flops=flops, bytes_accessed=size, transcendentals=0),
    )(*operands)


def to_core(zl, y, core, x, zh):
    return (zl, y, 1 - core, x, zh)


def total_over_all(keep, give):
    x = lax.axis_index("vec") // 2
    quarter = keep.shape[0] // 4
    mine = keep + route(give, to_core)

    def chunk(k):
        return lax.dynamic_slice_in_dim(mine, ((x + k) % 4) * quarter, quarter, 0)

    def along_y(k):
        return lambda zl, y, c, x, zh: (zl, (y + k) % 4, c, x, zh)

    def along_x(k):
        return lambda zl, y, c, x, zh: (zl, y, c, (x + k) % 4, zh)

    def along_z(k):
        def move(zl, y, c, x, zh):
            z = (zh * 2 + zl + k) % 4
            return (z % 2, y, c, x, z // 2)

        return move

    got = [route(chunk(k), along_x(k)) for k in (1, 2, 3)]
    mine = (chunk(0) + got[1]) + (got[0] + got[2])
    for along in (along_y, along_z):
        got = [route(mine, along(k)) for k in (1, 2, 3)]
        mine = (mine + got[1]) + (got[0] + got[2])
    return jnp.stack([mine] + [route(mine, along_x(k)) for k in (1, 2, 3)])


def local(vectors, labels, stiffness, mass):
    nvec, comps, _, plane = vectors.shape
    groups = lax.axis_size("vec")
    total = nvec * groups
    nz = lax.axis_size("space")
    cells = 3.0 * nz * plane
    tiles = plane // LANES
    per = tiles // groups
    z = lax.axis_index("space")
    h = lax.axis_index("vec")

    below = step_along(labels, "space", 1)
    lab = labels.reshape(plane // NX, NX)
    row = lax.broadcasted_iota(jnp.int32, lab.shape, 0)
    col = lax.broadcasted_iota(jnp.int32, lab.shape, 1)
    none = LEVELS
    upper = jnp.concatenate([jnp.full((1, NX), none, jnp.int32), lab[:-1]], 0)
    over = jnp.where(z == nz - 1, none, lab)
    under = jnp.where(z == 0, none, below.reshape(lab.shape))
    core = z % 2
    faces = jnp.stack(
        [
            jnp.where(col == NX - 1, none, lab),
            jnp.where(row == lab.shape[0] - 1, none, lab),
            upper,
            jnp.where(core == 0, under, over),
            jnp.where(core == 0, over, under),
            lab,
        ]
    )
    faces = faces.reshape(6, tiles, LANES)
    faces = lax.dynamic_slice_in_dim(faces, rows_of(h) * per, per, 1)
    stiff = stiffness.reshape(-1)

    piece = (per, comps, nvec, LANES)
    shape = (groups,) + piece
    edge = (groups // 2, comps, nvec, LANES)

    def exchange(pieces):
        got = [lax.ppermute(a, "vec", [(i, i ^ k) for i in range(groups)]) for k, a in zip(ORDER[1:], pieces[1:])]
        return [pieces[0]] + got

    def halo(u, first, last):
        yd = step_along(last, "vec", 1)
        yu = step_along(first, "vec", -1)
        za = lax.ppermute(u, "space", [(i, i + (1 if i % 2 else -1)) for i in range(1, nz - 1)])
        zb = lax.ppermute(u, "space", [(i, i ^ 1) for i in range(nz)])
        return u, yd, yu, za, zb

    coefs = [pltpu.VMEM((per, 31, SUB, LANES), jnp.float32)]
    moving = [pltpu.VMEM((nvec * comps * tiles, LANES), jnp.float32), pltpu.SemaphoreType.DMA((nvec // SUB,))]
    place = jnp.stack([h, h // 2, core]).astype(jnp.int32)
    work = total * total * per * comps * LANES
    packed = len(PAIRS) * TILE
    pieces = call(
        functools.partial(spread_kernel, tiles=tiles),
        [piece] * groups,
        (place, vectors.reshape(nvec * comps * tiles, LANES)),
        smem=1,
    )
    v, first, last = call(gather_kernel, [shape, edge, edge], [place] + exchange(pieces), smem=1)
    w1, first, last = call(
        stencil_kernel,
        [shape, edge, edge],
        (stiff, mass, faces, *halo(v, first, last)),
        scratch=coefs,
        smem=2,
        flops=20_000_000,
    )
    (early,) = call(early_kernel, [(packed, LANES)], (v, w1), flops=24 * work)
    w2, keep, give = call(
        late_kernel,
        [shape, (packed, LANES), (packed, LANES)],
        (place, stiff, mass, faces, *halo(w1, first, last), early),
        scratch=coefs,
        smem=3,
        flops=24 * work,
    )
    (mine,) = call(
        functools.partial(factor_kernel, cells=cells),
        [(2, total, total)],
        (place, total_over_all(keep, give)),
        scratch=[pltpu.VMEM((packed, LANES), jnp.float32), pltpu.VMEM((1, total, total), jnp.float32)],
        smem=1,
        flops=2 * work,
    )
    other = route(mine, to_core)
    pieces = call(combine_kernel, [piece] * groups, (place, mine, other, w2), smem=1, flops=12 * work)
    *pieces, mine, other = lax.optimization_barrier((*pieces, mine, other))
    (rayleigh,) = call(rayleigh_kernel, [(2, nvec, total)], (place, mine, other), smem=1, flops=2 * work)
    (refined,) = call(
        functools.partial(collect_kernel, tiles=tiles),
        [(nvec * comps * tiles, LANES)],
        [place] + exchange(pieces),
        scratch=moving,
        smem=1,
        far_out=True,
    )
    return refined.reshape(vectors.shape), rayleigh


def solution(mesh):
    return jax.shard_map(
        local,
        mesh=mesh,
        in_specs=(P("vec", None, "space", None), P("space", None), P(), P()),
        out_specs=(P("vec", None, "space", None), P(None, "vec", None)),
        check_vma=False,
    )
```

```python
import functools

import jax
import jax.numpy as jnp
from jax import lax
from jax.experimental import pallas as pl
from jax.experimental.pallas import tpu as pltpu
from jax.sharding import PartitionSpec as P

NX = 64
LANES = 128
SUB = 8
LEVELS = 4
BLOCK = 64
STEP = 8
ORDER = (0, 7, 5, 3, 4, 1, 6, 2)
ENTRIES = ((0, 0), (0, 1), (0, 2), (1, 1), (1, 2), (2, 2))
ENTRY_OF = {pair: i for i, pair in enumerate(ENTRIES)}
VMEM_LIMIT = 48 * 1024 * 1024
SPACE = (2, 4, 2)
VEC = (4, 2)
TILE = 64
PAIRS = ((0, 0), (1, 0), (1, 1), (2, 0), (2, 1), (2, 2))


def rows_of(device):
    x, far = device // VEC[1], device % VEC[1]
    return x + far * (2 * VEC[0] - 1 - 2 * x)


DEVICE_OF = sorted(range(VEC[0] * VEC[1]), key=rows_of)


def route(array, move):
    pairs = []
    for zl in range(SPACE[0]):
        for y in range(SPACE[1]):
            for core in range(SPACE[2]):
                for x in range(VEC[0]):
                    for zh in range(VEC[1]):
                        a, b, c, d, e = move(zl, y, core, x, zh)
                        here = (((zl * SPACE[1] + y) * SPACE[2] + core) * VEC[0] + x) * VEC[1] + zh
                        there = (((a * SPACE[1] + b) * SPACE[2] + c) * VEC[0] + d) * VEC[1] + e
                        pairs.append((here, there))
    return lax.ppermute(array, ("space", "vec"), pairs)


def step_along(array, axis, by):
    order = DEVICE_OF if axis == "vec" else range(lax.axis_size(axis))
    pairs = [(order[i], order[i + by]) for i in range(len(order)) if 0 <= i + by < len(order)]
    return lax.ppermute(array, axis, pairs)


def partner(place_ref, k):
    return jnp.bitwise_xor(place_ref[0], k)


def spread_kernel(place_ref, x_ref, *o_refs, tiles):
    per, comps, nvec = o_refs[0].shape[:3]
    stride = comps * tiles
    for k, o_ref in zip(ORDER, o_refs):
        first = rows_of(partner(place_ref, k)) * per
        for t in range(per):
            for c in range(comps):
                for v in range(0, nvec, SUB):
                    rows = pl.ds(first + (v * stride + c * tiles + t), SUB, stride)
                    o_ref[t, c, v : v + SUB, :] = x_ref[rows, :]


def collect_kernel(place_ref, *refs, tiles):
    x_refs, (o_ref, held, sems) = refs[:-3], refs[-3:]
    per, comps, nvec = x_refs[0].shape[:3]
    stride = comps * tiles
    stores = []
    for i, v in enumerate(range(0, nvec, SUB)):
        for k, x_ref in zip(ORDER, x_refs):
            first = rows_of(partner(place_ref, k)) * per
            for t in range(per):
                for c in range(comps):
                    rows = pl.ds(first + (v * stride + c * tiles + t), SUB, stride)
                    held[rows, :] = x_ref[t, c, v : v + SUB, :]
        rows = pl.ds(v * stride, SUB * stride)
        store = pltpu.make_async_copy(held.at[rows], o_ref.at[rows], sems.at[i])
        store.start()
        stores.append(store)
    for store in stores:
        store.wait()


def turn(a):
    return pltpu.roll(a, NX, 1)


def pack_edges(low, near, far, first_ref, last_ref, at):
    first_ref[at] = jnp.where(low, near[0], turn(far[0]))
    last_ref[at] = jnp.where(low, turn(near[1]), far[1])


def gather_kernel(place_ref, *refs):
    pieces, (o_ref, first_ref, last_ref) = refs[:-3], refs[-3:]
    groups, per, comps, nvec = o_ref.shape[:4]
    for k, x_ref in zip(ORDER, pieces):
        o_ref[partner(place_ref, k)] = x_ref[...]
    low = lax.broadcasted_iota(jnp.int32, (SUB, LANES), 1) < NX
    for q in range(groups // 2):
        for c in range(comps):
            for v in range(0, nvec, SUB):
                rows = slice(v, v + SUB)
                near, far = [[o_ref[g, t, c, rows, :] for t in (0, per - 1)] for g in (q, q + groups // 2)]
                pack_edges(low, near, far, first_ref, last_ref, (q, c, rows, slice(None)))


def stencil_kernel(stiff_ref, mass_ref, cls_ref, u_ref, yd_ref, yu_ref, za_ref, zb_ref, w_ref, *rest):
    edges, coef_ref = rest[:-1], rest[-1]
    groups, per, comps, nvec = u_ref.shape[:4]
    lane = lax.broadcasted_iota(jnp.int32, (SUB, LANES), 1)
    low = lane < NX

    def pick(cls, values):
        out = jnp.zeros((SUB, LANES), jnp.float32)
        for level in range(LEVELS):
            out = jnp.where(cls == level, values[level], out)
        return out

    for t in range(per):
        for face, direction in enumerate((0, 1, 1, 2, 2)):
            cls = jnp.broadcast_to(cls_ref[face, t : t + 1, :], (SUB, LANES))
            for i, (a, b) in enumerate(ENTRIES):
                spots = [((level * 3 + direction) * 3 + a) * 3 + b for level in range(LEVELS)]
                coef_ref[t, face * 6 + i] = pick(cls, [stiff_ref[s] for s in spots])
        cls = jnp.broadcast_to(cls_ref[5, t : t + 1, :], (SUB, LANES))
        coef_ref[t, 30] = pick(cls, [mass_ref[level] for level in range(LEVELS)])

    def mix(t, face, d):
        s = [coef_ref[t, face * 6 + i] for i in range(6)]
        return [
            s[ENTRY_OF[min(a, 0), max(a, 0)]] * d[0]
            + s[ENTRY_OF[min(a, 1), max(a, 1)]] * d[1]
            + s[ENTRY_OF[min(a, 2), max(a, 2)]] * d[2]
            for a in range(3)
        ]

    steps = nvec // SUB
    half = groups // 2

    def body(i, carry):
        q = i // steps
        rows = pl.ds(pl.multiple_of((i % steps) * SUB, SUB), SUB)
        ends = []
        for part in range(2):
            g = q + part * half
            tiles = [[u_ref[g, t, c, rows, :] for c in range(3)] for t in range(per)]
            below = [yd_ref[q, c, rows, :] for c in range(3)]
            above = [yu_ref[q, c, rows, :] for c in range(3)]
            if part == 0:
                above = [turn(a) for a in above]
            else:
                below = [turn(a) for a in below]
            swaps = [below] + [[turn(a) for a in line] for line in tiles] + [above]
            done = []
            for t in range(per):
                u = tiles[t]
                f = mix(t, 0, [pltpu.roll(u[c], LANES - 1, 1) - u[c] for c in range(3)])
                acc = [coef_ref[t, 30] * u[c] + (pltpu.roll(f[c], 1, 1) - f[c]) for c in range(3)]
                f = mix(t, 1, [jnp.where(low, swaps[t + 1][c], swaps[t + 2][c]) - u[c] for c in range(3)])
                acc = [acc[c] - f[c] for c in range(3)]
                f = mix(t, 2, [u[c] - jnp.where(low, swaps[t][c], swaps[t + 1][c]) for c in range(3)])
                acc = [acc[c] + f[c] for c in range(3)]
                f = mix(t, 3, [za_ref[g, t, c, rows, :] - u[c] for c in range(3)])
                acc = [acc[c] - f[c] for c in range(3)]
                f = mix(t, 4, [zb_ref[g, t, c, rows, :] - u[c] for c in range(3)])
                done.append([acc[c] - f[c] for c in range(3)])
                for c in range(3):
                    w_ref[g, t, c, rows, :] = done[t][c]
            ends.append((done[0], done[-1]))
        if edges:
            for c in range(3):
                near, far = [[end[c] for end in pair] for pair in ends]
                pack_edges(low, near, far, *edges, (q, c, rows, slice(None)))
        return carry

    lax.fori_loop(0, half * steps, body, 0)


def stacked(ref, t, c):
    groups = ref.shape[0]
    return jnp.concatenate([ref[g, t, c] for g in range(groups)], 0)


def wide(ref, k):
    comps = ref.shape[2]
    return jnp.concatenate([stacked(ref, (2 * k + j) // comps, (2 * k + j) % comps) for j in range(2)], 1)


def packed_products(b_ref, a_ref):
    chunks = a_ref.shape[1] * a_ref.shape[2] // 2
    total = None
    for k in range(chunks):
        a, b = wide(a_ref, k), wide(b_ref, k)
        both = [side[i : i + TILE] for i in range(0, a.shape[0], TILE) for side in (b, a)]
        part = dot(a, jnp.concatenate(both, 0), (1, 1))
        total = part if total is None else total + part
    return [total[i * TILE : (i + 1) * TILE, j * LANES : (j + 1) * LANES] for i, j in PAIRS]


def early_kernel(b_ref, a_ref, o_ref):
    for i, block in enumerate(packed_products(b_ref, a_ref)):
        o_ref[i * TILE : (i + 1) * TILE, :] = block


def late_kernel(place_ref, *refs):
    early_ref, w_ref, keep_ref, give_ref, coef_ref = refs[-5:]
    u_ref = refs[3]
    stencil_kernel(*refs[:-5], w_ref, coef_ref)
    even = place_ref[2] == 0
    for i, block in enumerate(packed_products(u_ref, w_ref)):
        rows = slice(i * TILE, (i + 1) * TILE)
        early = early_ref[rows, :]
        keep_ref[rows, :] = jnp.where(even, block, early)
        give_ref[rows, :] = jnp.where(even, early, block)


def eliminate(panels, cols):
    first, width = cols
    tile, lane0 = first // LANES, first % LANES
    lane = lax.broadcasted_iota(jnp.int32, (SUB, LANES), 1)
    sub = lax.broadcasted_iota(jnp.int32, (SUB, LANES), 0)
    strips = width // SUB
    states = []
    for panel in panels:
        state = [[panel[i * SUB : (i + 1) * SUB, a : a + LANES] for a in range(0, panel.shape[1], LANES)] for i in range(strips)]
        unit = [jnp.where(lane == lane0 + i * SUB + sub, 1.0, 0.0) for i in range(strips)]
        states.append([line + [u] for line, u in zip(state, unit)])
    scales = [[jnp.ones((SUB, LANES), jnp.float32) for _ in range(strips)] for _ in panels]

    def spread(row, like):
        return jnp.broadcast_to(row, (SUB, like.shape[1]))

    for j in range(0, width, STEP):
        strip, off = j // SUB, j % SUB
        for m, state in enumerate(states):
            columns = [
                [jnp.broadcast_to(state[i][tile][:, lane0 + j + s : lane0 + j + s + 1], (SUB, LANES)) for i in range(strip, strips)]
                for s in range(STEP)
            ]
            rows = [[spread(part[off + r : off + r + 1, :], part) for part in state[strip]] for r in range(STEP)]
            small = [[spread(columns[s][0][off + r : off + r + 1, :], columns[s][0]) for s in range(STEP)] for r in range(STEP)]
            inverse = []
            pivots = []
            for r in range(STEP):
                pivots.append(small[r][r])
                inverse.append(1.0 / small[r][r])
                for q in range(r + 1, STEP):
                    ratio = small[q][r] * inverse[r]
                    rows[q] = [a - ratio[:, : a.shape[1]] * b for a, b in zip(rows[q], rows[r])]
                    columns[q] = [a - ratio * b for a, b in zip(columns[q], columns[r])]
                    for p in range(q, STEP):
                        small[p][q] = small[p][q] - ratio * small[p][r]
            weights = [[a * inverse[s] for a in columns[s]] for s in range(STEP)]
            for i in range(strip, strips):
                line = []
                for n, part in enumerate(state[i]):
                    value = part
                    for s in range(STEP):
                        value = value - weights[s][i - strip][:, : part.shape[1]] * rows[s][n]
                    if i == strip:
                        at = sub[:, : part.shape[1]]
                        if off:
                            value = jnp.where(at < off, part, value)
                        for r in range(STEP):
                            value = jnp.where(at == off + r, rows[r][n], value)
                    line.append(value)
                state[i] = line
            for r in range(STEP):
                scales[m][strip] = jnp.where(sub == off + r, pivots[r], scales[m][strip])
    results = []
    for state, scale in zip(states, scales):
        inverse, reduced = [], []
        for line, pivot in zip(state, scale):
            root = lax.rsqrt(pivot)
            root = root * (1.5 - 0.5 * pivot * root * root)
            inverse.append(line[-1] * root)
            reduced.append(jnp.concatenate([part * root[:, : part.shape[1]] for part in line[:-1]], 1))
        results.append((jnp.concatenate(inverse, 0), jnp.concatenate(reduced, 0)))
    return results


def dot(a, b, dims):
    return lax.dot_general(
        a, b, ((dims[:1], dims[1:]), ((), ())), precision=lax.Precision.HIGHEST, preferred_element_type=jnp.float32
    )


def factor(scratch, total):
    count = scratch.shape[0]
    lane = lax.broadcasted_iota(jnp.int32, (1, total), 1)
    for first in range(0, total, BLOCK):
        last = first + BLOCK
        here = (lane >= first) & (lane < last)
        results = eliminate([scratch[m, first:last, :] for m in range(count)], (first, BLOCK))
        for m, (inverse, reduced) in enumerate(results):
            tile = first // LANES * LANES
            side = min(LANES, total - tile)
            parts = []
            if tile:
                parts.append(jnp.zeros((BLOCK, tile), jnp.float32))
            parts.append(inverse[:, :side])
            if tile + side < total:
                parts.append(jnp.zeros((BLOCK, total - tile - side), jnp.float32))
            inverse = jnp.concatenate(parts, 1)
            row = jnp.where(here, inverse, reduced)
            scratch[m, first:last, :] = jnp.where(lane < last, row, 0.0)
            if last < total:
                rest = scratch[m, last:, :]
                lower = dot(rest, inverse, (1, 1))
                scratch[m, last:, :] = jnp.where(here, 0.0, rest) - dot(lower, row, (1, 0))


def factor_kernel(place_ref, own_ref, o_ref, packed, scratch, *, cells):
    pieces, quarter = own_ref.shape[:2]
    total = o_ref.shape[1]
    for k in range(pieces):
        at = ((place_ref[1] + pieces - k) % pieces) * quarter
        packed[pl.ds(pl.multiple_of(at, SUB), quarter), :] = own_ref[k] * (1.0 / cells)
    for m, target in enumerate((o_ref.at[1], scratch.at[0])):
        for q, (i, j) in enumerate(PAIRS):
            block = packed[q * TILE : (q + 1) * TILE, m * TILE : (m + 1) * TILE]
            target[i * TILE : (i + 1) * TILE, j * TILE : (j + 1) * TILE] = block
            if i != j:
                target[j * TILE : (j + 1) * TILE, i * TILE : (i + 1) * TILE] = block.T
    factor(scratch, total)
    o_ref[0] = scratch[0]


def combine_kernel(place_ref, mine_ref, other_ref, w_ref, *o_refs):
    per, comps, nvec = w_ref.shape[1:4]
    groups = w_ref.shape[0]
    even = place_ref[2] == 0
    order = [pl.ds(pl.multiple_of(partner(place_ref, k) * nvec, SUB), nvec) for k in ORDER]
    inv = jnp.concatenate([jnp.where(even, mine_ref[0, rows, :], other_ref[0, rows, :]) for rows in order], 0)
    for n in range(per * comps // 2):
        out = dot(inv, wide(w_ref, n), (1, 0))
        for j in range(2):
            t, c = (2 * n + j) // comps, (2 * n + j) % comps
            for k in range(groups):
                o_refs[k][t, c] = out[k * nvec : (k + 1) * nvec, j * LANES : (j + 1) * LANES]


def rayleigh_kernel(place_ref, mine_ref, other_ref, ray_ref):
    nvec = ray_ref.shape[1]
    even = place_ref[2] == 0
    own = pl.ds(pl.multiple_of(place_ref[0] * nvec, SUB), nvec)
    ray_ref[0] = jnp.where(even, other_ref[1, own, :], mine_ref[1, own, :])
    rows = jnp.where(even, other_ref[0, own, :], mine_ref[0, own, :])
    rows = dot(rows, jnp.where(even, mine_ref[1], other_ref[1]), (1, 0))
    ray_ref[1] = dot(rows, jnp.where(even, other_ref[0], mine_ref[0]), (1, 1))


def call(kernel, outs, operands, scratch=(), smem=0, flops=0, far_out=False):
    inside, outside = pl.BlockSpec(memory_space=pltpu.VMEM), pl.BlockSpec(memory_space=pl.ANY)
    specs = [pl.BlockSpec(memory_space=pltpu.SMEM)] * smem
    specs += [inside] * (len(operands) - smem)
    size = sum(a.size * 4 for a in operands) + 4
    return pl.pallas_call(
        kernel,
        out_shape=[jax.ShapeDtypeStruct(dims, jnp.float32) for dims in outs],
        in_specs=specs,
        out_specs=[outside if far_out else inside] * len(outs),
        scratch_shapes=list(scratch),
        compiler_params=pltpu.CompilerParams(vmem_limit_bytes=VMEM_LIMIT),
        cost_estimate=pl.CostEstimate(flops=flops, bytes_accessed=size, transcendentals=0),
    )(*operands)


def to_core(zl, y, core, x, zh):
    return (zl, y, 1 - core, x, zh)


def total_over_all(keep, give):
    x = lax.axis_index("vec") // 2
    quarter = keep.shape[0] // 4
    mine = keep + route(give, to_core)

    def chunk(k):
        return lax.dynamic_slice_in_dim(mine, ((x + k) % 4) * quarter, quarter, 0)

    def along_y(k):
        return lambda zl, y, c, x, zh: (zl, (y + k) % 4, c, x, zh)

    def along_x(k):
        return lambda zl, y, c, x, zh: (zl, y, c, (x + k) % 4, zh)

    def along_z(k):
        def move(zl, y, c, x, zh):
            z = (zh * 2 + zl + k) % 4
            return (z % 2, y, c, x, z // 2)

        return move

    got = [route(chunk(k), along_x(k)) for k in (1, 2, 3)]
    mine = (chunk(0) + got[1]) + (got[0] + got[2])
    for along in (along_y, along_z):
        got = [route(mine, along(k)) for k in (1, 2, 3)]
        mine = (mine + got[1]) + (got[0] + got[2])
    return jnp.stack([mine] + [route(mine, along_x(k)) for k in (1, 2, 3)])


def local(vectors, labels, stiffness, mass):
    nvec, comps, _, plane = vectors.shape
    groups = lax.axis_size("vec")
    total = nvec * groups
    nz = lax.axis_size("space")
    cells = 3.0 * nz * plane
    tiles = plane // LANES
    per = tiles // groups
    z = lax.axis_index("space")
    h = lax.axis_index("vec")

    below = step_along(labels, "space", 1)
    lab = labels.reshape(plane // NX, NX)
    row = lax.broadcasted_iota(jnp.int32, lab.shape, 0)
    col = lax.broadcasted_iota(jnp.int32, lab.shape, 1)
    none = LEVELS
    upper = jnp.concatenate([jnp.full((1, NX), none, jnp.int32), lab[:-1]], 0)
    over = jnp.where(z == nz - 1, none, lab)
    under = jnp.where(z == 0, none, below.reshape(lab.shape))
    core = z % 2
    faces = jnp.stack(
        [
            jnp.where(col == NX - 1, none, lab),
            jnp.where(row == lab.shape[0] - 1, none, lab),
            upper,
            jnp.where(core == 0, under, over),
            jnp.where(core == 0, over, under),
            lab,
        ]
    )
    faces = faces.reshape(6, tiles, LANES)
    faces = lax.dynamic_slice_in_dim(faces, rows_of(h) * per, per, 1)
    stiff = stiffness.reshape(-1)

    piece = (per, comps, nvec, LANES)
    shape = (groups,) + piece
    edge = (groups // 2, comps, nvec, LANES)

    def exchange(pieces):
        got = [lax.ppermute(a, "vec", [(i, i ^ k) for i in range(groups)]) for k, a in zip(ORDER[1:], pieces[1:])]
        return [pieces[0]] + got

    def halo(u, first, last):
        yd = step_along(last, "vec", 1)
        yu = step_along(first, "vec", -1)
        za = lax.ppermute(u, "space", [(i, i + (1 if i % 2 else -1)) for i in range(1, nz - 1)])
        zb = lax.ppermute(u, "space", [(i, i ^ 1) for i in range(nz)])
        return u, yd, yu, za, zb

    coefs = [pltpu.VMEM((per, 31, SUB, LANES), jnp.float32)]
    moving = [pltpu.VMEM(((nvec + 1) * comps * tiles, LANES), jnp.float32), pltpu.SemaphoreType.DMA((nvec // SUB,))]
    place = jnp.stack([h, h // 2, core]).astype(jnp.int32)
    work = total * total * per * comps * LANES
    packed = len(PAIRS) * TILE
    pieces = call(
        functools.partial(spread_kernel, tiles=tiles),
        [piece] * groups,
        (place, jnp.pad(vectors.reshape(nvec * comps * tiles, LANES), ((0, comps * tiles), (0, 0)))),
        smem=1,
    )
    v, first, last = call(gather_kernel, [shape, edge, edge], [place] + exchange(pieces), smem=1)
    w1, first, last = call(
        stencil_kernel,
        [shape, edge, edge],
        (stiff, mass, faces, *halo(v, first, last)),
        scratch=coefs,
        smem=2,
        flops=20_000_000,
    )
    (early,) = call(early_kernel, [(packed, LANES)], (v, w1), flops=24 * work)
    w2, keep, give = call(
        late_kernel,
        [shape, (packed, LANES), (packed, LANES)],
        (place, stiff, mass, faces, *halo(w1, first, last), early),
        scratch=coefs,
        smem=3,
        flops=24 * work,
    )
    (mine,) = call(
        functools.partial(factor_kernel, cells=cells),
        [(2, total, total)],
        (place, total_over_all(keep, give)),
        scratch=[pltpu.VMEM((packed, LANES), jnp.float32), pltpu.VMEM((1, total, total), jnp.float32)],
        smem=1,
        flops=2 * work,
    )
    other = route(mine, to_core)
    pieces = call(combine_kernel, [piece] * groups, (place, mine, other, w2), smem=1, flops=12 * work)
    *pieces, mine, other = lax.optimization_barrier((*pieces, mine, other))
    (rayleigh,) = call(rayleigh_kernel, [(2, nvec, total)], (place, mine, other), smem=1, flops=2 * work)
    (refined,) = call(
        functools.partial(collect_kernel, tiles=tiles),
        [(nvec * comps * tiles, LANES)],
        [place] + exchange(pieces),
        scratch=moving,
        smem=1,
        far_out=True,
    )
    return refined.reshape(vectors.shape), rayleigh


def solution(mesh):
    return jax.shard_map(
        local,
        mesh=mesh,
        in_specs=(P("vec", None, "space", None), P("space", None), P(), P()),
        out_specs=(P("vec", None, "space", None), P(None, "vec", None)),
        check_vma=False,
    )
```

```python
import functools

import jax
import jax.numpy as jnp
from jax import lax
from jax.experimental import pallas as pl
from jax.experimental.pallas import tpu as pltpu
from jax.sharding import PartitionSpec as P

NX = 64
LANES = 128
SUB = 8
LEVELS = 4
BLOCK = 64
STEP = 8
ORDER = (0, 7, 5, 3, 4, 1, 6, 2)
ENTRIES = ((0, 0), (0, 1), (0, 2), (1, 1), (1, 2), (2, 2))
ENTRY_OF = {pair: i for i, pair in enumerate(ENTRIES)}
VMEM_LIMIT = 48 * 1024 * 1024
SPACE = (2, 4, 2)
VEC = (4, 2)
TILE = 64
PAIRS = ((0, 0), (1, 0), (1, 1), (2, 0), (2, 1), (2, 2))


def rows_of(device):
    x, far = device // VEC[1], device % VEC[1]
    return x + far * (2 * VEC[0] - 1 - 2 * x)


DEVICE_OF = sorted(range(VEC[0] * VEC[1]), key=rows_of)


def route(array, move):
    pairs = []
    for zl in range(SPACE[0]):
        for y in range(SPACE[1]):
            for core in range(SPACE[2]):
                for x in range(VEC[0]):
                    for zh in range(VEC[1]):
                        a, b, c, d, e = move(zl, y, core, x, zh)
                        here = (((zl * SPACE[1] + y) * SPACE[2] + core) * VEC[0] + x) * VEC[1] + zh
                        there = (((a * SPACE[1] + b) * SPACE[2] + c) * VEC[0] + d) * VEC[1] + e
                        pairs.append((here, there))
    return lax.ppermute(array, ("space", "vec"), pairs)


def step_along(array, axis, by):
    order = DEVICE_OF if axis == "vec" else range(lax.axis_size(axis))
    pairs = [(order[i], order[i + by]) for i in range(len(order)) if 0 <= i + by < len(order)]
    return lax.ppermute(array, axis, pairs)


def partner(place_ref, k):
    return jnp.bitwise_xor(place_ref[0], k)


def spread_kernel(place_ref, x_ref, *o_refs, tiles):
    per, comps, nvec = o_refs[0].shape[:3]
    stride = comps * tiles
    for k, o_ref in zip(ORDER, o_refs):
        first = rows_of(partner(place_ref, k)) * per
        for t in range(per):
            for c in range(comps):
                for v in range(0, nvec, SUB):
                    rows = pl.ds(first + (v * stride + c * tiles + t), SUB, stride)
                    o_ref[t, c, v : v + SUB, :] = x_ref[rows, :]


def collect_kernel(place_ref, *refs, tiles):
    x_refs, (o_ref, held, sems) = refs[:-3], refs[-3:]
    per, comps, nvec = x_refs[0].shape[:3]
    stride = comps * tiles
    stores = []
    for i, v in enumerate(range(0, nvec, SUB)):
        for k, x_ref in zip(ORDER, x_refs):
            first = rows_of(partner(place_ref, k)) * per
            for t in range(per):
                for c in range(comps):
                    rows = pl.ds(first + (v * stride + c * tiles + t), SUB, stride)
                    held[rows, :] = x_ref[t, c, v : v + SUB, :]
        rows = pl.ds(v * stride, SUB * stride)
        store = pltpu.make_async_copy(held.at[rows], o_ref.at[rows], sems.at[i])
        store.start()
        stores.append(store)
    for store in stores:
        store.wait()


def turn(a):
    return pltpu.roll(a, NX, 1)


def pack_edges(low, near, far, first_ref, last_ref, at):
    first_ref[at] = jnp.where(low, near[0], turn(far[0]))
    last_ref[at] = jnp.where(low, turn(near[1]), far[1])


def gather_kernel(place_ref, *refs):
    pieces, (o_ref, first_ref, last_ref) = refs[:-3], refs[-3:]
    groups, per, comps, nvec = o_ref.shape[:4]
    for k, x_ref in zip(ORDER, pieces):
        o_ref[partner(place_ref, k)] = x_ref[...]
    low = lax.broadcasted_iota(jnp.int32, (SUB, LANES), 1) < NX
    for q in range(groups // 2):
        for c in range(comps):
            for v in range(0, nvec, SUB):
                rows = slice(v, v + SUB)
                near, far = [[o_ref[g, t, c, rows, :] for t in (0, per - 1)] for g in (q, q + groups // 2)]
                pack_edges(low, near, far, first_ref, last_ref, (q, c, rows, slice(None)))


def stencil_kernel(stiff_ref, mass_ref, cls_ref, u_ref, yd_ref, yu_ref, za_ref, zb_ref, w_ref, *rest):
    edges, coef_ref = rest[:-1], rest[-1]
    groups, per, comps, nvec = u_ref.shape[:4]
    lane = lax.broadcasted_iota(jnp.int32, (SUB, LANES), 1)
    low = lane < NX

    def pick(cls, values):
        out = jnp.zeros((SUB, LANES), jnp.float32)
        for level in range(LEVELS):
            out = jnp.where(cls == level, values[level], out)
        return out

    for t in range(per):
        for face, direction in enumerate((0, 1, 1, 2, 2)):
            cls = jnp.broadcast_to(cls_ref[face, t : t + 1, :], (SUB, LANES))
            for i, (a, b) in enumerate(ENTRIES):
                spots = [((level * 3 + direction) * 3 + a) * 3 + b for level in range(LEVELS)]
                coef_ref[t, face * 6 + i] = pick(cls, [stiff_ref[s] for s in spots])
        cls = jnp.broadcast_to(cls_ref[5, t : t + 1, :], (SUB, LANES))
        coef_ref[t, 30] = pick(cls, [mass_ref[level] for level in range(LEVELS)])

    def mix(t, face, d):
        s = [coef_ref[t, face * 6 + i] for i in range(6)]
        return [
            s[ENTRY_OF[min(a, 0), max(a, 0)]] * d[0]
            + s[ENTRY_OF[min(a, 1), max(a, 1)]] * d[1]
            + s[ENTRY_OF[min(a, 2), max(a, 2)]] * d[2]
            for a in range(3)
        ]

    steps = nvec // SUB
    half = groups // 2

    def body(i, carry):
        q = i // steps
        rows = pl.ds(pl.multiple_of((i % steps) * SUB, SUB), SUB)
        ends = []
        for part in range(2):
            g = q + part * half
            tiles = [[u_ref[g, t, c, rows, :] for c in range(3)] for t in range(per)]
            below = [yd_ref[q, c, rows, :] for c in range(3)]
            above = [yu_ref[q, c, rows, :] for c in range(3)]
            if part == 0:
                above = [turn(a) for a in above]
            else:
                below = [turn(a) for a in below]
            swaps = [below] + [[turn(a) for a in line] for line in tiles] + [above]
            done = []
            for t in range(per):
                u = tiles[t]
                f = mix(t, 0, [pltpu.roll(u[c], LANES - 1, 1) - u[c] for c in range(3)])
                acc = [coef_ref[t, 30] * u[c] + (pltpu.roll(f[c], 1, 1) - f[c]) for c in range(3)]
                f = mix(t, 1, [jnp.where(low, swaps[t + 1][c], swaps[t + 2][c]) - u[c] for c in range(3)])
                acc = [acc[c] - f[c] for c in range(3)]
                f = mix(t, 2, [u[c] - jnp.where(low, swaps[t][c], swaps[t + 1][c]) for c in range(3)])
                acc = [acc[c] + f[c] for c in range(3)]
                f = mix(t, 3, [za_ref[g, t, c, rows, :] - u[c] for c in range(3)])
                acc = [acc[c] - f[c] for c in range(3)]
                f = mix(t, 4, [zb_ref[g, t, c, rows, :] - u[c] for c in range(3)])
                done.append([acc[c] - f[c] for c in range(3)])
                for c in range(3):
                    w_ref[g, t, c, rows, :] = done[t][c]
            ends.append((done[0], done[-1]))
        if edges:
            for c in range(3):
                near, far = [[end[c] for end in pair] for pair in ends]
                pack_edges(low, near, far, *edges, (q, c, rows, slice(None)))
        return carry

    lax.fori_loop(0, half * steps, body, 0)


def stacked(ref, t, c):
    groups = ref.shape[0]
    return jnp.concatenate([ref[g, t, c] for g in range(groups)], 0)


def wide(ref, k):
    comps = ref.shape[2]
    return jnp.concatenate([stacked(ref, (2 * k + j) // comps, (2 * k + j) % comps) for j in range(2)], 1)


def packed_products(b_ref, a_ref, emit):
    chunks = a_ref.shape[1] * a_ref.shape[2] // 2
    total = a_ref.shape[0] * a_ref.shape[3]

    def gather(acc):
        acc[...] = jnp.zeros_like(acc)

        def body(k, carry):
            a, b = wide(a_ref, k), wide(b_ref, k)
            both = [side[i : i + TILE] for i in range(0, total, TILE) for side in (b, a)]
            acc[...] += dot(a, jnp.concatenate(both, 0), (1, 1))
            return carry

        lax.fori_loop(0, chunks, body, 0)
        for n, (i, j) in enumerate(PAIRS):
            emit(slice(n * TILE, (n + 1) * TILE), acc[i * TILE : (i + 1) * TILE, j * LANES : (j + 1) * LANES])

    pl.run_scoped(gather, pltpu.VMEM((total, 2 * total), jnp.float32))


def early_kernel(b_ref, a_ref, o_ref):
    def emit(rows, block):
        o_ref[rows, :] = block

    packed_products(b_ref, a_ref, emit)


def late_kernel(place_ref, *refs):
    early_ref, w_ref, keep_ref, give_ref, coef_ref = refs[-5:]
    stencil_kernel(*refs[:-5], w_ref, coef_ref)
    even = place_ref[2] == 0

    def emit(rows, block):
        early = early_ref[rows, :]
        keep_ref[rows, :] = jnp.where(even, block, early)
        give_ref[rows, :] = jnp.where(even, early, block)

    packed_products(refs[3], w_ref, emit)


def eliminate(panels, cols):
    first, width = cols
    tile, lane0 = first // LANES, first % LANES
    lane = lax.broadcasted_iota(jnp.int32, (SUB, LANES), 1)
    sub = lax.broadcasted_iota(jnp.int32, (SUB, LANES), 0)
    strips = width // SUB
    states = []
    for panel in panels:
        state = [[panel[i * SUB : (i + 1) * SUB, a : a + LANES] for a in range(0, panel.shape[1], LANES)] for i in range(strips)]
        unit = [jnp.where(lane == lane0 + i * SUB + sub, 1.0, 0.0) for i in range(strips)]
        states.append([line + [u] for line, u in zip(state, unit)])
    scales = [[jnp.ones((SUB, LANES), jnp.float32) for _ in range(strips)] for _ in panels]

    def spread(row, like):
        return jnp.broadcast_to(row, (SUB, like.shape[1]))

    for j in range(0, width, STEP):
        strip, off = j // SUB, j % SUB
        for m, state in enumerate(states):
            columns = [
                [jnp.broadcast_to(state[i][tile][:, lane0 + j + s : lane0 + j + s + 1], (SUB, LANES)) for i in range(strip, strips)]
                for s in range(STEP)
            ]
            rows = [[spread(part[off + r : off + r + 1, :], part) for part in state[strip]] for r in range(STEP)]
            small = [[spread(columns[s][0][off + r : off + r + 1, :], columns[s][0]) for s in range(STEP)] for r in range(STEP)]
            inverse = []
            pivots = []
            for r in range(STEP):
                pivots.append(small[r][r])
                inverse.append(1.0 / small[r][r])
                for q in range(r + 1, STEP):
                    ratio = small[q][r] * inverse[r]
                    rows[q] = [a - ratio[:, : a.shape[1]] * b for a, b in zip(rows[q], rows[r])]
                    columns[q] = [a - ratio * b for a, b in zip(columns[q], columns[r])]
                    for p in range(q, STEP):
                        small[p][q] = small[p][q] - ratio * small[p][r]
            weights = [[a * inverse[s] for a in columns[s]] for s in range(STEP)]
            for i in range(strip, strips):
                line = []
                for n, part in enumerate(state[i]):
                    value = part
                    for s in range(STEP):
                        value = value - weights[s][i - strip][:, : part.shape[1]] * rows[s][n]
                    if i == strip:
                        at = sub[:, : part.shape[1]]
                        if off:
                            value = jnp.where(at < off, part, value)
                        for r in range(STEP):
                            value = jnp.where(at == off + r, rows[r][n], value)
                    line.append(value)
                state[i] = line
            for r in range(STEP):
                scales[m][strip] = jnp.where(sub == off + r, pivots[r], scales[m][strip])
    results = []
    for state, scale in zip(states, scales):
        inverse, reduced = [], []
        for line, pivot in zip(state, scale):
            root = lax.rsqrt(pivot)
            root = root * (1.5 - 0.5 * pivot * root * root)
            inverse.append(line[-1] * root)
            reduced.append(jnp.concatenate([part * root[:, : part.shape[1]] for part in line[:-1]], 1))
        results.append((jnp.concatenate(inverse, 0), jnp.concatenate(reduced, 0)))
    return results


def dot(a, b, dims):
    return lax.dot_general(
        a, b, ((dims[:1], dims[1:]), ((), ())), precision=lax.Precision.HIGHEST, preferred_element_type=jnp.float32
    )


def factor(scratch, total):
    count = scratch.shape[0]
    lane = lax.broadcasted_iota(jnp.int32, (1, total), 1)
    for first in range(0, total, BLOCK):
        last = first + BLOCK
        here = (lane >= first) & (lane < last)
        results = eliminate([scratch[m, first:last, :] for m in range(count)], (first, BLOCK))
        for m, (inverse, reduced) in enumerate(results):
            tile = first // LANES * LANES
            side = min(LANES, total - tile)
            parts = []
            if tile:
                parts.append(jnp.zeros((BLOCK, tile), jnp.float32))
            parts.append(inverse[:, :side])
            if tile + side < total:
                parts.append(jnp.zeros((BLOCK, total - tile - side), jnp.float32))
            inverse = jnp.concatenate(parts, 1)
            row = jnp.where(here, inverse, reduced)
            scratch[m, first:last, :] = jnp.where(lane < last, row, 0.0)
            if last < total:
                rest = scratch[m, last:, :]
                lower = dot(rest, inverse, (1, 1))
                scratch[m, last:, :] = jnp.where(here, 0.0, rest) - dot(lower, row, (1, 0))


def factor_kernel(place_ref, own_ref, o_ref, packed, scratch, *, cells):
    pieces, quarter = own_ref.shape[:2]
    total = o_ref.shape[1]
    for k in range(pieces):
        at = ((place_ref[1] + pieces - k) % pieces) * quarter
        packed[pl.ds(pl.multiple_of(at, SUB), quarter), :] = own_ref[k] * (1.0 / cells)
    for m, target in enumerate((o_ref.at[1], scratch.at[0])):
        for q, (i, j) in enumerate(PAIRS):
            block = packed[q * TILE : (q + 1) * TILE, m * TILE : (m + 1) * TILE]
            target[i * TILE : (i + 1) * TILE, j * TILE : (j + 1) * TILE] = block
            if i != j:
                target[j * TILE : (j + 1) * TILE, i * TILE : (i + 1) * TILE] = block.T
    factor(scratch, total)
    o_ref[0] = scratch[0]


def combine_kernel(place_ref, mine_ref, other_ref, w_ref, *o_refs):
    per, comps, nvec = w_ref.shape[1:4]
    groups = w_ref.shape[0]
    even = place_ref[2] == 0
    order = [pl.ds(pl.multiple_of(partner(place_ref, k) * nvec, SUB), nvec) for k in ORDER]
    inv = jnp.concatenate([jnp.where(even, mine_ref[0, rows, :], other_ref[0, rows, :]) for rows in order], 0)

    def body(n, carry):
        out = dot(inv, wide(w_ref, n), (1, 0))
        for j in range(2):
            t, c = (2 * n + j) // comps, (2 * n + j) % comps
            for k in range(groups):
                o_refs[k][t, c] = out[k * nvec : (k + 1) * nvec, j * LANES : (j + 1) * LANES]
        return carry

    lax.fori_loop(0, per * comps // 2, body, 0)


def rayleigh_kernel(place_ref, mine_ref, other_ref, ray_ref):
    nvec = ray_ref.shape[1]
    even = place_ref[2] == 0
    own = pl.ds(pl.multiple_of(place_ref[0] * nvec, SUB), nvec)
    ray_ref[0] = jnp.where(even, other_ref[1, own, :], mine_ref[1, own, :])
    rows = jnp.where(even, other_ref[0, own, :], mine_ref[0, own, :])
    rows = dot(rows, jnp.where(even, mine_ref[1], other_ref[1]), (1, 0))
    ray_ref[1] = dot(rows, jnp.where(even, other_ref[0], mine_ref[0]), (1, 1))


def call(kernel, outs, operands, scratch=(), smem=0, flops=0, far_out=False):
    inside, outside = pl.BlockSpec(memory_space=pltpu.VMEM), pl.BlockSpec(memory_space=pl.ANY)
    specs = [pl.BlockSpec(memory_space=pltpu.SMEM)] * smem
    specs += [inside] * (len(operands) - smem)
    size = sum(a.size * 4 for a in operands) + 4
    return pl.pallas_call(
        kernel,
        out_shape=[jax.ShapeDtypeStruct(dims, jnp.float32) for dims in outs],
        in_specs=specs,
        out_specs=[outside if far_out else inside] * len(outs),
        scratch_shapes=list(scratch),
        compiler_params=pltpu.CompilerParams(vmem_limit_bytes=VMEM_LIMIT),
        cost_estimate=pl.CostEstimate(flops=flops, bytes_accessed=size, transcendentals=0),
    )(*operands)


def to_core(zl, y, core, x, zh):
    return (zl, y, 1 - core, x, zh)


def total_over_all(keep, give):
    x = lax.axis_index("vec") // 2
    quarter = keep.shape[0] // 4
    mine = keep + route(give, to_core)

    def chunk(k):
        return lax.dynamic_slice_in_dim(mine, ((x + k) % 4) * quarter, quarter, 0)

    def along_y(k):
        return lambda zl, y, c, x, zh: (zl, (y + k) % 4, c, x, zh)

    def along_x(k):
        return lambda zl, y, c, x, zh: (zl, y, c, (x + k) % 4, zh)

    def along_z(k):
        def move(zl, y, c, x, zh):
            z = (zh * 2 + zl + k) % 4
            return (z % 2, y, c, x, z // 2)

        return move

    got = [route(chunk(k), along_x(k)) for k in (1, 2, 3)]
    mine = (chunk(0) + got[1]) + (got[0] + got[2])
    for along in (along_y, along_z):
        got = [route(mine, along(k)) for k in (1, 2, 3)]
        mine = (mine + got[1]) + (got[0] + got[2])
    return jnp.stack([mine] + [route(mine, along_x(k)) for k in (1, 2, 3)])


def local(vectors, labels, stiffness, mass):
    nvec, comps, _, plane = vectors.shape
    groups = lax.axis_size("vec")
    total = nvec * groups
    nz = lax.axis_size("space")
    cells = 3.0 * nz * plane
    tiles = plane // LANES
    per = tiles // groups
    z = lax.axis_index("space")
    h = lax.axis_index("vec")

    below = step_along(labels, "space", 1)
    lab = labels.reshape(plane // NX, NX)
    row = lax.broadcasted_iota(jnp.int32, lab.shape, 0)
    col = lax.broadcasted_iota(jnp.int32, lab.shape, 1)
    none = LEVELS
    upper = jnp.concatenate([jnp.full((1, NX), none, jnp.int32), lab[:-1]], 0)
    over = jnp.where(z == nz - 1, none, lab)
    under = jnp.where(z == 0, none, below.reshape(lab.shape))
    core = z % 2
    faces = jnp.stack(
        [
            jnp.where(col == NX - 1, none, lab),
            jnp.where(row == lab.shape[0] - 1, none, lab),
            upper,
            jnp.where(core == 0, under, over),
            jnp.where(core == 0, over, under),
            lab,
        ]
    )
    faces = faces.reshape(6, tiles, LANES)
    faces = lax.dynamic_slice_in_dim(faces, rows_of(h) * per, per, 1)
    stiff = stiffness.reshape(-1)

    piece = (per, comps, nvec, LANES)
    shape = (groups,) + piece
    edge = (groups // 2, comps, nvec, LANES)

    def exchange(pieces):
        got = [lax.ppermute(a, "vec", [(i, i ^ k) for i in range(groups)]) for k, a in zip(ORDER[1:], pieces[1:])]
        return [pieces[0]] + got

    def halo(u, first, last):
        yd = step_along(last, "vec", 1)
        yu = step_along(first, "vec", -1)
        za = lax.ppermute(u, "space", [(i, i + (1 if i % 2 else -1)) for i in range(1, nz - 1)])
        zb = lax.ppermute(u, "space", [(i, i ^ 1) for i in range(nz)])
        return u, yd, yu, za, zb

    coefs = [pltpu.VMEM((per, 31, SUB, LANES), jnp.float32)]
    moving = [pltpu.VMEM(((nvec + 1) * comps * tiles, LANES), jnp.float32), pltpu.SemaphoreType.DMA((nvec // SUB,))]
    place = jnp.stack([h, h // 2, core]).astype(jnp.int32)
    work = total * total * per * comps * LANES
    packed = len(PAIRS) * TILE
    pieces = call(
        functools.partial(spread_kernel, tiles=tiles),
        [piece] * groups,
        (place, jnp.pad(vectors.reshape(nvec * comps * tiles, LANES), ((0, comps * tiles), (0, 0)))),
        smem=1,
    )
    v, first, last = call(gather_kernel, [shape, edge, edge], [place] + exchange(pieces), smem=1)
    w1, first, last = call(
        stencil_kernel,
        [shape, edge, edge],
        (stiff, mass, faces, *halo(v, first, last)),
        scratch=coefs,
        smem=2,
        flops=20_000_000,
    )
    (early,) = call(early_kernel, [(packed, LANES)], (v, w1), flops=24 * work)
    w2, keep, give = call(
        late_kernel,
        [shape, (packed, LANES), (packed, LANES)],
        (place, stiff, mass, faces, *halo(w1, first, last), early),
        scratch=coefs,
        smem=3,
        flops=24 * work,
    )
    (mine,) = call(
        functools.partial(factor_kernel, cells=cells),
        [(2, total, total)],
        (place, total_over_all(keep, give)),
        scratch=[pltpu.VMEM((packed, LANES), jnp.float32), pltpu.VMEM((1, total, total), jnp.float32)],
        smem=1,
        flops=2 * work,
    )
    other = route(mine, to_core)
    pieces = call(combine_kernel, [piece] * groups, (place, mine, other, w2), smem=1, flops=12 * work)
    *pieces, mine, other = lax.optimization_barrier((*pieces, mine, other))
    (rayleigh,) = call(rayleigh_kernel, [(2, nvec, total)], (place, mine, other), smem=1, flops=2 * work)
    (refined,) = call(
        functools.partial(collect_kernel, tiles=tiles),
        [(nvec * comps * tiles, LANES)],
        [place] + exchange(pieces),
        scratch=moving,
        smem=1,
        far_out=True,
    )
    return refined.reshape(vectors.shape), rayleigh


def solution(mesh):
    return jax.shard_map(
        local,
        mesh=mesh,
        in_specs=(P("vec", None, "space", None), P("space", None), P(), P()),
        out_specs=(P("vec", None, "space", None), P(None, "vec", None)),
        check_vma=False,
    )
```

```python
import functools

import jax
import jax.numpy as jnp
from jax import lax
from jax.experimental import pallas as pl
from jax.experimental.pallas import tpu as pltpu
from jax.sharding import PartitionSpec as P

NX = 64
LANES = 128
SUB = 8
LEVELS = 4
BLOCK = 64
STEP = 8
ORDER = (0, 7, 5, 3, 4, 1, 6, 2)
ENTRIES = ((0, 0), (0, 1), (0, 2), (1, 1), (1, 2), (2, 2))
ENTRY_OF = {pair: i for i, pair in enumerate(ENTRIES)}
VMEM_LIMIT = 48 * 1024 * 1024
SPACE = (2, 4, 2)
VEC = (4, 2)
TILE = 64
PAIRS = ((0, 0), (1, 0), (1, 1), (2, 0), (2, 1), (2, 2))


def rows_of(device):
    x, far = device // VEC[1], device % VEC[1]
    return x + far * (2 * VEC[0] - 1 - 2 * x)


DEVICE_OF = sorted(range(VEC[0] * VEC[1]), key=rows_of)


def route(array, move):
    pairs = []
    for zl in range(SPACE[0]):
        for y in range(SPACE[1]):
            for core in range(SPACE[2]):
                for x in range(VEC[0]):
                    for zh in range(VEC[1]):
                        a, b, c, d, e = move(zl, y, core, x, zh)
                        here = (((zl * SPACE[1] + y) * SPACE[2] + core) * VEC[0] + x) * VEC[1] + zh
                        there = (((a * SPACE[1] + b) * SPACE[2] + c) * VEC[0] + d) * VEC[1] + e
                        pairs.append((here, there))
    return lax.ppermute(array, ("space", "vec"), pairs)


def step_along(array, axis, by):
    order = DEVICE_OF if axis == "vec" else range(lax.axis_size(axis))
    pairs = [(order[i], order[i + by]) for i in range(len(order)) if 0 <= i + by < len(order)]
    return lax.ppermute(array, axis, pairs)


def partner(place_ref, k):
    return jnp.bitwise_xor(place_ref[0], k)


def spread_kernel(place_ref, x_ref, *o_refs, tiles):
    per, comps, nvec = o_refs[0].shape[:3]
    stride = comps * tiles
    for k, o_ref in zip(ORDER, o_refs):
        first = rows_of(partner(place_ref, k)) * per
        for t in range(per):
            for c in range(comps):
                for v in range(0, nvec, SUB):
                    rows = pl.ds(first + (v * stride + c * tiles + t), SUB, stride)
                    o_ref[t, c, v : v + SUB, :] = x_ref[rows, :]


def collect_kernel(place_ref, *refs, tiles):
    x_refs, (o_ref, held, sems) = refs[:-3], refs[-3:]
    per, comps, nvec = x_refs[0].shape[:3]
    stride = comps * tiles
    stores = []
    for i, v in enumerate(range(0, nvec, SUB)):
        for k, x_ref in zip(ORDER, x_refs):
            first = rows_of(partner(place_ref, k)) * per
            for t in range(per):
                for c in range(comps):
                    rows = pl.ds(first + (v * stride + c * tiles + t), SUB, stride)
                    held[rows, :] = x_ref[t, c, v : v + SUB, :]
        rows = pl.ds(v * stride, SUB * stride)
        store = pltpu.make_async_copy(held.at[rows], o_ref.at[rows], sems.at[i])
        store.start()
        stores.append(store)
    for store in stores:
        store.wait()


def turn(a):
    return pltpu.roll(a, NX, 1)


def pack_edges(low, near, far, first_ref, last_ref, at):
    first_ref[at] = jnp.where(low, near[0], turn(far[0]))
    last_ref[at] = jnp.where(low, turn(near[1]), far[1])


def gather_kernel(place_ref, *refs):
    pieces, (o_ref, first_ref, last_ref) = refs[:-3], refs[-3:]
    groups, per, comps, nvec = o_ref.shape[:4]
    for k, x_ref in zip(ORDER, pieces):
        o_ref[partner(place_ref, k)] = x_ref[...]
    low = lax.broadcasted_iota(jnp.int32, (SUB, LANES), 1) < NX
    for q in range(groups // 2):
        for c in range(comps):
            for v in range(0, nvec, SUB):
                rows = slice(v, v + SUB)
                near, far = [[o_ref[g, t, c, rows, :] for t in (0, per - 1)] for g in (q, q + groups // 2)]
                pack_edges(low, near, far, first_ref, last_ref, (q, c, rows, slice(None)))


def stencil_kernel(stiff_ref, mass_ref, cls_ref, u_ref, yd_ref, yu_ref, za_ref, zb_ref, w_ref, *rest):
    edges, coef_ref = rest[:-1], rest[-1]
    groups, per, comps, nvec = u_ref.shape[:4]
    lane = lax.broadcasted_iota(jnp.int32, (SUB, LANES), 1)
    low = lane < NX

    def pick(cls, values):
        out = jnp.zeros((SUB, LANES), jnp.float32)
        for level in range(LEVELS):
            out = jnp.where(cls == level, values[level], out)
        return out

    for t in range(per):
        for face, direction in enumerate((0, 1, 1, 2, 2)):
            cls = jnp.broadcast_to(cls_ref[face, t : t + 1, :], (SUB, LANES))
            for i, (a, b) in enumerate(ENTRIES):
                spots = [((level * 3 + direction) * 3 + a) * 3 + b for level in range(LEVELS)]
                coef_ref[t, face * 6 + i] = pick(cls, [stiff_ref[s] for s in spots])
        cls = jnp.broadcast_to(cls_ref[5, t : t + 1, :], (SUB, LANES))
        coef_ref[t, 30] = pick(cls, [mass_ref[level] for level in range(LEVELS)])

    def mix(coef, face, d):
        s = coef[face * 6 : face * 6 + 6]
        return [
            s[ENTRY_OF[min(a, 0), max(a, 0)]] * d[0]
            + s[ENTRY_OF[min(a, 1), max(a, 1)]] * d[1]
            + s[ENTRY_OF[min(a, 2), max(a, 2)]] * d[2]
            for a in range(3)
        ]

    steps = nvec // SUB
    half = groups // 2

    def body(i, carry):
        q = i // steps
        rows = pl.ds(pl.multiple_of((i % steps) * SUB, SUB), SUB)
        places = (q, q + half)
        below = [yd_ref[q, c, rows, :] for c in range(3)]
        above = [yu_ref[q, c, rows, :] for c in range(3)]
        window = [[below, None], [[turn(a) for a in below], None]]
        here = [[u_ref[g, 0, c, rows, :] for c in range(3)] for g in places]
        for part in range(2):
            window[part][1] = [turn(a) for a in here[part]]
        for t in range(per):
            coef = [coef_ref[t, n] for n in range(31)]
            done = []
            for part, g in enumerate(places):
                u = here[part]
                if t + 1 < per:
                    here[part] = [u_ref[g, t + 1, c, rows, :] for c in range(3)]
                    after = [turn(a) for a in here[part]]
                else:
                    after = above if part else [turn(a) for a in above]
                before, swap = window[part]
                window[part] = [swap, after]
                f = mix(coef, 0, [pltpu.roll(u[c], LANES - 1, 1) - u[c] for c in range(3)])
                acc = [coef[30] * u[c] + (pltpu.roll(f[c], 1, 1) - f[c]) for c in range(3)]
                f = mix(coef, 1, [jnp.where(low, swap[c], after[c]) - u[c] for c in range(3)])
                acc = [acc[c] - f[c] for c in range(3)]
                f = mix(coef, 2, [u[c] - jnp.where(low, before[c], swap[c]) for c in range(3)])
                acc = [acc[c] + f[c] for c in range(3)]
                f = mix(coef, 3, [za_ref[g, t, c, rows, :] - u[c] for c in range(3)])
                acc = [acc[c] - f[c] for c in range(3)]
                f = mix(coef, 4, [zb_ref[g, t, c, rows, :] - u[c] for c in range(3)])
                done.append([acc[c] - f[c] for c in range(3)])
            for g, line in zip(places, done):
                for c in range(3):
                    w_ref[g, t, c, rows, :] = line[c]
            if edges and t == 0:
                for c in range(3):
                    edges[0][q, c, rows, :] = jnp.where(low, done[0][c], turn(done[1][c]))
            if edges and t == per - 1:
                for c in range(3):
                    edges[1][q, c, rows, :] = jnp.where(low, turn(done[0][c]), done[1][c])
        return carry

    lax.fori_loop(0, half * steps, body, 0)


def stacked(ref, t, c):
    groups = ref.shape[0]
    return jnp.concatenate([ref[g, t, c] for g in range(groups)], 0)


def wide(ref, k):
    comps = ref.shape[2]
    return jnp.concatenate([stacked(ref, (2 * k + j) // comps, (2 * k + j) % comps) for j in range(2)], 1)


def packed_products(b_ref, a_ref):
    chunks = a_ref.shape[1] * a_ref.shape[2] // 2
    total = None
    for k in range(chunks):
        a, b = wide(a_ref, k), wide(b_ref, k)
        both = [side[i : i + TILE] for i in range(0, a.shape[0], TILE) for side in (b, a)]
        part = dot(a, jnp.concatenate(both, 0), (1, 1))
        total = part if total is None else total + part
    return [total[i * TILE : (i + 1) * TILE, j * LANES : (j + 1) * LANES] for i, j in PAIRS]


def early_kernel(b_ref, a_ref, o_ref):
    for i, block in enumerate(packed_products(b_ref, a_ref)):
        o_ref[i * TILE : (i + 1) * TILE, :] = block


def late_kernel(place_ref, *refs):
    early_ref, w_ref, keep_ref, give_ref, coef_ref = refs[-5:]
    u_ref = refs[3]
    stencil_kernel(*refs[:-5], w_ref, coef_ref)
    even = place_ref[2] == 0
    for i, block in enumerate(packed_products(u_ref, w_ref)):
        rows = slice(i * TILE, (i + 1) * TILE)
        early = early_ref[rows, :]
        keep_ref[rows, :] = jnp.where(even, block, early)
        give_ref[rows, :] = jnp.where(even, early, block)


def eliminate(panels, cols):
    first, width = cols
    tile, lane0 = first // LANES, first % LANES
    lane = lax.broadcasted_iota(jnp.int32, (SUB, LANES), 1)
    sub = lax.broadcasted_iota(jnp.int32, (SUB, LANES), 0)
    strips = width // SUB
    states = []
    for panel in panels:
        state = [[panel[i * SUB : (i + 1) * SUB, a : a + LANES] for a in range(0, panel.shape[1], LANES)] for i in range(strips)]
        unit = [jnp.where(lane == lane0 + i * SUB + sub, 1.0, 0.0) for i in range(strips)]
        states.append([line + [u] for line, u in zip(state, unit)])
    scales = [[jnp.ones((SUB, LANES), jnp.float32) for _ in range(strips)] for _ in panels]

    def spread(row, like):
        return jnp.broadcast_to(row, (SUB, like.shape[1]))

    for j in range(0, width, STEP):
        strip, off = j // SUB, j % SUB
        for m, state in enumerate(states):
            columns = [
                [jnp.broadcast_to(state[i][tile][:, lane0 + j + s : lane0 + j + s + 1], (SUB, LANES)) for i in range(strip, strips)]
                for s in range(STEP)
            ]
            rows = [[spread(part[off + r : off + r + 1, :], part) for part in state[strip]] for r in range(STEP)]
            small = [[spread(columns[s][0][off + r : off + r + 1, :], columns[s][0]) for s in range(STEP)] for r in range(STEP)]
            inverse = []
            pivots = []
            for r in range(STEP):
                pivots.append(small[r][r])
                inverse.append(1.0 / small[r][r])
                for q in range(r + 1, STEP):
                    ratio = small[q][r] * inverse[r]
                    rows[q] = [a - ratio[:, : a.shape[1]] * b for a, b in zip(rows[q], rows[r])]
                    columns[q] = [a - ratio * b for a, b in zip(columns[q], columns[r])]
                    for p in range(q, STEP):
                        small[p][q] = small[p][q] - ratio * small[p][r]
            weights = [[a * inverse[s] for a in columns[s]] for s in range(STEP)]
            for i in range(strip, strips):
                line = []
                for n, part in enumerate(state[i]):
                    value = part
                    for s in range(STEP):
                        value = value - weights[s][i - strip][:, : part.shape[1]] * rows[s][n]
                    if i == strip:
                        at = sub[:, : part.shape[1]]
                        if off:
                            value = jnp.where(at < off, part, value)
                        for r in range(STEP):
                            value = jnp.where(at == off + r, rows[r][n], value)
                    line.append(value)
                state[i] = line
            for r in range(STEP):
                scales[m][strip] = jnp.where(sub == off + r, pivots[r], scales[m][strip])
    results = []
    for state, scale in zip(states, scales):
        inverse, reduced = [], []
        for line, pivot in zip(state, scale):
            root = lax.rsqrt(pivot)
            root = root * (1.5 - 0.5 * pivot * root * root)
            inverse.append(line[-1] * root)
            reduced.append(jnp.concatenate([part * root[:, : part.shape[1]] for part in line[:-1]], 1))
        results.append((jnp.concatenate(inverse, 0), jnp.concatenate(reduced, 0)))
    return results


def dot(a, b, dims):
    return lax.dot_general(
        a, b, ((dims[:1], dims[1:]), ((), ())), precision=lax.Precision.HIGHEST, preferred_element_type=jnp.float32
    )


def factor(scratch, total):
    count = scratch.shape[0]
    lane = lax.broadcasted_iota(jnp.int32, (1, total), 1)
    for first in range(0, total, BLOCK):
        last = first + BLOCK
        here = (lane >= first) & (lane < last)
        results = eliminate([scratch[m, first:last, :] for m in range(count)], (first, BLOCK))
        for m, (inverse, reduced) in enumerate(results):
            tile = first // LANES * LANES
            side = min(LANES, total - tile)
            parts = []
            if tile:
                parts.append(jnp.zeros((BLOCK, tile), jnp.float32))
            parts.append(inverse[:, :side])
            if tile + side < total:
                parts.append(jnp.zeros((BLOCK, total - tile - side), jnp.float32))
            inverse = jnp.concatenate(parts, 1)
            row = jnp.where(here, inverse, reduced)
            scratch[m, first:last, :] = jnp.where(lane < last, row, 0.0)
            if last < total:
                rest = scratch[m, last:, :]
                lower = dot(rest, inverse, (1, 1))
                scratch[m, last:, :] = jnp.where(here, 0.0, rest) - dot(lower, row, (1, 0))


def factor_kernel(place_ref, own_ref, o_ref, packed, scratch, *, cells):
    pieces, quarter = own_ref.shape[:2]
    total = o_ref.shape[1]
    for k in range(pieces):
        at = ((place_ref[1] + pieces - k) % pieces) * quarter
        packed[pl.ds(pl.multiple_of(at, SUB), quarter), :] = own_ref[k] * (1.0 / cells)
    for m, target in enumerate((o_ref.at[1], scratch.at[0])):
        for q, (i, j) in enumerate(PAIRS):
            block = packed[q * TILE : (q + 1) * TILE, m * TILE : (m + 1) * TILE]
            target[i * TILE : (i + 1) * TILE, j * TILE : (j + 1) * TILE] = block
            if i != j:
                target[j * TILE : (j + 1) * TILE, i * TILE : (i + 1) * TILE] = block.T
    factor(scratch, total)
    o_ref[0] = scratch[0]


def combine_kernel(place_ref, mine_ref, other_ref, w_ref, *o_refs):
    per, comps, nvec = w_ref.shape[1:4]
    groups = w_ref.shape[0]
    even = place_ref[2] == 0
    order = [pl.ds(pl.multiple_of(partner(place_ref, k) * nvec, SUB), nvec) for k in ORDER]
    inv = jnp.concatenate([jnp.where(even, mine_ref[0, rows, :], other_ref[0, rows, :]) for rows in order], 0)
    for n in range(per * comps // 2):
        out = dot(inv, wide(w_ref, n), (1, 0))
        for j in range(2):
            t, c = (2 * n + j) // comps, (2 * n + j) % comps
            for k in range(groups):
                o_refs[k][t, c] = out[k * nvec : (k + 1) * nvec, j * LANES : (j + 1) * LANES]


def rayleigh_kernel(place_ref, mine_ref, other_ref, ray_ref):
    nvec = ray_ref.shape[1]
    even = place_ref[2] == 0
    own = pl.ds(pl.multiple_of(place_ref[0] * nvec, SUB), nvec)
    ray_ref[0] = jnp.where(even, other_ref[1, own, :], mine_ref[1, own, :])
    rows = jnp.where(even, other_ref[0, own, :], mine_ref[0, own, :])
    rows = dot(rows, jnp.where(even, mine_ref[1], other_ref[1]), (1, 0))
    ray_ref[1] = dot(rows, jnp.where(even, other_ref[0], mine_ref[0]), (1, 1))


def call(kernel, outs, operands, scratch=(), smem=0, flops=0, far_out=False):
    inside, outside = pl.BlockSpec(memory_space=pltpu.VMEM), pl.BlockSpec(memory_space=pl.ANY)
    specs = [pl.BlockSpec(memory_space=pltpu.SMEM)] * smem
    specs += [inside] * (len(operands) - smem)
    size = sum(a.size * 4 for a in operands) + 4
    return pl.pallas_call(
        kernel,
        out_shape=[jax.ShapeDtypeStruct(dims, jnp.float32) for dims in outs],
        in_specs=specs,
        out_specs=[outside if far_out else inside] * len(outs),
        scratch_shapes=list(scratch),
        compiler_params=pltpu.CompilerParams(vmem_limit_bytes=VMEM_LIMIT),
        cost_estimate=pl.CostEstimate(flops=flops, bytes_accessed=size, transcendentals=0),
    )(*operands)


def to_core(zl, y, core, x, zh):
    return (zl, y, 1 - core, x, zh)


def total_over_all(keep, give):
    x = lax.axis_index("vec") // 2
    quarter = keep.shape[0] // 4
    mine = keep + route(give, to_core)

    def chunk(k):
        return lax.dynamic_slice_in_dim(mine, ((x + k) % 4) * quarter, quarter, 0)

    def along_y(k):
        return lambda zl, y, c, x, zh: (zl, (y + k) % 4, c, x, zh)

    def along_x(k):
        return lambda zl, y, c, x, zh: (zl, y, c, (x + k) % 4, zh)

    def along_z(k):
        def move(zl, y, c, x, zh):
            z = (zh * 2 + zl + k) % 4
            return (z % 2, y, c, x, z // 2)

        return move

    got = [route(chunk(k), along_x(k)) for k in (1, 2, 3)]
    mine = (chunk(0) + got[1]) + (got[0] + got[2])
    for along in (along_y, along_z):
        got = [route(mine, along(k)) for k in (1, 2, 3)]
        mine = (mine + got[1]) + (got[0] + got[2])
    return jnp.stack([mine] + [route(mine, along_x(k)) for k in (1, 2, 3)])


def local(vectors, labels, stiffness, mass):
    nvec, comps, _, plane = vectors.shape
    groups = lax.axis_size("vec")
    total = nvec * groups
    nz = lax.axis_size("space")
    cells = 3.0 * nz * plane
    tiles = plane // LANES
    per = tiles // groups
    z = lax.axis_index("space")
    h = lax.axis_index("vec")

    below = step_along(labels, "space", 1)
    lab = labels.reshape(plane // NX, NX)
    row = lax.broadcasted_iota(jnp.int32, lab.shape, 0)
    col = lax.broadcasted_iota(jnp.int32, lab.shape, 1)
    none = LEVELS
    upper = jnp.concatenate([jnp.full((1, NX), none, jnp.int32), lab[:-1]], 0)
    over = jnp.where(z == nz - 1, none, lab)
    under = jnp.where(z == 0, none, below.reshape(lab.shape))
    core = z % 2
    faces = jnp.stack(
        [
            jnp.where(col == NX - 1, none, lab),
            jnp.where(row == lab.shape[0] - 1, none, lab),
            upper,
            jnp.where(core == 0, under, over),
            jnp.where(core == 0, over, under),
            lab,
        ]
    )
    faces = faces.reshape(6, tiles, LANES)
    faces = lax.dynamic_slice_in_dim(faces, rows_of(h) * per, per, 1)
    stiff = stiffness.reshape(-1)

    piece = (per, comps, nvec, LANES)
    shape = (groups,) + piece
    edge = (groups // 2, comps, nvec, LANES)

    def exchange(pieces):
        got = [lax.ppermute(a, "vec", [(i, i ^ k) for i in range(groups)]) for k, a in zip(ORDER[1:], pieces[1:])]
        return [pieces[0]] + got

    def halo(u, first, last):
        yd = step_along(last, "vec", 1)
        yu = step_along(first, "vec", -1)
        za = lax.ppermute(u, "space", [(i, i + (1 if i % 2 else -1)) for i in range(1, nz - 1)])
        zb = lax.ppermute(u, "space", [(i, i ^ 1) for i in range(nz)])
        return u, yd, yu, za, zb

    coefs = [pltpu.VMEM((per, 31, SUB, LANES), jnp.float32)]
    moving = [pltpu.VMEM(((nvec + 1) * comps * tiles, LANES), jnp.float32), pltpu.SemaphoreType.DMA((nvec // SUB,))]
    place = jnp.stack([h, h // 2, core]).astype(jnp.int32)
    work = total * total * per * comps * LANES
    packed = len(PAIRS) * TILE
    pieces = call(
        functools.partial(spread_kernel, tiles=tiles),
        [piece] * groups,
        (place, jnp.pad(vectors.reshape(nvec * comps * tiles, LANES), ((0, comps * tiles), (0, 0)))),
        smem=1,
    )
    v, first, last = call(gather_kernel, [shape, edge, edge], [place] + exchange(pieces), smem=1)
    w1, first, last = call(
        stencil_kernel,
        [shape, edge, edge],
        (stiff, mass, faces, *halo(v, first, last)),
        scratch=coefs,
        smem=2,
        flops=20_000_000,
    )
    (early,) = call(early_kernel, [(packed, LANES)], (v, w1), flops=24 * work)
    w2, keep, give = call(
        late_kernel,
        [shape, (packed, LANES), (packed, LANES)],
        (place, stiff, mass, faces, *halo(w1, first, last), early),
        scratch=coefs,
        smem=3,
        flops=24 * work,
    )
    (mine,) = call(
        functools.partial(factor_kernel, cells=cells),
        [(2, total, total)],
        (place, total_over_all(keep, give)),
        scratch=[pltpu.VMEM((packed, LANES), jnp.float32), pltpu.VMEM((1, total, total), jnp.float32)],
        smem=1,
        flops=2 * work,
    )
    other = route(mine, to_core)
    pieces = call(combine_kernel, [piece] * groups, (place, mine, other, w2), smem=1, flops=12 * work)
    *pieces, mine, other = lax.optimization_barrier((*pieces, mine, other))
    (rayleigh,) = call(rayleigh_kernel, [(2, nvec, total)], (place, mine, other), smem=1, flops=2 * work)
    (refined,) = call(
        functools.partial(collect_kernel, tiles=tiles),
        [(nvec * comps * tiles, LANES)],
        [place] + exchange(pieces),
        scratch=moving,
        smem=1,
        far_out=True,
    )
    return refined.reshape(vectors.shape), rayleigh


def solution(mesh):
    return jax.shard_map(
        local,
        mesh=mesh,
        in_specs=(P("vec", None, "space", None), P("space", None), P(), P()),
        out_specs=(P("vec", None, "space", None), P(None, "vec", None)),
        check_vma=False,
    )
```
